128 devices in a mesh: section: 2 (over y_hi), ctx: 8 (over x, y_lo), wt: 8 (over z, core).
Axes of the slice: x: 4, y: 4 (y_hi: 2, y_lo: 2; y = y_hi * 2 + y_lo), z: 4, core: 2. Of those that a mesh axis runs over, the one named last changes fastest.
Arguments:
- inputs: bfloat16 [2, 1536, 2048], P(None, 'ctx', 'wt'), may hold values from -6 to 6
- cotangent: bfloat16 [2, 1536, 2048], P(None, 'ctx', 'wt'), may hold values from -6 to 6
- doc_bounds: int32 [2, 2], replicated, may hold values from 1 to 1535, as said below
- attn_gain: bfloat16 [2, 2048], P('section'), may hold values from 0.5 to 1.5
- w_query: bfloat16 [2, 2048, 2048], P('section', None, 'wt'), may hold values from -0.125 to 0.125
- w_key: bfloat16 [2, 2048, 512], P('section', None, 'wt'), may hold values from -0.125 to 0.125
- w_value: bfloat16 [2, 2048, 512], P('section', None, 'wt'), may hold values from -0.125 to 0.125
- w_out: bfloat16 [2, 2048, 2048], P('section', 'wt'), may hold values from -0.75 to 0.75
- mlp_gain: bfloat16 [2, 2048], P('section'), may hold values from 0.5 to 1.5
- w_gate: bfloat16 [2, 2048, 8192], P('section', None, 'wt'), may hold values from -0.125 to 0.125
- w_up: bfloat16 [2, 2048, 8192], P('section', None, 'wt'), may hold values from -0.125 to 0.125
- w_down: bfloat16 [2, 8192, 2048], P('section', 'wt'), may hold values from -0.125 to 0.125
Outputs:
- boundary: bfloat16 [2, 2, 1536, 2048], P('section', None, 'ctx', 'wt')
- gain_attn_grad: float32 [2, 2048], P('section', 'ctx')
- query_grad: float32 [2, 2048, 2048], P('section', 'ctx', 'wt')
- key_grad: float32 [2, 2048, 512], P('section', 'ctx', 'wt')
- value_grad: float32 [2, 2048, 512], P('section', 'ctx', 'wt')
- out_grad: float32 [2, 2048, 2048], P('section', 'wt', 'ctx')
- gain_mlp_grad: float32 [2, 2048], P('section', 'ctx')
- gate_grad: float32 [2, 2048, 8192], P('section', 'ctx', 'wt')
- up_grad: float32 [2, 2048, 8192], P('section', 'ctx', 'wt')
- down_grad: float32 [2, 8192, 2048], P('section', 'wt', 'ctx')
The draws below stay inside these ranges and needn't reach their ends.
Inputs may be any that keep to these rules, and one draw needn't show every extreme that they name: `doc_bounds`: row b: document 1 of micro-batch b begins at a position from 1 to 191, document 2 at a position from 1345 to 1535; document 0 begins at 0. In some row document 1 begins at 1, and in some row document 2 begins at 1535.
All inputs are finite; a program needn't handle non-finite values.
Results may differ from the reference program's by a relative error of at most 0.038.
Values may be sent and summed in bfloat16 or wider, within the bound.
A program may use at most 192 MiB of HBM per device.

```python
import jax
import jax.numpy as jnp
from jax import lax

D = 2048
H = 32
KV = 8
HD = 64
FF = 8192
MB = 2
SEQ = 1536
BLK = 192
LAYERS = 2


def draw_doc_bounds(key, part):
    key = jax.random.fold_in(key, 7)
    first_key, last_key, pick_key = jax.random.split(key, 3)
    middle = jax.random.randint(first_key, (MB, 1), 1, BLK)
    final = jax.random.randint(last_key, (MB, 1), SEQ - BLK + 1, SEQ)
    chosen = jax.random.randint(pick_key, (), 0, MB)
    rows = jnp.arange(MB, dtype=jnp.int32)[:, None]
    middle = jnp.where(rows == chosen, 1, middle)
    final = jnp.where(rows == (chosen + 1) % MB, SEQ - 1, final)
    return jnp.concatenate([middle, final], axis=1).astype(jnp.int32)


def levels(stream_key, shape, cuts, low, high):
    def one(dim, blocks):
        steps = jax.random.uniform(jax.random.fold_in(jax.random.fold_in(stream_key, 6), dim), (blocks,), jnp.float32, low / len(cuts), high / len(cuts))
        return jnp.repeat(jnp.exp(steps), shape[dim] // blocks).reshape((-1,) + (1,) * (len(shape) - dim - 1))

    level = one(*cuts[0])
    for cut in cuts[1:]:
        level = level * one(*cut)
    return level


def bell_draw(own_key, dims, spread, bound, shards=(), kind=jnp.bfloat16):
    gain = levels(own_key, dims, shards, -0.22, 0.18) if shards else 1.0
    entries = jax.random.normal(own_key, dims, jnp.float32) * spread * gain
    return jnp.minimum(jnp.maximum(entries, -bound), bound).astype(kind)


def setup_inputs(seed: int = 0) -> dict:
    key_list = jax.random.split(jax.random.key(seed), 13)
    inputs = bell_draw(key_list[0], (MB, SEQ, D), 1.0, 6.0, ((1, 8), (2, 8)))
    cotangent = bell_draw(key_list[1], (MB, SEQ, D), 1.0, 6.0, ((1, 8), (2, 8)))
    doc_bounds = draw_doc_bounds(jax.random.fold_in(key_list[12], 71), 0)
    attn_gain = jnp.clip(1.0 + 0.1 * jax.random.normal(key_list[3], (LAYERS, D), jnp.float32), 0.5, 1.5).astype(jnp.bfloat16)
    w_query = bell_draw(key_list[4], (LAYERS, D, H * HD), D ** -0.5, 0.125, ((0, 2), (2, 8)))
    w_key = bell_draw(key_list[5], (LAYERS, D, KV * HD), D ** -0.5, 0.125, ((0, 2), (2, 8)))
    w_value = bell_draw(key_list[6], (LAYERS, D, KV * HD), D ** -0.5, 0.125, ((0, 2), (2, 8)))
    w_out = bell_draw(key_list[7], (LAYERS, H * HD, D), (H * HD // 32) ** -0.5, 0.75, ((0, 2), (1, 8)))
    mlp_gain = jnp.clip(1.0 + 0.1 * jax.random.normal(key_list[8], (LAYERS, D), jnp.float32), 0.5, 1.5).astype(jnp.bfloat16)
    w_gate = bell_draw(key_list[9], (LAYERS, D, FF), D ** -0.5, 0.125, ((0, 2), (2, 8)))
    w_up = bell_draw(key_list[10], (LAYERS, D, FF), D ** -0.5, 0.125, ((0, 2), (2, 8)))
    w_down = bell_draw(key_list[11], (LAYERS, FF, D), (FF // 4) ** -0.5, 0.125, ((0, 2), (1, 8)))
    return dict(inputs=inputs, cotangent=cotangent, doc_bounds=doc_bounds, attn_gain=attn_gain, w_query=w_query, w_key=w_key, w_value=w_value, w_out=w_out, mlp_gain=mlp_gain, w_gate=w_gate, w_up=w_up, w_down=w_down)


eps = 1e-05
theta = 500000.0
neg_big = -1e+30
highest = lax.Precision.HIGHEST

@jax.custom_vjp
def low(v):
    return lax.optimization_barrier(v.astype(jnp.bfloat16)).astype(jnp.float32)

@jax.custom_vjp
def low_back(v):
    return v

def low_keep(v):
    return (low(v), None)

def low_pass(kept, grad):
    return (grad,)

def back_keep(v):
    return (v, None)

def back_low(kept, grad):
    return (low(grad),)
low.defvjp(low_keep, low_pass)
low_back.defvjp(back_keep, back_low)

def rope_freqs(head_width):
    index_steps = jnp.arange(head_width // 2, dtype=jnp.float32)
    inverse = theta ** (-2.0 * index_steps / head_width)
    wavelen = 2.0 * jnp.pi / inverse
    smooth = (8192.0 / wavelen - 1.0) / 3.0
    blended = (1.0 - smooth) * inverse / 32.0 + smooth * inverse
    return jnp.where(wavelen < 2048.0, inverse, jnp.where(wavelen > 8192.0, inverse / 32.0, blended))

def doc_info(bounds, places):
    starts = jnp.concatenate([jnp.zeros((1,), jnp.int32), bounds.astype(jnp.int32)])
    started = places[:, None] >= starts[None, :]
    doc_ids = lax.optimization_barrier(jnp.sum(started.astype(jnp.int32), axis=1)) - 1
    doc_begin = lax.optimization_barrier(jnp.max(jnp.where(started, starts[None, :], 0), axis=1))
    return (doc_ids, places - doc_begin)

def rope_tables(offsets, head_width):
    angles = offsets.astype(jnp.float32)[:, None] * rope_freqs(head_width)[None, :]
    return (jnp.concatenate([jnp.cos(angles)] * 2, axis=1), jnp.concatenate([jnp.sin(angles)] * 2, axis=1))

def rotate(vectors, cosine_table, sine_table):
    half_width = vectors.shape[-1] // 2
    turned = jnp.concatenate([-vectors[..., half_width:], vectors[..., :half_width]], axis=-1)
    return vectors * cosine_table + turned * sine_table

def product(left, right):
    return jnp.dot(left, right, precision=highest)

def normalize(hidden):
    return hidden * lax.rsqrt(lax.optimization_barrier(jnp.mean(hidden * hidden, axis=-1, keepdims=True)) + eps)

def attention(queries, key_heads, value_heads, visible):
    seq_len = queries.shape[0]
    groups = H // KV
    grouped = queries.reshape(seq_len, KV, groups, HD).transpose(1, 2, 0, 3)

    def one_head(operands):
        query_rows, key_rows, value_rows = operands
        raw_scores = jnp.einsum('gqd,kd->gqk', query_rows, key_rows, precision=highest) * HD ** (-0.5)
        scores = jnp.where(visible[None], low_back(raw_scores), neg_big)
        probabilities = low(jax.nn.softmax(scores, axis=-1))
        return jnp.einsum('gqk,kd->gqd', probabilities, value_rows, precision=highest)
    mixed_heads = lax.map(jax.checkpoint(one_head), (grouped, key_heads.transpose(1, 0, 2), value_heads.transpose(1, 0, 2)))
    return low(low_back(mixed_heads.transpose(2, 0, 1, 3).reshape(seq_len, H * HD)))

def apply_layer(hidden, weights, context):
    gain_attn, query_weight, key_weight, value_weight, out_weight, gain_mlp, gate_weight, up_weight, down_weight = weights
    cosine_table, sine_table, visible = context
    seq_len = hidden.shape[0]
    attn_in = low(normalize(hidden) * gain_attn)
    query_pre = low_back(product(attn_in, query_weight)).reshape(seq_len, H, HD)
    queries = low(rotate(query_pre, cosine_table[:, None, :], sine_table[:, None, :]))
    key_pre = low_back(product(attn_in, key_weight)).reshape(seq_len, KV, HD)
    key_heads = low(rotate(key_pre, cosine_table[:, None, :], sine_table[:, None, :]))
    value_heads = low(low_back(product(attn_in, value_weight))).reshape(seq_len, KV, HD)
    attn_mix = attention(queries, key_heads, value_heads, visible)
    mid = hidden + low_back(product(attn_mix, out_weight))
    mlp_in = low(normalize(mid) * gain_mlp)
    gate = low_back(product(mlp_in, gate_weight))
    up_proj = low_back(product(mlp_in, up_weight))
    inner = low(jax.nn.silu(gate) * up_proj)
    return mid + low_back(product(inner, down_weight))

def reference(inputs, cotangent, doc_bounds, attn_gain, w_query, w_key, w_value, w_out, mlp_gain, w_gate, w_up, w_down):
    params = tuple((array.astype(jnp.float32) for array in (attn_gain, w_query, w_key, w_value, w_out, mlp_gain, w_gate, w_up, w_down)))
    places = jnp.arange(SEQ, dtype=jnp.int32)
    contexts = []
    for batch_index in range(MB):
        doc_ids, offsets = doc_info(doc_bounds[batch_index], places)
        cosine_table, sine_table = rope_tables(offsets, HD)
        visible = (places[None, :] <= places[:, None]) & (doc_ids[None, :] == doc_ids[:, None])
        contexts.append((cosine_table, sine_table, visible))

    def forward(first_input, weights):
        results = []
        for batch_index in range(MB):
            hidden = first_input[batch_index]
            hidden = apply_layer(hidden, tuple((array[0] for array in weights)), contexts[batch_index])
            hidden = low(low_back(hidden))
            hidden = apply_layer(hidden, tuple((array[1] for array in weights)), contexts[batch_index])
            results.append(hidden)
        return jnp.stack(results)
    result, pullback = jax.vjp(forward, inputs.astype(jnp.float32), params)
    grad_inputs, grad_params = pullback(cotangent.astype(jnp.float32))
    boundary = jnp.stack([grad_inputs, result]).astype(jnp.bfloat16)
    return (boundary, grad_params[0], grad_params[1], grad_params[2], grad_params[3], grad_params[4], grad_params[5], grad_params[6], grad_params[7], grad_params[8])
```

```python
import functools

import jax
import jax.numpy as jnp
from jax import lax
from jax.experimental import pallas as pl
from jax.experimental.pallas import tpu as pltpu
from jax.sharding import PartitionSpec as P

HD = 64
eps = 1e-05
theta = 500000.0
neg_big = -1e30
MESH = pl.DeviceIdType.MESH
f32 = jnp.float32
bf16 = jnp.bfloat16
MiB = 1024 * 1024


def rope_freqs(head_width):
    index_steps = jnp.arange(head_width // 2, dtype=jnp.float32)
    inverse = theta ** (-2.0 * index_steps / head_width)
    wavelen = 2.0 * jnp.pi / inverse
    smooth = (8192.0 / wavelen - 1.0) / 3.0
    blended = (1.0 - smooth) * inverse / 32.0 + smooth * inverse
    return jnp.where(
        wavelen < 2048.0, inverse, jnp.where(wavelen > 8192.0, inverse / 32.0, blended)
    )


def doc_begins(bounds, places):
    starts = jnp.concatenate([jnp.zeros((1,), jnp.int32), bounds])
    started = places[:, None] >= starts[None, :]
    return jnp.max(jnp.where(started, starts[None, :], 0), axis=1)


def contract_rows(left, right):
    return lax.dot_general(
        left, right, (((0,), (0,)), ((), ())), preferred_element_type=jnp.float32
    )


def times_transposed(left, right):
    return lax.dot_general(
        left, right, (((1,), (1,)), ((), ())), preferred_element_type=jnp.float32
    )


def greet(peers):
    barrier = pltpu.get_barrier_semaphore()
    for peer in peers:
        pl.semaphore_signal(barrier, inc=1, device_id=peer, device_id_type=MESH)
    pl.semaphore_wait(barrier, len(peers))


def remote(src, dst, send, recv, peer):
    return pltpu.make_async_remote_copy(
        src_ref=src, dst_ref=dst, send_sem=send, recv_sem=recv, device_id=peer,
        device_id_type=MESH,
    )


FAR_FIRST = (2, 1, 3)


class WtPlace:
    def __init__(self, width):
        self.me = lax.axis_index("wt")
        self.z = self.me // 2
        self.core = self.me % 2
        self.sib = self.me + 1 - 2 * self.core
        self.width = width

    def peer(self, k):
        return lax.rem(self.z + k, 4) * 2 + self.core

    def cols(self, index):
        return pl.ds(pl.multiple_of(index * self.width, self.width), self.width)


class Gather:
    def __init__(self, place, out, sems, chunk, rows):
        self.place, self.out, self.chunk, self.rows = place, out, chunk, rows
        self.send, self.recv, self.fsend, self.frecv, self.local = sems

    def piece(self, index):
        return self.out.at[self.rows, self.place.cols(index)]

    def start(self, src):
        p, q = self.place, self.chunk
        mine = self.piece(p.me)
        self.own = pltpu.make_async_copy(src, mine, self.local.at[q])
        self.sent = [
            remote(src, mine, self.send.at[q, k], self.recv.at[q, k], {"wt": p.peer(k)})
            for k in FAR_FIRST
        ]
        self.sent.append(
            remote(src, mine, self.send.at[q, 0], self.recv.at[q, 0], {"wt": p.sib})
        )
        for copy in self.sent:
            copy.start()
        self.own.start()

    def forward(self):
        p, q = self.place, self.chunk
        self.passed = []
        for k in (1, 3, 2):
            got = self.piece(p.peer(4 - k))
            remote(got, got, self.send.at[q, k], self.recv.at[q, k], {"wt": p.sib}).wait_recv()
            copy = remote(got, got, self.fsend.at[q, k], self.frecv.at[q, k], {"wt": p.sib})
            copy.start()
            self.passed.append(copy)

    def finish(self):
        for copy in self.passed:
            copy.wait()
        self.sent[-1].wait_recv()
        for copy in self.sent:
            copy.wait_send()
        self.own.wait()


def gather_scratch(chunks):
    return [pltpu.SemaphoreType.DMA((chunks, 4)) for _ in range(4)] + [
        pltpu.SemaphoreType.DMA((chunks,))
    ]


def greet_wt(place, more=()):
    greet([{"wt": place.sib}] + [{"wt": place.peer(k)} for k in (1, 2, 3)] + list(more))


def gather_kernel(chunks, x, out, *sems):
    place = WtPlace(x.shape[1])
    greet_wt(place)
    rows = x.shape[0] // chunks
    parts = []
    for q in range(chunks):
        chunk_rows = pl.ds(q * rows, rows)
        part = Gather(place, out, sems, q, chunk_rows)
        part.start(x.at[chunk_rows])
        parts.append(part)
    for part in parts:
        part.forward()
    for part in parts:
        part.finish()


def wt_gather(x, collective_id, chunks=2):
    rows, width = x.shape
    return pl.pallas_call(
        functools.partial(gather_kernel, chunks),
        out_shape=jax.ShapeDtypeStruct((rows, 8 * width), x.dtype),
        in_specs=[pl.BlockSpec(memory_space=pltpu.VMEM)],
        out_specs=pl.BlockSpec(memory_space=pl.ANY),
        scratch_shapes=gather_scratch(chunks),
        compiler_params=pltpu.CompilerParams(
            collective_id=collective_id, has_side_effects=True, vmem_limit_bytes=32 * MiB
        ),
        name="gather_wt",
    )(x)


class Reduce:
    def __init__(self, place, part, bufs, chunk, rows):
        self.place, self.part, self.chunk, self.rows = place, part, chunk, rows
        (self.pair, self.out, self.landed, self.s1, self.r1, self.s2, self.r2) = bufs

    def start(self):
        p, q = self.place, self.chunk
        self.first = {}
        for k in (2, 1, 3, 0):
            target = lax.rem(p.z + k, 4) * 2 + 1 - p.core
            copy = remote(
                self.part.at[self.rows, p.cols(target)], self.pair.at[q, k],
                self.s1.at[q, k], self.r1.at[q, k], {"wt": p.sib},
            )
            copy.start()
            self.first[k] = copy

    def pass_on(self):
        p, q = self.place, self.chunk
        self.second = {}
        for k in (2, 1, 3):
            self.first[k].wait_recv()
            own = self.part[self.rows, p.cols(p.peer(k))]
            both = own.astype(f32) + self.pair[q, k].astype(f32)
            self.out[q, k] = both.astype(bf16)
            copy = remote(
                self.out.at[q, k], self.landed.at[q, k], self.s2.at[q, k], self.r2.at[q, k],
                {"wt": p.peer(k)},
            )
            copy.start()
            self.second[k] = copy

    def total(self):
        p, q = self.place, self.chunk
        self.first[0].wait_recv()
        total = self.part[self.rows, p.cols(p.me)].astype(f32) + self.pair[q, 0].astype(f32)
        for k in (1, 3, 2):
            self.second[k].wait_recv()
            total = total + self.landed[q, k].astype(f32)
        return total

    def finish(self):
        for copy in self.first.values():
            copy.wait_send()
        for copy in self.second.values():
            copy.wait_send()


def reduce_scratch(chunks, rows, width):
    return [pltpu.VMEM((chunks, 4, rows, width), bf16) for _ in range(3)] + [
        pltpu.SemaphoreType.DMA((chunks, 4)) for _ in range(4)
    ]


def column(line, blocks):
    eye = lax.broadcasted_iota(jnp.int32, (128, 128), 0) == lax.broadcasted_iota(
        jnp.int32, (128, 128), 1
    )
    parts = [
        jnp.sum(
            jnp.where(eye, jnp.broadcast_to(line[j : j + 1, :], (128, 128)), 0.0),
            axis=1, keepdims=True,
        )
        for j in range(blocks)
    ]
    return jnp.concatenate(parts, axis=0)


def swap_sections(src, dst, send, recv):
    return remote(src, dst, send, recv, {"section": 1 - lax.axis_index("section")})


def forward_mid_kernel(chunks, part, skip, mid, whole, agsrc, *scratch):
    bufs, sems = scratch[:7], scratch[7:]
    place = WtPlace(skip.shape[1])
    greet_wt(place)
    rows = skip.shape[0] // chunks
    spans = [pl.ds(q * rows, rows) for q in range(chunks)]
    sums = [Reduce(place, part, bufs, q, spans[q]) for q in range(chunks)]
    gathers = [Gather(place, whole, sems, q, spans[q]) for q in range(chunks)]
    for one in sums:
        one.start()
    for one in sums:
        one.pass_on()
    for q in range(chunks):
        value = skip[spans[q], :].astype(f32) + sums[q].total()
        mid[spans[q], :] = value
        agsrc[spans[q], :] = value.astype(bf16)
        gathers[q].start(agsrc.at[spans[q]])
    for one in gathers:
        one.forward()
    for one in gathers:
        one.finish()
    for one in sums:
        one.finish()


def forward_mid(part, skip, collective_id, chunks=2):
    rows, width = skip.shape
    return pl.pallas_call(
        functools.partial(forward_mid_kernel, chunks),
        out_shape=(
            jax.ShapeDtypeStruct((rows, width), f32),
            jax.ShapeDtypeStruct((rows, 8 * width), bf16),
        ),
        in_specs=[pl.BlockSpec(memory_space=pltpu.VMEM)] * 2,
        out_specs=(
            pl.BlockSpec(memory_space=pltpu.VMEM),
            pl.BlockSpec(memory_space=pl.ANY),
        ),
        scratch_shapes=[pltpu.VMEM((rows, width), bf16)]
        + reduce_scratch(chunks, rows // chunks, width)
        + gather_scratch(chunks),
        compiler_params=pltpu.CompilerParams(
            collective_id=collective_id, has_side_effects=True, vmem_limit_bytes=32 * MiB
        ),
        name="sum_mid_gather",
    )(part, skip)


def forward_pass_kernel(
    chunks, part, mid, begin, share, whole, agsrc, arrived, xsend, xrecv, *scratch
):
    bufs, sems = scratch[:7], scratch[7:]
    place = WtPlace(mid.shape[1])
    section = lax.axis_index("section")
    greet_wt(place, [{"section": 1 - section}])
    rows = mid.shape[0] // chunks
    spans = [pl.ds(q * rows, rows) for q in range(chunks)]
    sums = [Reduce(place, part, bufs, q, spans[q]) for q in range(chunks)]
    gathers = [Gather(place, whole, sems, q, spans[q]) for q in range(chunks)]
    swaps = []
    for one in sums:
        one.start()
    for one in sums:
        one.pass_on()
    for q in range(chunks):
        agsrc[spans[q], :] = (mid[spans[q], :] + sums[q].total()).astype(bf16)
        swap = swap_sections(
            agsrc.at[spans[q]], arrived.at[spans[q]], xsend.at[q], xrecv.at[q]
        )
        swap.start()
        swaps.append(swap)
    for q in range(chunks):
        swaps[q].wait_recv()
        share[spans[q], :] = jnp.where(
            section == 0, begin[spans[q], :].astype(f32), arrived[spans[q], :].astype(f32)
        ).astype(bf16)
        gathers[q].start(share.at[spans[q]])
    for one in gathers:
        one.forward()
    for one in gathers:
        one.finish()
    for one in sums:
        one.finish()
    for one in swaps:
        one.wait_send()


def forward_pass(part, mid, begin, collective_id, chunks=2):
    rows, width = mid.shape
    return pl.pallas_call(
        functools.partial(forward_pass_kernel, chunks),
        out_shape=(
            jax.ShapeDtypeStruct((rows, width), bf16),
            jax.ShapeDtypeStruct((rows, 8 * width), bf16),
        ),
        in_specs=[pl.BlockSpec(memory_space=pltpu.VMEM)] * 3,
        out_specs=(
            pl.BlockSpec(memory_space=pltpu.VMEM),
            pl.BlockSpec(memory_space=pl.ANY),
        ),
        scratch_shapes=[
            pltpu.VMEM((rows, width), bf16),
            pltpu.VMEM((rows, width), bf16),
            pltpu.SemaphoreType.DMA((chunks,)),
            pltpu.SemaphoreType.DMA((chunks,)),
        ]
        + reduce_scratch(chunks, rows // chunks, width)
        + gather_scratch(chunks),
        compiler_params=pltpu.CompilerParams(
            collective_id=collective_id, has_side_effects=True, vmem_limit_bytes=32 * MiB
        ),
        name="sum_pass_gather",
    )(part, mid, begin)


def forward_last_kernel(chunks, part, mid, result, *bufs):
    place = WtPlace(mid.shape[1])
    greet_wt(place)
    rows = mid.shape[0] // chunks
    spans = [pl.ds(q * rows, rows) for q in range(chunks)]
    sums = [Reduce(place, part, bufs, q, spans[q]) for q in range(chunks)]
    for one in sums:
        one.start()
    for one in sums:
        one.pass_on()
    for q in range(chunks):
        result[spans[q], :] = (mid[spans[q], :] + sums[q].total()).astype(bf16)
    for one in sums:
        one.finish()


def forward_last(part, mid, collective_id, chunks=2):
    rows, width = mid.shape
    return pl.pallas_call(
        functools.partial(forward_last_kernel, chunks),
        out_shape=jax.ShapeDtypeStruct((rows, width), bf16),
        in_specs=[pl.BlockSpec(memory_space=pltpu.VMEM)] * 2,
        out_specs=pl.BlockSpec(memory_space=pltpu.VMEM),
        scratch_shapes=reduce_scratch(chunks, rows // chunks, width),
        compiler_params=pltpu.CompilerParams(
            collective_id=collective_id, has_side_effects=True, vmem_limit_bytes=32 * MiB
        ),
        name="sum_last",
    )(part, mid)


def everyone(place):
    return [lax.rem(place.me + d, 8) for d in range(1, 8)]


class Lines:
    def __init__(self, place, line, slots, send, recv):
        self.line, self.slots = line, slots
        self.copies = [
            remote(line, slots.at[d], send.at[d], recv.at[d], {"wt": lax.rem(place.me + d, 8)})
            for d in range(1, 8)
        ]

    def start(self):
        for copy in self.copies:
            copy.start()

    def total(self):
        total = self.line[...]
        for d, copy in enumerate(self.copies, start=1):
            copy.wait_recv()
            total = total + self.slots[d]
        return total

    def finish(self):
        for copy in self.copies:
            copy.wait_send()


def backward_kernel(
    mode, chunks, part, line, above, own, factor, gain, *rest
):
    if mode == "mid":
        share, piece, whole, agsrc, *scratch = rest
    elif mode == "pass":
        begin, share, whole, agsrc, arrived, xsend, xrecv, *scratch = rest
    else:
        other, share, pieces, piece, gsend, grecv, *scratch = rest
    slots, lsend, lrecv, *scratch = scratch
    bufs, sems = scratch[:7], scratch[7:]
    place = WtPlace(own.shape[1])
    section = lax.axis_index("section")
    greet(
        [{"wt": peer} for peer in everyone(place)]
        + ([{"section": 1 - section}] if mode == "pass" else [])
    )
    rows = own.shape[0] // chunks
    depth = 8 * own.shape[1]
    spans = [pl.ds(q * rows, rows) for q in range(chunks)]
    sums = [Reduce(place, part, bufs, q, spans[q]) for q in range(chunks)]
    gathers = [Gather(place, whole, sems, q, spans[q]) for q in range(chunks)] if (
        mode != "last") else []
    lines = Lines(place, line, slots, lsend, lrecv)
    lines.start()
    for one in sums:
        one.start()
    for one in sums:
        one.pass_on()
    mean = column(lines.total(), own.shape[0] // 128) * (1.0 / depth)
    swaps = []
    terms = jnp.zeros((1, own.shape[1]), f32)
    for q in range(chunks):
        span = spans[q]
        total = sums[q].total()
        scale = factor[span, :]
        normed = own[span, :] * scale
        if mode != "pass":
            terms = terms + jnp.sum(total * normed, axis=0, keepdims=True)
        grad = above[span, :].astype(f32) + scale * (
            total * gain[...] - normed * mean[q * rows : (q + 1) * rows]
        )
        if mode == "mid":
            share[span, :] = grad
            agsrc[span, :] = grad.astype(bf16)
            gathers[q].start(agsrc.at[span])
        elif mode == "pass":
            agsrc[span, :] = grad.astype(bf16)
            swap = swap_sections(agsrc.at[span], arrived.at[span], xsend.at[q], xrecv.at[q])
            swap.start()
            swaps.append(swap)
        else:
            share[span, :] = grad.astype(bf16)
    if mode == "mid":
        piece[...] = jnp.broadcast_to(terms, piece.shape)
    if mode == "pass":
        for q in range(chunks):
            span = spans[q]
            swaps[q].wait_recv()
            share[span, :] = jnp.where(
                section == 1, begin[span, :].astype(f32), arrived[span, :].astype(f32)
            ).astype(bf16)
            gathers[q].start(share.at[span])
    if mode == "last":
        piece[0:8, :] = jnp.broadcast_to(terms, (8, own.shape[1]))
        piece[8:16, :] = other[...]
        copies = [
            remote(
                piece, pieces.at[place.me], gsend.at[d], grecv.at[d],
                {"wt": lax.rem(place.me + d, 8)},
            )
            for d in range(1, 8)
        ]
        for copy in copies:
            copy.start()
        pieces[place.me] = piece[...]
        for copy in copies:
            copy.wait()
    for one in gathers:
        one.forward()
    for one in gathers:
        one.finish()
    for one in sums:
        one.finish()
    for one in swaps:
        one.wait_send()
    lines.finish()


def backward_sum(mode, part, line, above, own, factor, gain, extra, collective_id, chunks=2):
    rows, width = own.shape
    vmem = pl.BlockSpec(memory_space=pltpu.VMEM)
    hbm = pl.BlockSpec(memory_space=pl.ANY)
    whole = jax.ShapeDtypeStruct((rows, 8 * width), bf16)
    if mode == "mid":
        out_shape = (
            jax.ShapeDtypeStruct((rows, width), f32),
            jax.ShapeDtypeStruct((8, width), f32),
            whole,
        )
        out_specs = (vmem, vmem, hbm)
        scratch = [pltpu.VMEM((rows, width), bf16)]
    elif mode == "pass":
        out_shape = (jax.ShapeDtypeStruct((rows, width), bf16), whole)
        out_specs = (vmem, hbm)
        scratch = [pltpu.VMEM((rows, width), bf16)] * 2 + [
            pltpu.SemaphoreType.DMA((chunks,)),
            pltpu.SemaphoreType.DMA((chunks,)),
        ]
    else:
        out_shape = (
            jax.ShapeDtypeStruct((rows, width), bf16),
            jax.ShapeDtypeStruct((8, 16, width), f32),
        )
        out_specs = (vmem, vmem)
        scratch = [
            pltpu.VMEM((16, width), f32),
            pltpu.SemaphoreType.DMA((8,)),
            pltpu.SemaphoreType.DMA((8,)),
        ]
    scratch += [
        pltpu.VMEM((8, 8, 128), f32),
        pltpu.SemaphoreType.DMA((8,)),
        pltpu.SemaphoreType.DMA((8,)),
    ]
    scratch += reduce_scratch(chunks, rows // chunks, width)
    if mode != "last":
        scratch += gather_scratch(chunks)
    operands = [part, line, above, own, factor, gain] + extra
    return pl.pallas_call(
        functools.partial(backward_kernel, mode, chunks),
        out_shape=out_shape,
        in_specs=[vmem] * len(operands),
        out_specs=out_specs,
        scratch_shapes=scratch,
        compiler_params=pltpu.CompilerParams(
            collective_id=collective_id, has_side_effects=True, vmem_limit_bytes=32 * MiB
        ),
        name="sum_back_" + mode,
    )(*operands)


def lanes(shape):
    return lax.broadcasted_iota(jnp.int32, shape, len(shape) - 1)


def turn(u, cosine, sine):
    low_half = jnp.bitwise_and(lanes(u.shape), HD - 1) < HD // 2
    turned = jnp.where(low_half, -pltpu.roll(u, 128 - HD // 2, 1), pltpu.roll(u, HD // 2, 1))
    return u * cosine + turned * sine


def turn_back(y, cosine, sine):
    low_half = jnp.bitwise_and(lanes(y.shape), HD - 1) < HD // 2
    z = y * sine
    turned = jnp.where(low_half, pltpu.roll(z, 128 - HD // 2, 1), -pltpu.roll(z, HD // 2, 1))
    return y * cosine + turned


def kv_gather_kernel(n, kv, cosine, sine, out, mine, send, recv, local):
    me = lax.axis_index("ctx")
    barrier = pltpu.get_barrier_semaphore()
    for d in range(1, n):

        @pl.when(me - d >= 0)
        def _():
            pl.semaphore_signal(
                barrier, inc=1, device_id={"ctx": me - d}, device_id_type=MESH
            )

    rows = kv.shape[0] // 2
    turned = turn(kv[...], cosine[...], sine[...]).astype(bf16)
    mine[0] = turned[:rows]
    mine[1] = turned[rows:]
    own = pltpu.make_async_copy(mine, out.at[me], local)
    own.start()

    @pl.when(me < n - 1)
    def _():
        pl.semaphore_wait(barrier, n - 1 - me)

    def copy(d):
        return remote(mine, out.at[me], send.at[d], recv.at[d], {"ctx": lax.rem(me + d, n)})

    for d in range(1, n):

        @pl.when(me + d < n)
        def _():
            copy(d).start()

    for d in range(1, n):

        @pl.when(me - d >= 0)
        def _():
            copy(d).wait_recv()

    for d in range(1, n):

        @pl.when(me + d < n)
        def _():
            copy(d).wait_send()

    own.wait()


def kv_gather(kv, cosine, sine, collective_id):
    n = 8
    rows = kv.shape[0] // 2
    return pl.pallas_call(
        functools.partial(kv_gather_kernel, n),
        out_shape=jax.ShapeDtypeStruct((n, 2, rows, 128), bf16),
        in_specs=[pl.BlockSpec(memory_space=pltpu.VMEM)] * 3,
        out_specs=pl.BlockSpec(memory_space=pl.ANY),
        scratch_shapes=[
            pltpu.VMEM((2, rows, 128), bf16),
            pltpu.SemaphoreType.DMA((n,)),
            pltpu.SemaphoreType.DMA((n,)),
            pltpu.SemaphoreType.DMA,
        ],
        compiler_params=pltpu.CompilerParams(
            collective_id=collective_id, has_side_effects=True, vmem_limit_bytes=32 * MiB
        ),
        name="gather_kv",
    )(kv, cosine, sine)


def kv_sum_kernel(n, terms, cosine, sine, out, slots, total, send, recv):
    me = lax.axis_index("ctx")
    barrier = pltpu.get_barrier_semaphore()
    for d in range(1, n):

        @pl.when(me + d < n)
        def _():
            pl.semaphore_signal(
                barrier, inc=1, device_id={"ctx": lax.rem(me + d, n)}, device_id_type=MESH
            )

    @pl.when(me > 0)
    def _():
        pl.semaphore_wait(barrier, me)

    def copy(d):
        back = lax.rem(me + n - d, n)
        return remote(terms.at[back], slots.at[d], send.at[d], recv.at[d], {"ctx": back})

    for d in range(1, n):

        @pl.when(me - d >= 0)
        def _():
            copy(d).start()

    total[...] = terms[me].astype(f32)
    for d in range(1, n):

        @pl.when(me + d < n)
        def _():
            copy(d).wait_recv()
            total[...] += slots[d].astype(f32)

    rows = terms.shape[2]
    for b in range(2):
        span = pl.ds(b * rows, rows)
        out[span, :] = turn_back(total[b], cosine[span, :], sine[span, :]).astype(bf16)
    for d in range(1, n):

        @pl.when(me - d >= 0)
        def _():
            copy(d).wait_send()


def kv_sum(terms, cosine, sine, collective_id):
    n, two, rows, width = terms.shape
    return pl.pallas_call(
        functools.partial(kv_sum_kernel, n),
        out_shape=jax.ShapeDtypeStruct((2 * rows, width), bf16),
        in_specs=[pl.BlockSpec(memory_space=pltpu.VMEM)] * 3,
        out_specs=pl.BlockSpec(memory_space=pltpu.VMEM),
        scratch_shapes=[
            pltpu.VMEM((n, 2, rows, width), bf16),
            pltpu.VMEM((2, rows, width), f32),
            pltpu.SemaphoreType.DMA((n,)),
            pltpu.SemaphoreType.DMA((n,)),
        ],
        compiler_params=pltpu.CompilerParams(
            collective_id=collective_id, has_side_effects=True, vmem_limit_bytes=32 * MiB
        ),
        name="sum_kv",
    )(terms, cosine, sine)


def visible_keys(bounds, b, key_block, me, rows, heads):
    row = lax.broadcasted_iota(jnp.int32, (1, heads * rows), 1)
    for head in range(1, heads):
        row = row - jnp.where(lanes((1, heads * rows)) >= head * rows, rows, 0)
    place = me * rows + row
    first, second = bounds[b, 0], bounds[b, 1]
    begin = jnp.where(place >= second, second, jnp.where(place >= first, first, 0))
    key = key_block * rows + lax.broadcasted_iota(jnp.int32, (rows, 1), 0)
    return (key <= place) & (key >= begin)


def stack_queries(flat, cosine, sine, b, rows, stacked):
    span = pl.ds(b * rows, rows)
    low = lanes((rows, 128)) < HD
    for pair in range(2):
        u = turn(flat[span, 128 * pair : 128 * pair + 128], cosine[span, :], sine[span, :])
        u = u.astype(bf16).astype(f32) * (HD**-0.5)
        even = jnp.where(low, u, 0.0)
        odd = jnp.where(low, pltpu.roll(u, HD, 1), 0.0)
        stacked[b, pl.ds(2 * pair * rows, rows), :] = even.astype(bf16)
        stacked[b, pl.ds((2 * pair + 1) * rows, rows), :] = odd.astype(bf16)


def attention_kernel(bounds, flat, cosine, sine, kv, mix, logs, mixed, stacked, acc):
    me = lax.axis_index("ctx")
    rows = kv.shape[2]
    heads = 4
    for b in range(2):
        stack_queries(flat, cosine, sine, b, rows, stacked)
    acc[...] = jnp.zeros_like(acc)

    def block(j, carry):
        after = []
        for b in range(2):
            peak, total = carry[2 * b : 2 * b + 2]
            keys = kv[j, b]
            scores = times_transposed(keys, stacked[b])
            scores = jnp.where(visible_keys(bounds, b, j, me, rows, heads), scores, neg_big)
            new_peak = jnp.maximum(peak, jnp.max(scores, axis=0, keepdims=True))
            shrink = jnp.exp(peak - new_peak)
            weight = jnp.exp(scores - new_peak)
            total = total * shrink + jnp.sum(weight, axis=0, keepdims=True)
            acc[b] = acc[b] * shrink + contract_rows(keys, weight.astype(bf16))
            after += [new_peak, total]
        return tuple(after)

    zero = jnp.zeros((1, heads * rows), f32)
    done = lax.fori_loop(0, me + 1, block, (zero + neg_big, zero) * 2)
    low = lanes((rows, 128)) < HD
    for b in range(2):
        peak, total = done[2 * b : 2 * b + 2]
        out = acc[b] / total
        mixed[b] = out
        logs[b] = peak + jnp.log(total)
        upright = out.T
        for pair in range(2):
            even = upright[2 * pair * rows : (2 * pair + 1) * rows]
            odd = upright[(2 * pair + 1) * rows : (2 * pair + 2) * rows]
            both = jnp.where(low, pltpu.roll(even, HD, 1), odd)
            mix[pl.ds(b * rows, rows), 128 * pair : 128 * pair + 128] = both.astype(bf16)


def attention(bounds, flat, cosine, sine, kv):
    rows = kv.shape[2]
    vmem = pl.BlockSpec(memory_space=pltpu.VMEM)
    return pl.pallas_call(
        attention_kernel,
        out_shape=(
            jax.ShapeDtypeStruct((2 * rows, 256), bf16),
            jax.ShapeDtypeStruct((2, 1, 4 * rows), f32),
            jax.ShapeDtypeStruct((2, 128, 4 * rows), f32),
        ),
        in_specs=[pl.BlockSpec(memory_space=pltpu.SMEM)] + [vmem] * 4,
        out_specs=(vmem, vmem, vmem),
        scratch_shapes=[
            pltpu.VMEM((2, 4 * rows, 128), bf16),
            pltpu.VMEM((2, 128, 4 * rows), f32),
        ],
        compiler_params=pltpu.CompilerParams(vmem_limit_bytes=40 * MiB),
        name="attention",
    )(bounds, flat, cosine, sine, kv)


def attention_back_kernel(
    bounds, flat, cosine, sine, kv, logs, mixed, grad, out, terms, stacked, grads, acc
):
    me = lax.axis_index("ctx")
    rows = kv.shape[2]
    heads = 4
    low = lanes((rows, 128)) < HD
    deltas = []
    for b in range(2):
        stack_queries(flat, cosine, sine, b, rows, stacked)
        for pair in range(2):
            u = grad[pl.ds(b * rows, rows), 128 * pair : 128 * pair + 128].astype(f32)
            even = jnp.where(low, 0.0, pltpu.roll(u, HD, 1))
            odd = jnp.where(low, 0.0, u)
            grads[b, pl.ds(2 * pair * rows, rows), :] = even.astype(bf16)
            grads[b, pl.ds((2 * pair + 1) * rows, rows), :] = odd.astype(bf16)
        deltas.append(
            jnp.sum(mixed[b] * grads[b].astype(f32).T, axis=0, keepdims=True)
        )
    acc[...] = jnp.zeros_like(acc)

    def block(j, carry):
        for b in range(2):
            keys = kv[j, b]
            scores = times_transposed(keys, stacked[b])
            probs = jnp.where(
                visible_keys(bounds, b, j, me, rows, heads), jnp.exp(scores - logs[b]), 0.0
            )
            grad_probs = times_transposed(keys, grads[b])
            grad_scores = (probs * (grad_probs - deltas[b])).astype(bf16)
            acc[b] += contract_rows(keys, grad_scores)
            terms[j, b] = (
                jnp.dot(grad_scores, stacked[b], preferred_element_type=f32)
                + jnp.dot(probs.astype(bf16), grads[b], preferred_element_type=f32)
            ).astype(bf16)
        return carry

    lax.fori_loop(0, me + 1, block, 0)
    for b in range(2):
        span = pl.ds(b * rows, rows)
        upright = acc[b].T * (HD**-0.5)
        for pair in range(2):
            even = upright[2 * pair * rows : (2 * pair + 1) * rows]
            odd = upright[(2 * pair + 1) * rows : (2 * pair + 2) * rows]
            both = jnp.where(low, even, pltpu.roll(odd, HD, 1))
            out[span, 128 * pair : 128 * pair + 128] = turn_back(
                both, cosine[span, :], sine[span, :]
            ).astype(bf16)


def attention_back(bounds, flat, cosine, sine, kv, logs, mixed, grad):
    rows = kv.shape[2]
    vmem = pl.BlockSpec(memory_space=pltpu.VMEM)
    return pl.pallas_call(
        attention_back_kernel,
        out_shape=(
            jax.ShapeDtypeStruct((2 * rows, 256), bf16),
            jax.ShapeDtypeStruct(kv.shape, bf16),
        ),
        in_specs=[pl.BlockSpec(memory_space=pltpu.SMEM)] + [vmem] * 7,
        out_specs=(vmem, vmem),
        scratch_shapes=[
            pltpu.VMEM((2, 4 * rows, 128), bf16),
            pltpu.VMEM((2, 4 * rows, 128), bf16),
            pltpu.VMEM((2, 128, 4 * rows), f32),
        ],
        compiler_params=pltpu.CompilerParams(vmem_limit_bytes=40 * MiB),
        name="attention_back",
    )(bounds, flat, cosine, sine, kv, logs, mixed, grad)


def owners_kernel(n, dims, *refs):
    count = len(dims)
    arrays, outs = refs[:count], refs[count : 2 * count]
    send, recv, local = refs[2 * count :]
    me = lax.axis_index("ctx")
    greet([{"ctx": lax.rem(me + d, n)} for d in range(1, n)])

    def cut(array, dim, owner):
        length = array.shape[dim] // n
        span = pl.ds(pl.multiple_of(owner * length, length), length)
        return array.at[span] if dim == 0 else array.at[:, span]

    copies = []
    for i in range(count):
        for d in range(1, n):
            owner = lax.rem(me + d, n)
            copy = remote(
                cut(arrays[i], dims[i], owner), outs[i].at[me], send.at[i, d], recv.at[i, d],
                {"ctx": owner},
            )
            copy.start()
            copies.append(copy)
    for i in range(count):
        own = pltpu.make_async_copy(
            cut(arrays[i], dims[i], me), outs[i].at[me], local.at[i]
        )
        own.start()
        copies.append(own)
    for copy in copies:
        copy.wait()


def to_owners(arrays, dims, collective_id):
    n = 8
    shapes = []
    for array, dim in zip(arrays, dims):
        shape = list(array.shape)
        shape[dim] //= n
        shapes.append(jax.ShapeDtypeStruct((n, *shape), array.dtype))
    hbm = pl.BlockSpec(memory_space=pl.ANY)
    return pl.pallas_call(
        functools.partial(owners_kernel, n, dims),
        out_shape=tuple(shapes),
        in_specs=[hbm] * len(arrays),
        out_specs=(hbm,) * len(arrays),
        scratch_shapes=[
            pltpu.SemaphoreType.DMA((len(arrays), n)),
            pltpu.SemaphoreType.DMA((len(arrays), n)),
            pltpu.SemaphoreType.DMA((len(arrays),)),
        ],
        compiler_params=pltpu.CompilerParams(
            collective_id=collective_id, has_side_effects=True
        ),
        name="grads_to_owners",
    )(*arrays)


def per_device(
    inputs,
    cotangent,
    doc_bounds,
    attn_gain,
    w_query,
    w_key,
    w_value,
    w_out,
    mlp_gain,
    w_gate,
    w_up,
    w_down,
):
    ctx_rank = lax.axis_index("ctx")
    wt_rank = lax.axis_index("wt")
    micro_count, block_rows, share_width = inputs.shape
    rows = micro_count * block_rows
    gain_attn = attn_gain.astype(f32)
    gain_mlp = mlp_gain.astype(f32)
    own_gain_attn = lax.dynamic_slice_in_dim(gain_attn, wt_rank * share_width, share_width, 1)
    own_gain_mlp = lax.dynamic_slice_in_dim(gain_mlp, wt_rank * share_width, share_width, 1)
    w_qkv = jnp.concatenate([w_query[0], w_key[0], w_value[0]], axis=1)
    w_o, w_g, w_u, w_d = w_out[0], w_gate[0], w_up[0], w_down[0]
    begin = inputs.reshape(rows, share_width)
    cot = cotangent.reshape(rows, share_width)

    places = ctx_rank * block_rows + jnp.arange(block_rows, dtype=jnp.int32)
    offsets = jnp.concatenate(
        [places - doc_begins(doc_bounds[b], places) for b in range(micro_count)]
    )
    angles = offsets.astype(f32)[:, None] * rope_freqs(HD)[None, :]
    cos_half, sin_half = jnp.cos(angles), jnp.sin(angles)
    cosine = jnp.concatenate([cos_half] * 4, axis=1)
    sine = jnp.concatenate([sin_half] * 4, axis=1)
    key_lane = jnp.arange(128)[None, :] < HD
    kv_cosine = jnp.where(key_lane, cosine, 1.0)
    kv_sine = jnp.where(key_lane, sine, 0.0)

    def forward(whole, share, tick):
        hidden = whole.astype(f32)
        factor = lax.rsqrt(jnp.mean(hidden * hidden, axis=-1, keepdims=True) + eps)
        attn_in = (hidden * factor * gain_attn).astype(bf16)
        pre = jnp.dot(attn_in, w_qkv, preferred_element_type=f32)
        q_pre, kv_pre = pre[:, :256], pre[:, 256:]
        kv = kv_gather(kv_pre, kv_cosine, kv_sine, 1)
        mix, logs, mixed = attention(doc_bounds, q_pre, cosine, sine, kv)
        part = jnp.dot(mix, w_o, preferred_element_type=f32).astype(bf16)
        mid, mid_whole = forward_mid(part, share, 2)
        mid_wide = mid_whole.astype(f32)
        mid_factor = lax.rsqrt(jnp.mean(mid_wide * mid_wide, axis=-1, keepdims=True) + eps)
        mlp_in = (mid_wide * mid_factor * gain_mlp).astype(bf16)
        gate = jnp.dot(mlp_in, w_g, preferred_element_type=f32)
        up = jnp.dot(mlp_in, w_u, preferred_element_type=f32)
        inner = (jax.nn.silu(gate) * up).astype(bf16)
        part = jnp.dot(inner, w_d, preferred_element_type=f32).astype(bf16)
        saved = dict(
            whole=whole, share=share, factor=factor, attn_in=attn_in, q_pre=q_pre, kv=kv,
            mix=mix, logs=logs, mixed=mixed, mid=mid, mid_whole=mid_whole,
            mid_factor=mid_factor, mlp_in=mlp_in, gate=gate, up=up, inner=inner,
        )
        return part, saved

    def line_of(part, whole, factor, gain):
        dots = jnp.sum(part * (whole.astype(f32) * factor * gain), axis=1)
        return jnp.concatenate(
            [dots.reshape(rows // 128, 128), jnp.zeros((8 - rows // 128, 128), f32)]
        )

    def backward(grad, grad_share, saved):
        gate, up = saved["gate"], saved["up"]
        grad_inner = times_transposed(grad, w_d)
        sigmoid = jax.nn.sigmoid(gate)
        grad_gate = (grad_inner * up * sigmoid * (1.0 + gate * (1.0 - sigmoid))).astype(bf16)
        grad_up = (grad_inner * gate * sigmoid).astype(bf16)
        part = times_transposed(grad_gate, w_g) + times_transposed(grad_up, w_u)
        line = line_of(part, saved["mid_whole"], saved["mid_factor"], gain_mlp)
        grad_mid, piece, grad_attn = backward_sum(
            "mid", part.astype(bf16), line, grad_share, saved["mid"], saved["mid_factor"],
            own_gain_mlp, [], 3,
        )
        grad_mix = times_transposed(grad_attn, w_o).astype(bf16)
        grad_query, terms = attention_back(
            doc_bounds, saved["q_pre"], cosine, sine, saved["kv"], saved["logs"],
            saved["mixed"], grad_mix,
        )
        grad_kv = kv_sum(terms, kv_cosine, kv_sine, 4)
        grad_pre = jnp.concatenate([grad_query, grad_kv], axis=1)
        part = times_transposed(grad_pre, w_qkv)
        line = line_of(part, saved["whole"], saved["factor"], gain_attn)
        operands = (
            part.astype(bf16), line, grad_mid, saved["share"].astype(f32), saved["factor"],
            own_gain_attn,
        )
        return operands, dict(
            grad_gate=grad_gate, grad_up=grad_up, grad_attn=grad_attn, grad_pre=grad_pre,
            piece=piece,
        )

    whole_cot = wt_gather(cot, 5)
    part, saved = forward(wt_gather(begin, 6), begin, 0)
    share, whole = forward_pass(part, saved["mid"], begin, 7)
    part, saved = forward(whole, share, 1)
    result = forward_last(part, saved["mid"], 8)

    operands, _ = backward(whole_cot, cot, saved)
    section = lax.axis_index("section")
    grad_share, grad = backward_sum("pass", *operands, [cot], 9)
    operands, kept = backward(grad, grad_share, saved)
    first_grad, pieces = backward_sum("last", *operands, [kept["piece"]], 10)

    arrays = (
        contract_rows(saved["inner"], grad).astype(bf16),
        contract_rows(saved["mlp_in"], kept["grad_gate"]).astype(bf16),
        contract_rows(saved["mlp_in"], kept["grad_up"]).astype(bf16),
        contract_rows(saved["mix"], kept["grad_attn"]).astype(bf16),
        contract_rows(saved["attn_in"], kept["grad_pre"]).astype(bf16),
        pieces.reshape(8 * 16, share_width),
    )
    sent = to_owners(arrays, (1, 0, 0, 1, 0, 0), 11)
    down, gate, up, out, pre, gains = (jnp.sum(one.astype(f32), axis=0) for one in sent)
    boundary = jnp.where(section == 0, first_grad, result)
    return (
        boundary.reshape(1, micro_count, block_rows, share_width),
        gains[0][None],
        pre[:, :256][None],
        pre[:, 256:320][None],
        pre[:, 320:][None],
        out[None],
        gains[8][None],
        gate[None],
        up[None],
        down[None],
    )


def solution(mesh):
    return jax.shard_map(
        per_device,
        mesh=mesh,
        in_specs=(
            P(None, "ctx", "wt"),
            P(None, "ctx", "wt"),
            P(),
            P("section", None),
            P("section", None, "wt"),
            P("section", None, "wt"),
            P("section", None, "wt"),
            P("section", "wt", None),
            P("section", None),
            P("section", None, "wt"),
            P("section", None, "wt"),
            P("section", "wt", None),
        ),
        out_specs=(
            P("section", None, "ctx", "wt"),
            P("section", "ctx"),
            P("section", "ctx", "wt"),
            P("section", "ctx", "wt"),
            P("section", "ctx", "wt"),
            P("section", "wt", "ctx"),
            P("section", "ctx"),
            P("section", "ctx", "wt"),
            P("section", "ctx", "wt"),
            P("section", "wt", "ctx"),
        ),
        check_vma=False,
    )
```

```python
import functools

import jax
import jax.numpy as jnp
from jax import lax
from jax.experimental import pallas as pl
from jax.experimental.pallas import tpu as pltpu
from jax.sharding import PartitionSpec as P

HD = 64
eps = 1e-05
theta = 500000.0
neg_big = -1e30
MESH = pl.DeviceIdType.MESH
f32 = jnp.float32
bf16 = jnp.bfloat16
MiB = 1024 * 1024


def rope_freqs(head_width):
    index_steps = jnp.arange(head_width // 2, dtype=jnp.float32)
    inverse = theta ** (-2.0 * index_steps / head_width)
    wavelen = 2.0 * jnp.pi / inverse
    smooth = (8192.0 / wavelen - 1.0) / 3.0
    blended = (1.0 - smooth) * inverse / 32.0 + smooth * inverse
    return jnp.where(
        wavelen < 2048.0, inverse, jnp.where(wavelen > 8192.0, inverse / 32.0, blended)
    )


def doc_begins(bounds, places):
    starts = jnp.concatenate([jnp.zeros((1,), jnp.int32), bounds])
    started = places[:, None] >= starts[None, :]
    return jnp.max(jnp.where(started, starts[None, :], 0), axis=1)


def contract_rows(left, right):
    return lax.dot_general(
        left, right, (((0,), (0,)), ((), ())), preferred_element_type=jnp.float32
    )


def times_transposed(left, right):
    return lax.dot_general(
        left, right, (((1,), (1,)), ((), ())), preferred_element_type=jnp.float32
    )


def greet(peers):
    barrier = pltpu.get_barrier_semaphore()
    for peer in peers:
        pl.semaphore_signal(barrier, inc=1, device_id=peer, device_id_type=MESH)
    pl.semaphore_wait(barrier, len(peers))


def remote(src, dst, send, recv, peer):
    return pltpu.make_async_remote_copy(
        src_ref=src, dst_ref=dst, send_sem=send, recv_sem=recv, device_id=peer,
        device_id_type=MESH,
    )


class WtPlace:
    def __init__(self, width):
        self.me = lax.axis_index("wt")
        self.z = self.me // 2
        self.core = self.me % 2
        self.sib = self.me + 1 - 2 * self.core
        self.width = width

    def peer(self, k):
        return lax.rem(self.z + k + 4, 4) * 2 + self.core

    def cols(self, index):
        return pl.ds(pl.multiple_of(index * self.width, self.width), self.width)


def way(chunk):
    return 1 if chunk % 2 == 0 else -1


class Gather:
    def __init__(self, place, out, sems, chunk, rows):
        self.place, self.out, self.chunk, self.rows = place, out, chunk, rows
        self.send, self.recv, self.fsend, self.frecv, self.local = sems
        self.s = way(chunk)

    def piece(self, index):
        return self.out.at[self.rows, self.place.cols(index)]

    def aside(self, k):
        p, q = self.place, self.chunk
        got = self.piece(p.peer(-k))
        return remote(got, got, self.fsend.at[q, k % 4], self.frecv.at[q, k % 4], {"wt": p.sib})

    def start(self, src):
        p, q = self.place, self.chunk
        mine = self.piece(p.me)
        self.own = pltpu.make_async_copy(src, mine, self.local.at[q])
        self.sent = []
        for hop in (self.s, -self.s):
            k = hop % 4
            copy = remote(
                src, mine, self.send.at[q, k], self.recv.at[q, k], {"wt": p.peer(hop)}
            )
            copy.start()
            self.sent.append(copy)
        copy = remote(src, mine, self.fsend.at[q, 0], self.frecv.at[q, 0], {"wt": p.sib})
        copy.start()
        self.sent.append(copy)
        self.own.start()

    def forward(self):
        p, q, s = self.place, self.chunk, self.s
        self.passed = []
        self.sent[0].wait_recv()
        got = self.piece(p.peer(-s))
        copy = remote(got, got, self.send.at[q, 2], self.recv.at[q, 2], {"wt": p.peer(s)})
        copy.start()
        self.sent.append(copy)
        near = self.aside(s)
        near.start()
        self.passed.append(near)

    def forward_more(self):
        s = self.s
        self.sent[1].wait_recv()
        near = self.aside(-s)
        near.start()
        self.passed.append(near)
        self.sent[3].wait_recv()
        near = self.aside(2)
        near.start()
        self.passed.append(near)

    def finish(self):
        for copy in self.passed:
            copy.wait()
        self.sent[2].wait_recv()
        for copy in self.sent:
            copy.wait_send()
        self.own.wait()


def gather_all(gathers):
    for one in gathers:
        one.forward()
    for one in gathers:
        one.forward_more()
    for one in gathers:
        one.finish()


def gather_scratch(chunks):
    return [pltpu.SemaphoreType.DMA((chunks, 4)) for _ in range(4)] + [
        pltpu.SemaphoreType.DMA((chunks,))
    ]


def greet_wt(place, more=()):
    greet([{"wt": place.sib}] + [{"wt": place.peer(k)} for k in (1, -1)] + list(more))


def gather_kernel(chunks, x, out, *sems):
    place = WtPlace(x.shape[1])
    greet_wt(place)
    rows = x.shape[0] // chunks
    parts = []
    for q in range(chunks):
        chunk_rows = pl.ds(q * rows, rows)
        part = Gather(place, out, sems, q, chunk_rows)
        part.start(x.at[chunk_rows])
        parts.append(part)
    gather_all(parts)


def wt_gather(x, collective_id, chunks=4):
    rows, width = x.shape
    return pl.pallas_call(
        functools.partial(gather_kernel, chunks),
        out_shape=jax.ShapeDtypeStruct((rows, 8 * width), x.dtype),
        in_specs=[pl.BlockSpec(memory_space=pltpu.VMEM)],
        out_specs=pl.BlockSpec(memory_space=pl.ANY),
        scratch_shapes=gather_scratch(chunks),
        compiler_params=pltpu.CompilerParams(
            collective_id=collective_id, has_side_effects=True, vmem_limit_bytes=32 * MiB
        ),
        name="gather_wt",
    )(x)


class Reduce:
    def __init__(self, place, part, bufs, chunk, rows):
        self.place, self.part, self.chunk, self.rows = place, part, chunk, rows
        (self.pair, self.out, self.landed, self.s1, self.r1, self.s2, self.r2) = bufs
        self.s = way(chunk)

    def start(self):
        p, q, s = self.place, self.chunk, self.s
        self.first = {}
        for k in (2, -s, s, 0):
            target = lax.rem(p.z + k + 4, 4) * 2 + 1 - p.core
            copy = remote(
                self.part.at[self.rows, p.cols(target)], self.pair.at[q, k % 4],
                self.s1.at[q, k % 4], self.r1.at[q, k % 4], {"wt": p.sib},
            )
            copy.start()
            self.first[k] = copy

    def both(self, k):
        p, q = self.place, self.chunk
        self.first[k].wait_recv()
        own = self.part[self.rows, p.cols(p.peer(k))]
        return own.astype(f32) + self.pair[q, k % 4].astype(f32)

    def onward(self, k, value, hop):
        p, q = self.place, self.chunk
        self.out[q, k % 4] = value.astype(bf16)
        copy = remote(
            self.out.at[q, k % 4], self.landed.at[q, k % 4], self.s2.at[q, k % 4],
            self.r2.at[q, k % 4], {"wt": p.peer(hop)},
        )
        copy.start()
        self.second[k] = copy

    def pass_on(self):
        self.second = {}
        self.onward(2, self.both(2), self.s)
        self.onward(-self.s, self.both(-self.s), -self.s)

    def pass_more(self):
        q, s = self.chunk, self.s
        value = self.both(s)
        self.second[2].wait_recv()
        self.onward(s, value + self.landed[q, 2].astype(f32), s)

    def total(self):
        q = self.chunk
        total = self.both(0)
        for k in (-self.s, self.s):
            self.second[k].wait_recv()
            total = total + self.landed[q, k % 4].astype(f32)
        return total

    def finish(self):
        for copy in self.first.values():
            copy.wait_send()
        for copy in self.second.values():
            copy.wait_send()


def reduce_scratch(chunks, rows, width):
    return [pltpu.VMEM((chunks, 4, rows, width), bf16) for _ in range(3)] + [
        pltpu.SemaphoreType.DMA((chunks, 4)) for _ in range(4)
    ]


def column(line, blocks):
    eye = lax.broadcasted_iota(jnp.int32, (128, 128), 0) == lax.broadcasted_iota(
        jnp.int32, (128, 128), 1
    )
    parts = [
        jnp.sum(
            jnp.where(eye, jnp.broadcast_to(line[j : j + 1, :], (128, 128)), 0.0),
            axis=1, keepdims=True,
        )
        for j in range(blocks)
    ]
    return jnp.concatenate(parts, axis=0)


def swap_sections(src, dst, send, recv):
    return remote(src, dst, send, recv, {"section": 1 - lax.axis_index("section")})


def forward_mid_kernel(chunks, part, skip, mid, whole, agsrc, *scratch):
    bufs, sems = scratch[:7], scratch[7:]
    place = WtPlace(skip.shape[1])
    greet_wt(place)
    rows = skip.shape[0] // chunks
    spans = [pl.ds(q * rows, rows) for q in range(chunks)]
    sums = [Reduce(place, part, bufs, q, spans[q]) for q in range(chunks)]
    gathers = [Gather(place, whole, sems, q, spans[q]) for q in range(chunks)]
    for one in sums:
        one.start()
    for one in sums:
        one.pass_on()
    for one in sums:
        one.pass_more()
    for q in range(chunks):
        value = skip[spans[q], :].astype(f32) + sums[q].total()
        mid[spans[q], :] = value
        agsrc[spans[q], :] = value.astype(bf16)
        gathers[q].start(agsrc.at[spans[q]])
    gather_all(gathers)
    for one in sums:
        one.finish()


def forward_mid(part, skip, collective_id, chunks=4):
    rows, width = skip.shape
    return pl.pallas_call(
        functools.partial(forward_mid_kernel, chunks),
        out_shape=(
            jax.ShapeDtypeStruct((rows, width), f32),
            jax.ShapeDtypeStruct((rows, 8 * width), bf16),
        ),
        in_specs=[pl.BlockSpec(memory_space=pltpu.VMEM)] * 2,
        out_specs=(
            pl.BlockSpec(memory_space=pltpu.VMEM),
            pl.BlockSpec(memory_space=pl.ANY),
        ),
        scratch_shapes=[pltpu.VMEM((rows, width), bf16)]
        + reduce_scratch(chunks, rows // chunks, width)
        + gather_scratch(chunks),
        compiler_params=pltpu.CompilerParams(
            collective_id=collective_id, has_side_effects=True, vmem_limit_bytes=32 * MiB
        ),
        name="sum_mid_gather",
    )(part, skip)


def forward_pass_kernel(
    chunks, part, mid, begin, share, whole, agsrc, arrived, xsend, xrecv, *scratch
):
    bufs, sems = scratch[:7], scratch[7:]
    place = WtPlace(mid.shape[1])
    section = lax.axis_index("section")
    greet_wt(place, [{"section": 1 - section}])
    rows = mid.shape[0] // chunks
    spans = [pl.ds(q * rows, rows) for q in range(chunks)]
    sums = [Reduce(place, part, bufs, q, spans[q]) for q in range(chunks)]
    gathers = [Gather(place, whole, sems, q, spans[q]) for q in range(chunks)]
    swaps = []
    for one in sums:
        one.start()
    for one in sums:
        one.pass_on()
    for one in sums:
        one.pass_more()
    for q in range(chunks):
        agsrc[spans[q], :] = (mid[spans[q], :] + sums[q].total()).astype(bf16)
        swap = swap_sections(
            agsrc.at[spans[q]], arrived.at[spans[q]], xsend.at[q], xrecv.at[q]
        )
        swap.start()
        swaps.append(swap)
    for q in range(chunks):
        swaps[q].wait_recv()
        share[spans[q], :] = jnp.where(
            section == 0, begin[spans[q], :].astype(f32), arrived[spans[q], :].astype(f32)
        ).astype(bf16)
        gathers[q].start(share.at[spans[q]])
    gather_all(gathers)
    for one in sums:
        one.finish()
    for one in swaps:
        one.wait_send()


def forward_pass(part, mid, begin, collective_id, chunks=4):
    rows, width = mid.shape
    return pl.pallas_call(
        functools.partial(forward_pass_kernel, chunks),
        out_shape=(
            jax.ShapeDtypeStruct((rows, width), bf16),
            jax.ShapeDtypeStruct((rows, 8 * width), bf16),
        ),
        in_specs=[pl.BlockSpec(memory_space=pltpu.VMEM)] * 3,
        out_specs=(
            pl.BlockSpec(memory_space=pltpu.VMEM),
            pl.BlockSpec(memory_space=pl.ANY),
        ),
        scratch_shapes=[
            pltpu.VMEM((rows, width), bf16),
            pltpu.VMEM((rows, width), bf16),
            pltpu.SemaphoreType.DMA((chunks,)),
            pltpu.SemaphoreType.DMA((chunks,)),
        ]
        + reduce_scratch(chunks, rows // chunks, width)
        + gather_scratch(chunks),
        compiler_params=pltpu.CompilerParams(
            collective_id=collective_id, has_side_effects=True, vmem_limit_bytes=32 * MiB
        ),
        name="sum_pass_gather",
    )(part, mid, begin)


def add_up(dst, sources, step=64):
    def some(i, carry):
        span = pl.ds(pl.multiple_of(i * step, step), step)
        total = sources[0][span, :].astype(f32)
        for source in sources[1:]:
            total = total + source[span, :].astype(f32)
        dst[span, :] = total.astype(dst.dtype)
        return carry

    lax.fori_loop(0, dst.shape[0] // step, some, 0)


class CtxPlace:
    def __init__(self):
        self.me = lax.axis_index("ctx")
        self.x = self.me // 2
        self.y = self.me % 2

    def at(self, k, y):
        return lax.rem(self.x + k + 4, 4) * 2 + y

    def x_peer(self, hop):
        return {"ctx": self.at(hop, self.y)}

    def y_peer(self):
        return {"ctx": self.at(0, 1 - self.y)}

    def near(self):
        return [self.x_peer(1), self.x_peer(-1), self.y_peer()]

    def all(self):
        return [{"ctx": lax.rem(self.me + d, 8)} for d in range(1, 8)]


class XRing:
    def __init__(self, place, s, loaded, bufs, sems):
        self.place, self.s, self.loaded = place, s, loaded
        self.via, self.near, self.joined, self.summed = bufs
        self.send, self.recv = sems
        self.copies = {}

    def go(self, i, src, dst, hop):
        copy = remote(src, dst, self.send.at[i], self.recv.at[i], self.place.x_peer(hop))
        copy.start()
        self.copies[i] = copy

    def start(self, k):
        if k == 2:
            self.go(0, self.loaded(2), self.via, self.s)
        elif k == -self.s:
            self.go(1, self.loaded(k), self.near, k)

    def join(self):
        self.copies[0].wait_recv()
        add_up(self.summed, [self.loaded(self.s), self.via])
        self.go(2, self.summed, self.joined, self.s)

    def total(self, dst):
        self.copies[1].wait_recv()
        self.copies[2].wait_recv()
        add_up(dst, [self.loaded(0), self.near, self.joined])

    def finish(self):
        for copy in self.copies.values():
            copy.wait_send()


def cut(array, dim, owner):
    length = array.shape[dim] // 8
    span = pl.ds(pl.multiple_of(owner * length, length), length)
    return array.at[span] if dim == 0 else array.at[:, span]


BLOCKS = (2, -1, 1, 0)


class XFirst:
    def __init__(self, place, array, dim, out, scratch):
        self.place, self.array, self.dim, self.out = place, array, dim, out
        (self.held, bufs, summed, self.swapped, self.lsem, sems, self.ssend, self.srecv) = scratch
        held = self.held
        self.rings = [
            XRing(
                place, way(y), lambda k, y=y: held.at[k % 4, y],
                [bufs.at[y, j] for j in range(3)] + [summed.at[y]],
                [sems.at[0, y], sems.at[1, y]],
            )
            for y in (0, 1)
        ]

    def start(self):
        self.loads = {}
        for k in BLOCKS:
            for y in (0, 1):
                copy = pltpu.make_async_copy(
                    cut(self.array, self.dim, self.place.at(k, y)), self.held.at[k % 4, y],
                    self.lsem.at[k % 4, y],
                )
                copy.start()
                self.loads[k, y] = copy

    def first(self):
        for k in BLOCKS:
            for y in (0, 1):
                self.loads[k, y].wait()
                self.rings[y].start(k)

    def join(self):
        for ring in self.rings:
            ring.join()

    def swap(self):
        for y in (0, 1):
            self.rings[y].total(self.swapped.at[1 + y])
        self.across = remote(
            self.swapped.at[1 + (1 - self.place.y)], self.swapped.at[0], self.ssend.at[0],
            self.srecv.at[0], self.place.y_peer(),
        )
        self.across.start()

    def total(self):
        self.across.wait_recv()
        add_up(self.out, [self.swapped.at[1 + self.place.y], self.swapped.at[0]])

    def finish(self):
        for ring in self.rings:
            ring.finish()
        self.across.wait_send()


class YFirst:
    def __init__(self, place, array, dim, out, scratch):
        self.place, self.array, self.dim, self.out = place, array, dim, out
        (self.held, bufs, summed, self.swapped, self.lsem, sems, self.ssend, self.srecv) = scratch
        swapped = self.swapped
        self.half = half = self.held.shape[1] // 2
        self.rings = [
            XRing(
                place, way(h), lambda k, h=h: swapped.at[k % 4, pl.ds(h * half, half)],
                [bufs.at[h, j] for j in range(3)] + [summed.at[h]],
                [sems.at[0, h], sems.at[1, h]],
            )
            for h in (0, 1)
        ]

    def start(self):
        self.swaps, self.loads = {}, {}
        for k in BLOCKS:
            copy = remote(
                cut(self.array, self.dim, self.place.at(k, 1 - self.place.y)),
                self.swapped.at[k % 4], self.ssend.at[k % 4], self.srecv.at[k % 4],
                self.place.y_peer(),
            )
            copy.start()
            self.swaps[k] = copy
        for k in BLOCKS:
            copy = pltpu.make_async_copy(
                cut(self.array, self.dim, self.place.at(k, self.place.y)),
                self.held.at[k % 4], self.lsem.at[k % 4],
            )
            copy.start()
            self.loads[k] = copy

    def first(self):
        for k in BLOCKS:
            self.loads[k].wait()
            self.swaps[k].wait_recv()
            block = self.swapped.at[k % 4]
            add_up(block, [block, self.held.at[k % 4]])
            for ring in self.rings:
                ring.start(k)

    def join(self):
        for ring in self.rings:
            ring.join()

    def total(self):
        for h, ring in enumerate(self.rings):
            ring.total(self.out.at[pl.ds(h * self.half, self.half)])

    def finish(self):
        for ring in self.rings:
            ring.finish()
        for copy in self.swaps.values():
            copy.wait_send()


def ctx_scratch(shapes, dims, modes):
    scratch = []
    for shape, dim, mode in zip(shapes, dims, modes):
        rows, width = owned(shape, dim)
        if mode == "x":
            held, ring = (4, 2, rows, width), (2, 3, rows, width)
        else:
            held, ring = (4, rows, width), (2, 3, rows // 2, width)
        scratch += [
            pltpu.VMEM(held, bf16),
            pltpu.VMEM(ring, bf16),
            pltpu.VMEM((2, *ring[2:]), bf16),
            pltpu.VMEM((3 if mode == "x" else 4, rows, width), bf16),
            pltpu.SemaphoreType.DMA((4, 2) if mode == "x" else (4,)),
            pltpu.SemaphoreType.DMA((2, 2, 3)),
            pltpu.SemaphoreType.DMA((4,)),
            pltpu.SemaphoreType.DMA((4,)),
        ]
    return scratch


def owned(shape, dim):
    return tuple(n // 8 if i == dim else n for i, n in enumerate(shape))


class CtxSums:
    def __init__(self, place, arrays, dims, modes, outs, scratch):
        sums = [
            (XFirst if mode == "x" else YFirst)(
                place, arrays[i], dims[i], outs[i], scratch[8 * i : 8 * i + 8]
            )
            for i, mode in enumerate(modes)
        ]
        self.xs = [one for one, mode in zip(sums, modes) if mode == "x"]
        self.ys = [one for one, mode in zip(sums, modes) if mode == "y"]

    def start(self):
        for one in self.xs + self.ys:
            one.start()

    def first(self):
        for one in self.xs:
            one.first()

    def middle(self):
        for one in self.ys[:-1]:
            one.first()
            one.join()
        for one in self.xs:
            one.join()
        for one in self.ys[-1:]:
            one.first()

    def later(self):
        for one in self.xs:
            one.swap()
        for one in self.ys[-1:]:
            one.join()

    def end(self):
        for one in self.ys[:-1] + self.xs + self.ys[-1:]:
            one.total()
        for one in self.xs + self.ys:
            one.finish()


def everyone(place):
    return [lax.rem(place.me + d, 8) for d in range(1, 8)]


class Lines:
    def __init__(self, place, line, slots, send, recv):
        self.line, self.slots = line, slots
        self.copies = [
            remote(line, slots.at[d], send.at[d], recv.at[d], {"wt": lax.rem(place.me + d, 8)})
            for d in range(1, 8)
        ]

    def start(self):
        for copy in self.copies:
            copy.start()

    def total(self):
        total = self.line[...]
        for d, copy in enumerate(self.copies, start=1):
            copy.wait_recv()
            total = total + self.slots[d]
        return total

    def finish(self):
        for copy in self.copies:
            copy.wait_send()


def backward_kernel(mode, chunks, dims, modes, part, line, above, own, factor, gain, *rest):
    count = len(dims)
    arrays, rest = rest[:count], rest[count:]
    if mode == "mid":
        share, piece, whole, *rest = rest
    elif mode == "pass":
        begin, share, whole, *rest = rest
    else:
        other, last_part, last_mid, share, result, gain_out, *rest = rest
    outs, rest = rest[:count], rest[count:]
    scratch, rest = rest[: 8 * count], rest[8 * count :]
    if mode == "mid":
        agsrc, *rest = rest
    elif mode == "pass":
        agsrc, arrived, xsend, xrecv, *rest = rest
    else:
        piece, pieces, gsend, grecv, gain_slots, osend, orecv, *rest = rest
        last_bufs, rest = rest[:7], rest[7:]
    slots, lsend, lrecv, *rest = rest
    bufs, sems = rest[:7], rest[7:]
    place, ctx = WtPlace(own.shape[1]), CtxPlace()
    section = lax.axis_index("section")
    greet(
        [{"wt": peer} for peer in everyone(place)]
        + ([{"section": 1 - section}] if mode == "pass" else [])
        + (ctx.all() if mode == "last" else ctx.near() if count else [])
    )
    rows = own.shape[0] // chunks
    depth = 8 * own.shape[1]
    spans = [pl.ds(q * rows, rows) for q in range(chunks)]
    sums = [Reduce(place, part, bufs, q, spans[q]) for q in range(chunks)]
    gathers = [Gather(place, whole, sems, q, spans[q]) for q in range(chunks)] if (
        mode != "last") else []
    lines = Lines(place, line, slots, lsend, lrecv)
    beside = CtxSums(ctx, arrays, dims, modes, outs, scratch) if count else None
    lines.start()
    for one in sums:
        one.start()
    if beside:
        beside.start()
    for one in sums:
        one.pass_on()
    if beside:
        beside.first()
    for one in sums:
        one.pass_more()
    mean = column(lines.total(), own.shape[0] // 128) * (1.0 / depth)
    swaps = []
    terms = jnp.zeros((1, own.shape[1]), f32)
    for q in range(chunks):
        span = spans[q]
        total = sums[q].total()
        scale = factor[span, :]
        normed = own[span, :] * scale
        if mode != "pass":
            terms = terms + jnp.sum(total * normed, axis=0, keepdims=True)
        grad = above[span, :].astype(f32) + scale * (
            total * gain[...] - normed * mean[q * rows : (q + 1) * rows]
        )
        if mode == "mid":
            share[span, :] = grad
            agsrc[span, :] = grad.astype(bf16)
            gathers[q].start(agsrc.at[span])
        elif mode == "pass":
            agsrc[span, :] = grad.astype(bf16)
            swap = swap_sections(agsrc.at[span], arrived.at[span], xsend.at[q], xrecv.at[q])
            swap.start()
            swaps.append(swap)
        else:
            share[span, :] = grad.astype(bf16)
    if mode == "mid":
        piece[...] = jnp.broadcast_to(terms, piece.shape)
    if mode == "pass":
        for q in range(chunks):
            span = spans[q]
            swaps[q].wait_recv()
            share[span, :] = jnp.where(
                section == 1, begin[span, :].astype(f32), arrived[span, :].astype(f32)
            ).astype(bf16)
            gathers[q].start(share.at[span])
    if mode == "last":
        piece[0:8, :] = jnp.broadcast_to(terms, (8, own.shape[1]))
        piece[8:16, :] = other[...]
        piece_copies = [
            remote(
                piece, pieces.at[place.me], gsend.at[d], grecv.at[d],
                {"wt": lax.rem(place.me + d, 8)},
            )
            for d in range(1, 8)
        ]
        for copy in piece_copies:
            copy.start()
        last_sums = [Reduce(place, last_part, last_bufs, q, spans[q]) for q in range(chunks)]
        for one in last_sums:
            one.start()
        for one in last_sums:
            one.pass_on()
        pieces[place.me] = piece[...]
        for copy in piece_copies:
            copy.wait()
        owner_copies = []
        for d in range(1, 8):
            owner = lax.rem(ctx.me + d, 8)
            copy = remote(
                pieces.at[owner], gain_slots.at[d], osend.at[d], orecv.at[d], {"ctx": owner}
            )
            copy.start()
            owner_copies.append(copy)
        for one in last_sums:
            one.pass_more()
        for q in range(chunks):
            span = spans[q]
            result[span, :] = (last_mid[span, :] + last_sums[q].total()).astype(bf16)
        sums = sums + last_sums
    for one in gathers:
        one.forward()
    for one in gathers:
        one.forward_more()
    if beside:
        beside.middle()
    for one in gathers:
        one.finish()
    for one in sums:
        one.finish()
    for one in swaps:
        one.wait_send()
    lines.finish()
    if beside:
        beside.later()
    if mode == "last":
        total = pieces[ctx.me]
        for d, copy in enumerate(owner_copies, start=1):
            copy.wait_recv()
            total = total + gain_slots[d]
        gain_out[...] = total
        for copy in owner_copies:
            copy.wait_send()
    if beside:
        beside.end()


def backward_sum(
    mode, part, line, above, own, factor, gain, arrays, dims, modes, extra, collective_id,
    chunks=4
):
    rows, width = own.shape
    vmem = pl.BlockSpec(memory_space=pltpu.VMEM)
    hbm = pl.BlockSpec(memory_space=pl.ANY)
    whole = jax.ShapeDtypeStruct((rows, 8 * width), bf16)
    one_sum = reduce_scratch(chunks, rows // chunks, width)
    seven = [pltpu.SemaphoreType.DMA((8,)), pltpu.SemaphoreType.DMA((8,))]
    if mode == "mid":
        out_shape = (
            jax.ShapeDtypeStruct((rows, width), f32),
            jax.ShapeDtypeStruct((8, width), f32),
            whole,
        )
        out_specs = (vmem, vmem, hbm)
        scratch = [pltpu.VMEM((rows, width), bf16)]
    elif mode == "pass":
        out_shape = (jax.ShapeDtypeStruct((rows, width), bf16), whole)
        out_specs = (vmem, hbm)
        scratch = [pltpu.VMEM((rows, width), bf16)] * 2 + [
            pltpu.SemaphoreType.DMA((chunks,)),
            pltpu.SemaphoreType.DMA((chunks,)),
        ]
    else:
        out_shape = (
            jax.ShapeDtypeStruct((rows, width), bf16),
            jax.ShapeDtypeStruct((rows, width), bf16),
            jax.ShapeDtypeStruct((16, width), f32),
        )
        out_specs = (vmem, vmem, vmem)
        scratch = [pltpu.VMEM((16, width), f32), pltpu.VMEM((8, 16, width), f32)]
        scratch += seven + [pltpu.VMEM((8, 16, width), f32)] + seven + one_sum
    scratch += [pltpu.VMEM((8, 8, 128), f32)] + seven + one_sum
    if mode != "last":
        scratch += gather_scratch(chunks)
    operands = [part, line, above, own, factor, gain] + arrays + extra
    shapes = [array.shape for array in arrays]
    return pl.pallas_call(
        functools.partial(backward_kernel, mode, chunks, dims, modes),
        out_shape=out_shape
        + tuple(jax.ShapeDtypeStruct(owned(*one), f32) for one in zip(shapes, dims)),
        in_specs=[vmem] * 6 + [hbm] * len(arrays) + [vmem] * len(extra),
        out_specs=out_specs + (vmem,) * len(arrays),
        scratch_shapes=ctx_scratch(shapes, dims, modes) + scratch,
        compiler_params=pltpu.CompilerParams(
            collective_id=collective_id, has_side_effects=True,
            vmem_limit_bytes=(56 if arrays else 32) * MiB,
        ),
        name="sum_back_" + mode,
    )(*operands)


def lanes(shape):
    return lax.broadcasted_iota(jnp.int32, shape, len(shape) - 1)


def turn(u, cosine, sine):
    low_half = jnp.bitwise_and(lanes(u.shape), HD - 1) < HD // 2
    turned = jnp.where(low_half, -pltpu.roll(u, 128 - HD // 2, 1), pltpu.roll(u, HD // 2, 1))
    return u * cosine + turned * sine


def turn_back(y, cosine, sine):
    low_half = jnp.bitwise_and(lanes(y.shape), HD - 1) < HD // 2
    z = y * sine
    turned = jnp.where(low_half, pltpu.roll(z, 128 - HD // 2, 1), -pltpu.roll(z, HD // 2, 1))
    return y * cosine + turned


def kv_gather_kernel(n, kv, cosine, sine, out, mine, send, recv, local):
    me = lax.axis_index("ctx")
    barrier = pltpu.get_barrier_semaphore()
    for d in range(1, n):

        @pl.when(me - d >= 0)
        def _():
            pl.semaphore_signal(
                barrier, inc=1, device_id={"ctx": me - d}, device_id_type=MESH
            )

    rows = kv.shape[0] // 2
    turned = turn(kv[...], cosine[...], sine[...]).astype(bf16)
    mine[0] = turned[:rows]
    mine[1] = turned[rows:]
    own = pltpu.make_async_copy(mine, out.at[me], local)
    own.start()

    @pl.when(me < n - 1)
    def _():
        pl.semaphore_wait(barrier, n - 1 - me)

    def copy(d):
        return remote(mine, out.at[me], send.at[d], recv.at[d], {"ctx": lax.rem(me + d, n)})

    for d in range(1, n):

        @pl.when(me + d < n)
        def _():
            copy(d).start()

    for d in range(1, n):

        @pl.when(me - d >= 0)
        def _():
            copy(d).wait_recv()

    for d in range(1, n):

        @pl.when(me + d < n)
        def _():
            copy(d).wait_send()

    own.wait()


def kv_gather(kv, cosine, sine, collective_id):
    n = 8
    rows = kv.shape[0] // 2
    return pl.pallas_call(
        functools.partial(kv_gather_kernel, n),
        out_shape=jax.ShapeDtypeStruct((n, 2, rows, 128), bf16),
        in_specs=[pl.BlockSpec(memory_space=pltpu.VMEM)] * 3,
        out_specs=pl.BlockSpec(memory_space=pl.ANY),
        scratch_shapes=[
            pltpu.VMEM((2, rows, 128), bf16),
            pltpu.SemaphoreType.DMA((n,)),
            pltpu.SemaphoreType.DMA((n,)),
            pltpu.SemaphoreType.DMA,
        ],
        compiler_params=pltpu.CompilerParams(
            collective_id=collective_id, has_side_effects=True, vmem_limit_bytes=32 * MiB
        ),
        name="gather_kv",
    )(kv, cosine, sine)


def kv_sum_kernel(n, terms, cosine, sine, out, slots, total, send, recv):
    me = lax.axis_index("ctx")
    barrier = pltpu.get_barrier_semaphore()
    for d in range(1, n):

        @pl.when(me + d < n)
        def _():
            pl.semaphore_signal(
                barrier, inc=1, device_id={"ctx": lax.rem(me + d, n)}, device_id_type=MESH
            )

    @pl.when(me > 0)
    def _():
        pl.semaphore_wait(barrier, me)

    def copy(d):
        back = lax.rem(me + n - d, n)
        return remote(terms.at[back], slots.at[d], send.at[d], recv.at[d], {"ctx": back})

    for d in range(1, n):

        @pl.when(me - d >= 0)
        def _():
            copy(d).start()

    total[...] = terms[me].astype(f32)
    for d in range(1, n):

        @pl.when(me + d < n)
        def _():
            copy(d).wait_recv()
            total[...] += slots[d].astype(f32)

    rows = terms.shape[2]
    for b in range(2):
        span = pl.ds(b * rows, rows)
        out[span, :] = turn_back(total[b], cosine[span, :], sine[span, :]).astype(bf16)
    for d in range(1, n):

        @pl.when(me - d >= 0)
        def _():
            copy(d).wait_send()


def kv_sum(terms, cosine, sine, collective_id):
    n, two, rows, width = terms.shape
    return pl.pallas_call(
        functools.partial(kv_sum_kernel, n),
        out_shape=jax.ShapeDtypeStruct((2 * rows, width), bf16),
        in_specs=[pl.BlockSpec(memory_space=pltpu.VMEM)] * 3,
        out_specs=pl.BlockSpec(memory_space=pltpu.VMEM),
        scratch_shapes=[
            pltpu.VMEM((n, 2, rows, width), bf16),
            pltpu.VMEM((2, rows, width), f32),
            pltpu.SemaphoreType.DMA((n,)),
            pltpu.SemaphoreType.DMA((n,)),
        ],
        compiler_params=pltpu.CompilerParams(
            collective_id=collective_id, has_side_effects=True, vmem_limit_bytes=32 * MiB
        ),
        name="sum_kv",
    )(terms, cosine, sine)


def visible_keys(bounds, b, key_block, me, rows, heads):
    row = lax.broadcasted_iota(jnp.int32, (1, heads * rows), 1)
    for head in range(1, heads):
        row = row - jnp.where(lanes((1, heads * rows)) >= head * rows, rows, 0)
    place = me * rows + row
    first, second = bounds[b, 0], bounds[b, 1]
    begin = jnp.where(place >= second, second, jnp.where(place >= first, first, 0))
    key = key_block * rows + lax.broadcasted_iota(jnp.int32, (rows, 1), 0)
    return (key <= place) & (key >= begin)


def stack_queries(flat, cosine, sine, b, rows, stacked):
    span = pl.ds(b * rows, rows)
    low = lanes((rows, 128)) < HD
    for pair in range(2):
        u = turn(flat[span, 128 * pair : 128 * pair + 128], cosine[span, :], sine[span, :])
        u = u.astype(bf16).astype(f32) * (HD**-0.5)
        even = jnp.where(low, u, 0.0)
        odd = jnp.where(low, pltpu.roll(u, HD, 1), 0.0)
        stacked[b, pl.ds(2 * pair * rows, rows), :] = even.astype(bf16)
        stacked[b, pl.ds((2 * pair + 1) * rows, rows), :] = odd.astype(bf16)


def attention_kernel(bounds, flat, cosine, sine, kv, mix, logs, mixed, stacked, acc):
    me = lax.axis_index("ctx")
    rows = kv.shape[2]
    heads = 4
    for b in range(2):
        stack_queries(flat, cosine, sine, b, rows, stacked)
    acc[...] = jnp.zeros_like(acc)

    def block(j, carry):
        after = []
        for b in range(2):
            peak, total = carry[2 * b : 2 * b + 2]
            keys = kv[j, b]
            scores = times_transposed(keys, stacked[b])
            scores = jnp.where(visible_keys(bounds, b, j, me, rows, heads), scores, neg_big)
            new_peak = jnp.maximum(peak, jnp.max(scores, axis=0, keepdims=True))
            shrink = jnp.exp(peak - new_peak)
            weight = jnp.exp(scores - new_peak)
            total = total * shrink + jnp.sum(weight, axis=0, keepdims=True)
            acc[b] = acc[b] * shrink + contract_rows(keys, weight.astype(bf16))
            after += [new_peak, total]
        return tuple(after)

    zero = jnp.zeros((1, heads * rows), f32)
    done = lax.fori_loop(0, me + 1, block, (zero + neg_big, zero) * 2)
    low = lanes((rows, 128)) < HD
    for b in range(2):
        peak, total = done[2 * b : 2 * b + 2]
        out = acc[b] / total
        mixed[b] = out
        logs[b] = peak + jnp.log(total)
        upright = out.T
        for pair in range(2):
            even = upright[2 * pair * rows : (2 * pair + 1) * rows]
            odd = upright[(2 * pair + 1) * rows : (2 * pair + 2) * rows]
            both = jnp.where(low, pltpu.roll(even, HD, 1), odd)
            mix[pl.ds(b * rows, rows), 128 * pair : 128 * pair + 128] = both.astype(bf16)


def attention(bounds, flat, cosine, sine, kv):
    rows = kv.shape[2]
    vmem = pl.BlockSpec(memory_space=pltpu.VMEM)
    return pl.pallas_call(
        attention_kernel,
        out_shape=(
            jax.ShapeDtypeStruct((2 * rows, 256), bf16),
            jax.ShapeDtypeStruct((2, 1, 4 * rows), f32),
            jax.ShapeDtypeStruct((2, 128, 4 * rows), f32),
        ),
        in_specs=[pl.BlockSpec(memory_space=pltpu.SMEM)] + [vmem] * 4,
        out_specs=(vmem, vmem, vmem),
        scratch_shapes=[
            pltpu.VMEM((2, 4 * rows, 128), bf16),
            pltpu.VMEM((2, 128, 4 * rows), f32),
        ],
        compiler_params=pltpu.CompilerParams(vmem_limit_bytes=40 * MiB),
        name="attention",
    )(bounds, flat, cosine, sine, kv)


def attention_back_kernel(
    bounds, flat, cosine, sine, kv, logs, mixed, grad, out, terms, stacked, grads, acc
):
    me = lax.axis_index("ctx")
    rows = kv.shape[2]
    heads = 4
    low = lanes((rows, 128)) < HD
    deltas = []
    for b in range(2):
        stack_queries(flat, cosine, sine, b, rows, stacked)
        for pair in range(2):
            u = grad[pl.ds(b * rows, rows), 128 * pair : 128 * pair + 128].astype(f32)
            even = jnp.where(low, 0.0, pltpu.roll(u, HD, 1))
            odd = jnp.where(low, 0.0, u)
            grads[b, pl.ds(2 * pair * rows, rows), :] = even.astype(bf16)
            grads[b, pl.ds((2 * pair + 1) * rows, rows), :] = odd.astype(bf16)
        deltas.append(
            jnp.sum(mixed[b] * grads[b].astype(f32).T, axis=0, keepdims=True)
        )
    acc[...] = jnp.zeros_like(acc)

    def block(j, carry):
        for b in range(2):
            keys = kv[j, b]
            scores = times_transposed(keys, stacked[b])
            probs = jnp.where(
                visible_keys(bounds, b, j, me, rows, heads), jnp.exp(scores - logs[b]), 0.0
            )
            grad_probs = times_transposed(keys, grads[b])
            grad_scores = (probs * (grad_probs - deltas[b])).astype(bf16)
            acc[b] += contract_rows(keys, grad_scores)
            terms[j, b] = (
                jnp.dot(grad_scores, stacked[b], preferred_element_type=f32)
                + jnp.dot(probs.astype(bf16), grads[b], preferred_element_type=f32)
            ).astype(bf16)
        return carry

    lax.fori_loop(0, me + 1, block, 0)
    for b in range(2):
        span = pl.ds(b * rows, rows)
        upright = acc[b].T * (HD**-0.5)
        for pair in range(2):
            even = upright[2 * pair * rows : (2 * pair + 1) * rows]
            odd = upright[(2 * pair + 1) * rows : (2 * pair + 2) * rows]
            both = jnp.where(low, even, pltpu.roll(odd, HD, 1))
            out[span, 128 * pair : 128 * pair + 128] = turn_back(
                both, cosine[span, :], sine[span, :]
            ).astype(bf16)


def attention_back(bounds, flat, cosine, sine, kv, logs, mixed, grad):
    rows = kv.shape[2]
    vmem = pl.BlockSpec(memory_space=pltpu.VMEM)
    return pl.pallas_call(
        attention_back_kernel,
        out_shape=(
            jax.ShapeDtypeStruct((2 * rows, 256), bf16),
            jax.ShapeDtypeStruct(kv.shape, bf16),
        ),
        in_specs=[pl.BlockSpec(memory_space=pltpu.SMEM)] + [vmem] * 7,
        out_specs=(vmem, vmem),
        scratch_shapes=[
            pltpu.VMEM((2, 4 * rows, 128), bf16),
            pltpu.VMEM((2, 4 * rows, 128), bf16),
            pltpu.VMEM((2, 128, 4 * rows), f32),
        ],
        compiler_params=pltpu.CompilerParams(vmem_limit_bytes=40 * MiB),
        name="attention_back",
    )(bounds, flat, cosine, sine, kv, logs, mixed, grad)


def per_device(
    inputs,
    cotangent,
    doc_bounds,
    attn_gain,
    w_query,
    w_key,
    w_value,
    w_out,
    mlp_gain,
    w_gate,
    w_up,
    w_down,
):
    ctx_rank = lax.axis_index("ctx")
    wt_rank = lax.axis_index("wt")
    micro_count, block_rows, share_width = inputs.shape
    rows = micro_count * block_rows
    gain_attn = attn_gain.astype(f32)
    gain_mlp = mlp_gain.astype(f32)
    own_gain_attn = lax.dynamic_slice_in_dim(gain_attn, wt_rank * share_width, share_width, 1)
    own_gain_mlp = lax.dynamic_slice_in_dim(gain_mlp, wt_rank * share_width, share_width, 1)
    w_qkv = jnp.concatenate([w_query[0], w_key[0], w_value[0]], axis=1)
    w_o, w_g, w_u, w_d = w_out[0], w_gate[0], w_up[0], w_down[0]
    begin = inputs.reshape(rows, share_width)
    cot = cotangent.reshape(rows, share_width)

    places = ctx_rank * block_rows + jnp.arange(block_rows, dtype=jnp.int32)
    offsets = jnp.concatenate(
        [places - doc_begins(doc_bounds[b], places) for b in range(micro_count)]
    )
    angles = offsets.astype(f32)[:, None] * rope_freqs(HD)[None, :]
    cos_half, sin_half = jnp.cos(angles), jnp.sin(angles)
    cosine = jnp.concatenate([cos_half] * 4, axis=1)
    sine = jnp.concatenate([sin_half] * 4, axis=1)
    key_lane = jnp.arange(128)[None, :] < HD
    kv_cosine = jnp.where(key_lane, cosine, 1.0)
    kv_sine = jnp.where(key_lane, sine, 0.0)

    def forward(whole, share, tick):
        hidden = whole.astype(f32)
        factor = lax.rsqrt(jnp.mean(hidden * hidden, axis=-1, keepdims=True) + eps)
        attn_in = (hidden * factor * gain_attn).astype(bf16)
        pre = jnp.dot(attn_in, w_qkv, preferred_element_type=f32)
        q_pre, kv_pre = pre[:, :256], pre[:, 256:]
        kv = kv_gather(kv_pre, kv_cosine, kv_sine, 1)
        mix, logs, mixed = attention(doc_bounds, q_pre, cosine, sine, kv)
        part = jnp.dot(mix, w_o, preferred_element_type=f32).astype(bf16)
        mid, mid_whole = forward_mid(part, share, 2)
        mid_wide = mid_whole.astype(f32)
        mid_factor = lax.rsqrt(jnp.mean(mid_wide * mid_wide, axis=-1, keepdims=True) + eps)
        mlp_in = (mid_wide * mid_factor * gain_mlp).astype(bf16)
        gate = jnp.dot(mlp_in, w_g, preferred_element_type=f32)
        up = jnp.dot(mlp_in, w_u, preferred_element_type=f32)
        inner = lax.optimization_barrier((jax.nn.silu(gate) * up).astype(bf16))
        part = jnp.dot(inner, w_d, preferred_element_type=f32).astype(bf16)
        saved = dict(
            whole=whole, share=share, factor=factor, attn_in=attn_in, q_pre=q_pre, kv=kv,
            mix=mix, logs=logs, mixed=mixed, mid=mid, mid_whole=mid_whole,
            mid_factor=mid_factor, mlp_in=mlp_in, gate=gate, up=up, inner=inner,
        )
        return part, saved

    def line_of(part, whole, factor, gain):
        dots = jnp.sum(part * (whole.astype(f32) * factor * gain), axis=1)
        return jnp.concatenate(
            [dots.reshape(rows // 128, 128), jnp.zeros((8 - rows // 128, 128), f32)]
        )

    def backward(grad, grad_share, saved, last):
        gate, up = saved["gate"], saved["up"]
        grad_inner = times_transposed(grad, w_d)
        sigmoid = jax.nn.sigmoid(gate)
        grad_gate = (grad_inner * up * sigmoid * (1.0 + gate * (1.0 - sigmoid))).astype(bf16)
        grad_up = (grad_inner * gate * sigmoid).astype(bf16)
        part = times_transposed(grad_gate, w_g) + times_transposed(grad_up, w_u)
        line = line_of(part, saved["mid_whole"], saved["mid_factor"], gain_mlp)
        arrays = []
        if last:
            half = saved["inner"].shape[1] // 2
            arrays = [
                contract_rows(saved["inner"][:, :half], grad).astype(bf16),
                contract_rows(saved["inner"][:, half:], grad).astype(bf16),
            ]
        grad_mid, piece, grad_attn, *down = backward_sum(
            "mid", part.astype(bf16), line, grad_share, saved["mid"], saved["mid_factor"],
            own_gain_mlp, arrays, (1, 1)[: len(arrays)], ("x", "y")[: len(arrays)], [],
            8 if last else 3,
        )
        grad_mix = times_transposed(grad_attn, w_o).astype(bf16)
        grad_query, terms = attention_back(
            doc_bounds, saved["q_pre"], cosine, sine, saved["kv"], saved["logs"],
            saved["mixed"], grad_mix,
        )
        grad_kv = kv_sum(terms, kv_cosine, kv_sine, 4)
        grad_pre = jnp.concatenate([grad_query, grad_kv], axis=1)
        part = times_transposed(grad_pre, w_qkv)
        line = line_of(part, saved["whole"], saved["factor"], gain_attn)
        operands = (
            part.astype(bf16), line, grad_mid, saved["share"].astype(f32), saved["factor"],
            own_gain_attn,
        )
        return operands, dict(
            grad_gate=grad_gate, grad_up=grad_up, grad_attn=grad_attn, grad_pre=grad_pre,
            piece=piece, down=down,
        )

    whole_cot = lax.all_gather(cot, "wt", axis=1, tiled=True)
    part, saved = forward(wt_gather(begin, 6), begin, 0)
    share, whole = forward_pass(part, saved["mid"], begin, 7)
    part, saved = forward(whole, share, 1)
    last_part = part

    operands, _ = backward(whole_cot, cot, saved, False)
    section = lax.axis_index("section")
    grad_share, grad = backward_sum("pass", *operands, [], (), (), [cot], 9)
    operands, kept = backward(grad, grad_share, saved, True)
    arrays = [
        contract_rows(saved["mlp_in"], kept["grad_up"]).astype(bf16),
        contract_rows(saved["attn_in"], kept["grad_pre"]).astype(bf16),
        contract_rows(saved["mix"], kept["grad_attn"]).astype(bf16),
        contract_rows(saved["mlp_in"], kept["grad_gate"]).astype(bf16),
    ]
    first_grad, result, gains, up, pre, out, gate = backward_sum(
        "last", *operands, arrays, (0, 0, 1, 0), ("x", "x", "y", "y"),
        [kept["piece"], last_part, saved["mid"]], 10,
    )
    down = jnp.concatenate(kept["down"], axis=0)
    boundary = jnp.where(section == 0, first_grad, result)
    return (
        boundary.reshape(1, micro_count, block_rows, share_width),
        gains[0][None],
        pre[:, :256][None],
        pre[:, 256:320][None],
        pre[:, 320:][None],
        out[None],
        gains[8][None],
        gate[None],
        up[None],
        down[None],
    )


def solution(mesh):
    return jax.shard_map(
        per_device,
        mesh=mesh,
        in_specs=(
            P(None, "ctx", "wt"),
            P(None, "ctx", "wt"),
            P(),
            P("section", None),
            P("section", None, "wt"),
            P("section", None, "wt"),
            P("section", None, "wt"),
            P("section", "wt", None),
            P("section", None),
            P("section", None, "wt"),
            P("section", None, "wt"),
            P("section", "wt", None),
        ),
        out_specs=(
            P("section", None, "ctx", "wt"),
            P("section", "ctx"),
            P("section", "ctx", "wt"),
            P("section", "ctx", "wt"),
            P("section", "ctx", "wt"),
            P("section", "wt", "ctx"),
            P("section", "ctx"),
            P("section", "ctx", "wt"),
            P("section", "ctx", "wt"),
            P("section", "wt", "ctx"),
        ),
        check_vma=False,
    )
```

```python
import functools

import jax
import jax.numpy as jnp
from jax import lax
from jax.experimental import pallas as pl
from jax.experimental.pallas import tpu as pltpu
from jax.sharding import PartitionSpec as P

HD = 64
eps = 1e-05
theta = 500000.0
neg_big = -1e30
MESH = pl.DeviceIdType.MESH
f32 = jnp.float32
bf16 = jnp.bfloat16
MiB = 1024 * 1024


def rope_freqs(head_width):
    index_steps = jnp.arange(head_width // 2, dtype=jnp.float32)
    inverse = theta ** (-2.0 * index_steps / head_width)
    wavelen = 2.0 * jnp.pi / inverse
    smooth = (8192.0 / wavelen - 1.0) / 3.0
    blended = (1.0 - smooth) * inverse / 32.0 + smooth * inverse
    return jnp.where(
        wavelen < 2048.0, inverse, jnp.where(wavelen > 8192.0, inverse / 32.0, blended)
    )


def doc_begins(bounds, places):
    starts = jnp.concatenate([jnp.zeros((1,), jnp.int32), bounds])
    started = places[:, None] >= starts[None, :]
    return jnp.max(jnp.where(started, starts[None, :], 0), axis=1)


def contract_rows(left, right):
    return lax.dot_general(
        left, right, (((0,), (0,)), ((), ())), preferred_element_type=jnp.float32
    )


def times_transposed(left, right):
    return lax.dot_general(
        left, right, (((1,), (1,)), ((), ())), preferred_element_type=jnp.float32
    )


def greet(peers):
    barrier = pltpu.get_barrier_semaphore()
    for peer in peers:
        pl.semaphore_signal(barrier, inc=1, device_id=peer, device_id_type=MESH)
    pl.semaphore_wait(barrier, len(peers))


def remote(src, dst, send, recv, peer):
    return pltpu.make_async_remote_copy(
        src_ref=src, dst_ref=dst, send_sem=send, recv_sem=recv, device_id=peer,
        device_id_type=MESH,
    )


class WtPlace:
    def __init__(self, width):
        self.me = lax.axis_index("wt")
        self.z = self.me // 2
        self.core = self.me % 2
        self.sib = self.me + 1 - 2 * self.core
        self.width = width

    def peer(self, k):
        return lax.rem(self.z + k + 4, 4) * 2 + self.core

    def cols(self, index):
        return pl.ds(pl.multiple_of(index * self.width, self.width), self.width)


def way(chunk):
    return 1 if chunk % 2 == 0 else -1


class Gather:
    def __init__(self, place, out, sems, chunk, rows):
        self.place, self.out, self.chunk, self.rows = place, out, chunk, rows
        self.send, self.recv, self.fsend, self.frecv, self.local = sems
        self.s = way(chunk)

    def piece(self, index):
        return self.out.at[self.rows, self.place.cols(index)]

    def aside(self, k):
        p, q = self.place, self.chunk
        got = self.piece(p.peer(-k))
        return remote(got, got, self.fsend.at[q, k % 4], self.frecv.at[q, k % 4], {"wt": p.sib})

    def start(self, src):
        p, q = self.place, self.chunk
        mine = self.piece(p.me)
        self.own = pltpu.make_async_copy(src, mine, self.local.at[q])
        self.sent = []
        for hop in (self.s, -self.s):
            k = hop % 4
            copy = remote(
                src, mine, self.send.at[q, k], self.recv.at[q, k], {"wt": p.peer(hop)}
            )
            copy.start()
            self.sent.append(copy)
        copy = remote(src, mine, self.fsend.at[q, 0], self.frecv.at[q, 0], {"wt": p.sib})
        copy.start()
        self.sent.append(copy)
        self.own.start()

    def forward(self):
        p, q, s = self.place, self.chunk, self.s
        self.passed = []
        self.sent[0].wait_recv()
        got = self.piece(p.peer(-s))
        copy = remote(got, got, self.send.at[q, 2], self.recv.at[q, 2], {"wt": p.peer(s)})
        copy.start()
        self.sent.append(copy)
        near = self.aside(s)
        near.start()
        self.passed.append(near)

    def forward_more(self):
        s = self.s
        self.sent[1].wait_recv()
        near = self.aside(-s)
        near.start()
        self.passed.append(near)
        self.sent[3].wait_recv()
        near = self.aside(2)
        near.start()
        self.passed.append(near)

    def finish(self):
        for copy in self.passed:
            copy.wait()
        self.sent[2].wait_recv()
        for copy in self.sent:
            copy.wait_send()
        self.own.wait()


def gather_all(gathers):
    for one in gathers:
        one.forward()
    for one in gathers:
        one.forward_more()
    for one in gathers:
        one.finish()


def gather_scratch(chunks):
    return [pltpu.SemaphoreType.DMA((chunks, 4)) for _ in range(4)] + [
        pltpu.SemaphoreType.DMA((chunks,))
    ]


def greet_wt(place, more=()):
    greet([{"wt": place.sib}] + [{"wt": place.peer(k)} for k in (1, -1)] + list(more))


def gather_kernel(chunks, x, out, *sems):
    place = WtPlace(x.shape[1])
    greet_wt(place)
    rows = x.shape[0] // chunks
    parts = []
    for q in range(chunks):
        chunk_rows = pl.ds(q * rows, rows)
        part = Gather(place, out, sems, q, chunk_rows)
        part.start(x.at[chunk_rows])
        parts.append(part)
    gather_all(parts)


def wt_gather(x, collective_id, chunks=4):
    rows, width = x.shape
    return pl.pallas_call(
        functools.partial(gather_kernel, chunks),
        out_shape=jax.ShapeDtypeStruct((rows, 8 * width), x.dtype),
        in_specs=[pl.BlockSpec(memory_space=pltpu.VMEM)],
        out_specs=pl.BlockSpec(memory_space=pl.ANY),
        scratch_shapes=gather_scratch(chunks),
        compiler_params=pltpu.CompilerParams(
            collective_id=collective_id, has_side_effects=True, vmem_limit_bytes=32 * MiB
        ),
        name="gather_wt",
    )(x)


class Reduce:
    def __init__(self, place, part, bufs, chunk, rows):
        self.place, self.part, self.chunk, self.rows = place, part, chunk, rows
        (self.pair, self.out, self.landed, self.s1, self.r1, self.s2, self.r2) = bufs
        self.s = way(chunk)

    def start(self):
        p, q, s = self.place, self.chunk, self.s
        self.first = {}
        for k in (2, -s, s, 0):
            target = lax.rem(p.z + k + 4, 4) * 2 + 1 - p.core
            copy = remote(
                self.part.at[self.rows, p.cols(target)], self.pair.at[q, k % 4],
                self.s1.at[q, k % 4], self.r1.at[q, k % 4], {"wt": p.sib},
            )
            copy.start()
            self.first[k] = copy

    def both(self, k):
        p, q = self.place, self.chunk
        self.first[k].wait_recv()
        own = self.part[self.rows, p.cols(p.peer(k))]
        return own.astype(f32) + self.pair[q, k % 4].astype(f32)

    def onward(self, k, value, hop):
        p, q = self.place, self.chunk
        self.out[q, k % 4] = value.astype(bf16)
        copy = remote(
            self.out.at[q, k % 4], self.landed.at[q, k % 4], self.s2.at[q, k % 4],
            self.r2.at[q, k % 4], {"wt": p.peer(hop)},
        )
        copy.start()
        self.second[k] = copy

    def pass_on(self):
        self.second = {}
        self.onward(2, self.both(2), self.s)
        self.onward(-self.s, self.both(-self.s), -self.s)

    def pass_more(self):
        q, s = self.chunk, self.s
        value = self.both(s)
        self.second[2].wait_recv()
        self.onward(s, value + self.landed[q, 2].astype(f32), s)

    def total(self):
        q = self.chunk
        total = self.both(0)
        for k in (-self.s, self.s):
            self.second[k].wait_recv()
            total = total + self.landed[q, k % 4].astype(f32)
        return total

    def finish(self):
        for copy in self.first.values():
            copy.wait_send()
        for copy in self.second.values():
            copy.wait_send()


def sum_in_turn(sums, use):
    for one in sums:
        one.start()
    for one in sums:
        one.pass_on()
    for one in sums:
        one.pass_more()
    for q in range(len(sums)):
        use(q)


def reduce_scratch(chunks, rows, width):
    return [pltpu.VMEM((chunks, 4, rows, width), bf16) for _ in range(3)] + [
        pltpu.SemaphoreType.DMA((chunks, 4)) for _ in range(4)
    ]


def column(line, blocks):
    eye = lax.broadcasted_iota(jnp.int32, (128, 128), 0) == lax.broadcasted_iota(
        jnp.int32, (128, 128), 1
    )
    parts = [
        jnp.sum(
            jnp.where(eye, jnp.broadcast_to(line[j : j + 1, :], (128, 128)), 0.0),
            axis=1, keepdims=True,
        )
        for j in range(blocks)
    ]
    return jnp.concatenate(parts, axis=0)


def swap_sections(src, dst, send, recv):
    return remote(src, dst, send, recv, {"section": 1 - lax.axis_index("section")})


def forward_mid_kernel(chunks, part, skip, mid, whole, agsrc, *scratch):
    bufs, sems = scratch[:7], scratch[7:]
    place = WtPlace(skip.shape[1])
    greet_wt(place)
    rows = skip.shape[0] // chunks
    spans = [pl.ds(q * rows, rows) for q in range(chunks)]
    sums = [Reduce(place, part, bufs, q, spans[q]) for q in range(chunks)]
    gathers = [Gather(place, whole, sems, q, spans[q]) for q in range(chunks)]

    def use(q):
        value = skip[spans[q], :].astype(f32) + sums[q].total()
        mid[spans[q], :] = value
        agsrc[spans[q], :] = value.astype(bf16)
        gathers[q].start(agsrc.at[spans[q]])

    sum_in_turn(sums, use)
    gather_all(gathers)
    for one in sums:
        one.finish()


def forward_mid(part, skip, collective_id, chunks=4):
    rows, width = skip.shape
    return pl.pallas_call(
        functools.partial(forward_mid_kernel, chunks),
        out_shape=(
            jax.ShapeDtypeStruct((rows, width), f32),
            jax.ShapeDtypeStruct((rows, 8 * width), bf16),
        ),
        in_specs=[pl.BlockSpec(memory_space=pltpu.VMEM)] * 2,
        out_specs=(
            pl.BlockSpec(memory_space=pltpu.VMEM),
            pl.BlockSpec(memory_space=pl.ANY),
        ),
        scratch_shapes=[pltpu.VMEM((rows, width), bf16)]
        + reduce_scratch(chunks, rows // chunks, width)
        + gather_scratch(chunks),
        compiler_params=pltpu.CompilerParams(
            collective_id=collective_id, has_side_effects=True, vmem_limit_bytes=32 * MiB
        ),
        name="sum_mid_gather",
    )(part, skip)


def forward_pass_kernel(
    chunks, part, mid, begin, share, whole, agsrc, arrived, xsend, xrecv, *scratch
):
    bufs, sems = scratch[:7], scratch[7:]
    place = WtPlace(mid.shape[1])
    section = lax.axis_index("section")
    greet_wt(place, [{"section": 1 - section}])
    rows = mid.shape[0] // chunks
    spans = [pl.ds(q * rows, rows) for q in range(chunks)]
    sums = [Reduce(place, part, bufs, q, spans[q]) for q in range(chunks)]
    gathers = [Gather(place, whole, sems, q, spans[q]) for q in range(chunks)]
    swaps = []

    def use(q):
        agsrc[spans[q], :] = (mid[spans[q], :] + sums[q].total()).astype(bf16)
        swap = swap_sections(
            agsrc.at[spans[q]], arrived.at[spans[q]], xsend.at[q], xrecv.at[q]
        )
        swap.start()
        swaps.append(swap)

    sum_in_turn(sums, use)
    for q in range(chunks):
        swaps[q].wait_recv()
        share[spans[q], :] = jnp.where(
            section == 0, begin[spans[q], :].astype(f32), arrived[spans[q], :].astype(f32)
        ).astype(bf16)
        gathers[q].start(share.at[spans[q]])
    gather_all(gathers)
    for one in sums:
        one.finish()
    for one in swaps:
        one.wait_send()


def forward_pass(part, mid, begin, collective_id, chunks=4):
    rows, width = mid.shape
    return pl.pallas_call(
        functools.partial(forward_pass_kernel, chunks),
        out_shape=(
            jax.ShapeDtypeStruct((rows, width), bf16),
            jax.ShapeDtypeStruct((rows, 8 * width), bf16),
        ),
        in_specs=[pl.BlockSpec(memory_space=pltpu.VMEM)] * 3,
        out_specs=(
            pl.BlockSpec(memory_space=pltpu.VMEM),
            pl.BlockSpec(memory_space=pl.ANY),
        ),
        scratch_shapes=[
            pltpu.VMEM((rows, width), bf16),
            pltpu.VMEM((rows, width), bf16),
            pltpu.SemaphoreType.DMA((chunks,)),
            pltpu.SemaphoreType.DMA((chunks,)),
        ]
        + reduce_scratch(chunks, rows // chunks, width)
        + gather_scratch(chunks),
        compiler_params=pltpu.CompilerParams(
            collective_id=collective_id, has_side_effects=True, vmem_limit_bytes=32 * MiB
        ),
        name="sum_pass_gather",
    )(part, mid, begin)


def add_up(dst, sources, step=64):
    def some(i, carry):
        span = pl.ds(pl.multiple_of(i * step, step), step)
        total = sources[0][span, :].astype(f32)
        for source in sources[1:]:
            total = total + source[span, :].astype(f32)
        dst[span, :] = total.astype(dst.dtype)
        return carry

    lax.fori_loop(0, dst.shape[0] // step, some, 0)


class CtxPlace:
    def __init__(self):
        self.me = lax.axis_index("ctx")
        self.x = self.me // 2
        self.y = self.me % 2

    def at(self, k, y):
        return lax.rem(self.x + k + 4, 4) * 2 + y

    def x_peer(self, hop):
        return {"ctx": self.at(hop, self.y)}

    def y_peer(self):
        return {"ctx": self.at(0, 1 - self.y)}

    def near(self):
        return [self.x_peer(1), self.x_peer(-1), self.y_peer()]

    def all(self):
        return [{"ctx": lax.rem(self.me + d, 8)} for d in range(1, 8)]


class XRing:
    def __init__(self, place, s, loaded, bufs, sems):
        self.place, self.s, self.loaded = place, s, loaded
        self.via, self.near, self.joined, self.summed = bufs
        self.send, self.recv = sems
        self.copies = {}

    def go(self, i, src, dst, hop):
        copy = remote(src, dst, self.send.at[i], self.recv.at[i], self.place.x_peer(hop))
        copy.start()
        self.copies[i] = copy

    def start(self, k):
        if k == 2:
            self.go(0, self.loaded(2), self.via, self.s)
        elif k == -self.s:
            self.go(1, self.loaded(k), self.near, k)

    def join(self):
        self.copies[0].wait_recv()
        add_up(self.summed, [self.loaded(self.s), self.via])
        self.go(2, self.summed, self.joined, self.s)

    def total(self, dst):
        self.copies[1].wait_recv()
        self.copies[2].wait_recv()
        add_up(dst, [self.loaded(0), self.near, self.joined])

    def finish(self):
        for copy in self.copies.values():
            copy.wait_send()


def cut(array, dim, owner):
    length = array.shape[dim] // 8
    span = pl.ds(pl.multiple_of(owner * length, length), length)
    return array.at[span] if dim == 0 else array.at[:, span]


BLOCKS = (2, -1, 1, 0)


class XFirst:
    def __init__(self, place, array, dim, out, scratch):
        self.place, self.array, self.dim, self.out = place, array, dim, out
        (self.held, bufs, summed, self.swapped, self.lsem, sems, self.ssend, self.srecv) = scratch
        held = self.held
        self.rings = [
            XRing(
                place, way(y), lambda k, y=y: held.at[k % 4, y],
                [bufs.at[y, j] for j in range(3)] + [summed.at[y]],
                [sems.at[0, y], sems.at[1, y]],
            )
            for y in (0, 1)
        ]

    def start(self):
        self.loads = {}
        for k in BLOCKS:
            for y in (0, 1):
                copy = pltpu.make_async_copy(
                    cut(self.array, self.dim, self.place.at(k, y)), self.held.at[k % 4, y],
                    self.lsem.at[k % 4, y],
                )
                copy.start()
                self.loads[k, y] = copy

    def first(self):
        for k in BLOCKS:
            for y in (0, 1):
                self.loads[k, y].wait()
                self.rings[y].start(k)

    def join(self):
        for ring in self.rings:
            ring.join()

    def swap(self):
        for y in (0, 1):
            self.rings[y].total(self.swapped.at[1 + y])
        self.across = remote(
            self.swapped.at[1 + (1 - self.place.y)], self.swapped.at[0], self.ssend.at[0],
            self.srecv.at[0], self.place.y_peer(),
        )
        self.across.start()

    def total(self):
        self.across.wait_recv()
        add_up(self.out, [self.swapped.at[1 + self.place.y], self.swapped.at[0]])

    def finish(self):
        for ring in self.rings:
            ring.finish()
        self.across.wait_send()


class YFirst:
    def __init__(self, place, array, dim, out, scratch):
        self.place, self.array, self.dim, self.out = place, array, dim, out
        (self.held, bufs, summed, self.swapped, self.lsem, sems, self.ssend, self.srecv) = scratch
        swapped = self.swapped
        self.half = half = self.held.shape[1] // 2
        self.rings = [
            XRing(
                place, way(h), lambda k, h=h: swapped.at[k % 4, pl.ds(h * half, half)],
                [bufs.at[h, j] for j in range(3)] + [summed.at[h]],
                [sems.at[0, h], sems.at[1, h]],
            )
            for h in (0, 1)
        ]

    def start(self):
        self.swaps, self.loads = {}, {}
        for k in BLOCKS:
            copy = remote(
                cut(self.array, self.dim, self.place.at(k, 1 - self.place.y)),
                self.swapped.at[k % 4], self.ssend.at[k % 4], self.srecv.at[k % 4],
                self.place.y_peer(),
            )
            copy.start()
            self.swaps[k] = copy
        for k in BLOCKS:
            copy = pltpu.make_async_copy(
                cut(self.array, self.dim, self.place.at(k, self.place.y)),
                self.held.at[k % 4], self.lsem.at[k % 4],
            )
            copy.start()
            self.loads[k] = copy

    def first(self):
        for k in BLOCKS:
            self.loads[k].wait()
            self.swaps[k].wait_recv()
            block = self.swapped.at[k % 4]
            add_up(block, [block, self.held.at[k % 4]])
            for ring in self.rings:
                ring.start(k)

    def join(self):
        for ring in self.rings:
            ring.join()

    def total(self):
        for h, ring in enumerate(self.rings):
            ring.total(self.out.at[pl.ds(h * self.half, self.half)])

    def finish(self):
        for ring in self.rings:
            ring.finish()
        for copy in self.swaps.values():
            copy.wait_send()


def ctx_scratch(shapes, dims, modes):
    scratch = []
    for shape, dim, mode in zip(shapes, dims, modes):
        rows, width = owned(shape, dim)
        if mode == "x":
            held, ring = (4, 2, rows, width), (2, 3, rows, width)
        else:
            held, ring = (4, rows, width), (2, 3, rows // 2, width)
        scratch += [
            pltpu.VMEM(held, bf16),
            pltpu.VMEM(ring, bf16),
            pltpu.VMEM((2, *ring[2:]), bf16),
            pltpu.VMEM((3 if mode == "x" else 4, rows, width), bf16),
            pltpu.SemaphoreType.DMA((4, 2) if mode == "x" else (4,)),
            pltpu.SemaphoreType.DMA((2, 2, 3)),
            pltpu.SemaphoreType.DMA((4,)),
            pltpu.SemaphoreType.DMA((4,)),
        ]
    return scratch


def owned(shape, dim):
    return tuple(n // 8 if i == dim else n for i, n in enumerate(shape))


class CtxSums:
    def __init__(self, place, arrays, dims, modes, outs, scratch):
        sums = [
            (XFirst if mode == "x" else YFirst)(
                place, arrays[i], dims[i], outs[i], scratch[8 * i : 8 * i + 8]
            )
            for i, mode in enumerate(modes)
        ]
        self.xs = [one for one, mode in zip(sums, modes) if mode == "x"]
        self.ys = [one for one, mode in zip(sums, modes) if mode == "y"]

    def start(self):
        for one in self.xs + self.ys:
            one.start()

    def first(self):
        for one in self.xs:
            one.first()

    def middle(self):
        for one in self.ys[:-1]:
            one.first()
            one.join()
        for one in self.xs:
            one.join()
        for one in self.ys[-1:]:
            one.first()

    def later(self):
        for one in self.xs:
            one.swap()
        for one in self.ys[-1:]:
            one.join()

    def end(self):
        for one in self.ys[:-1] + self.xs + self.ys[-1:]:
            one.total()
        for one in self.xs + self.ys:
            one.finish()


def everyone(place):
    return [lax.rem(place.me + d, 8) for d in range(1, 8)]


class Lines:
    def __init__(self, place, line, slots, send, recv):
        self.line, self.slots = line, slots
        self.copies = [
            remote(line, slots.at[d], send.at[d], recv.at[d], {"wt": lax.rem(place.me + d, 8)})
            for d in range(1, 8)
        ]

    def start(self):
        for copy in self.copies:
            copy.start()

    def total(self):
        total = self.line[...]
        for d, copy in enumerate(self.copies, start=1):
            copy.wait_recv()
            total = total + self.slots[d]
        return total

    def finish(self):
        for copy in self.copies:
            copy.wait_send()


def backward_kernel(mode, chunks, dims, modes, part, line, above, own, factor, gain, *rest):
    count = len(dims)
    arrays, rest = rest[:count], rest[count:]
    if mode == "mid":
        share, piece, whole, *rest = rest
    elif mode == "pass":
        begin, share, whole, *rest = rest
    else:
        other, last_part, last_mid, share, result, gain_out, *rest = rest
    outs, rest = rest[:count], rest[count:]
    scratch, rest = rest[: 8 * count], rest[8 * count :]
    if mode == "mid":
        agsrc, *rest = rest
    elif mode == "pass":
        agsrc, arrived, xsend, xrecv, *rest = rest
    else:
        piece, pieces, gsend, grecv, gain_slots, osend, orecv, *rest = rest
        last_bufs, rest = rest[:7], rest[7:]
    slots, lsend, lrecv, *rest = rest
    bufs, sems = rest[:7], rest[7:]
    place, ctx = WtPlace(own.shape[1]), CtxPlace()
    section = lax.axis_index("section")
    greet(
        [{"wt": peer} for peer in everyone(place)]
        + ([{"section": 1 - section}] if mode == "pass" else [])
        + (ctx.all() if mode == "last" else ctx.near() if count else [])
    )
    rows = own.shape[0] // chunks
    depth = 8 * own.shape[1]
    spans = [pl.ds(q * rows, rows) for q in range(chunks)]
    sums = [Reduce(place, part, bufs, q, spans[q]) for q in range(chunks)]
    gathers = [Gather(place, whole, sems, q, spans[q]) for q in range(chunks)] if (
        mode != "last") else []
    lines = Lines(place, line, slots, lsend, lrecv)
    beside = CtxSums(ctx, arrays, dims, modes, outs, scratch) if count else None
    lines.start()
    for one in sums:
        one.start()
    if beside:
        beside.start()
    for one in sums:
        one.pass_on()
    if beside:
        beside.first()
    for one in sums:
        one.pass_more()
    mean = column(lines.total(), own.shape[0] // 128) * (1.0 / depth)
    swaps = []
    terms = jnp.zeros((1, own.shape[1]), f32)
    for q in range(chunks):
        span = spans[q]
        total = sums[q].total()
        scale = factor[span, :]
        normed = own[span, :] * scale
        if mode != "pass":
            terms = terms + jnp.sum(total * normed, axis=0, keepdims=True)
        grad = above[span, :].astype(f32) + scale * (
            total * gain[...] - normed * mean[q * rows : (q + 1) * rows]
        )
        if mode == "mid":
            share[span, :] = grad
            agsrc[span, :] = grad.astype(bf16)
            gathers[q].start(agsrc.at[span])
        elif mode == "pass":
            agsrc[span, :] = grad.astype(bf16)
            swap = swap_sections(agsrc.at[span], arrived.at[span], xsend.at[q], xrecv.at[q])
            swap.start()
            swaps.append(swap)
        else:
            share[span, :] = grad.astype(bf16)
    if mode == "mid":
        piece[...] = jnp.broadcast_to(terms, piece.shape)
    if mode == "pass":
        for q in range(chunks):
            span = spans[q]
            swaps[q].wait_recv()
            share[span, :] = jnp.where(
                section == 1, begin[span, :].astype(f32), arrived[span, :].astype(f32)
            ).astype(bf16)
            gathers[q].start(share.at[span])
    if mode == "last":
        piece[0:8, :] = jnp.broadcast_to(terms, (8, own.shape[1]))
        piece[8:16, :] = other[...]
        piece_copies = [
            remote(
                piece, pieces.at[place.me], gsend.at[d], grecv.at[d],
                {"wt": lax.rem(place.me + d, 8)},
            )
            for d in range(1, 8)
        ]
        for copy in piece_copies:
            copy.start()
        last_sums = [Reduce(place, last_part, last_bufs, q, spans[q]) for q in range(chunks)]
        for one in last_sums:
            one.start()
        for one in last_sums:
            one.pass_on()
        pieces[place.me] = piece[...]
        for copy in piece_copies:
            copy.wait()
        owner_copies = []
        for d in range(1, 8):
            owner = lax.rem(ctx.me + d, 8)
            copy = remote(
                pieces.at[owner], gain_slots.at[d], osend.at[d], orecv.at[d], {"ctx": owner}
            )
            copy.start()
            owner_copies.append(copy)
        for one in last_sums:
            one.pass_more()
        for q in range(chunks):
            span = spans[q]
            result[span, :] = (last_mid[span, :] + last_sums[q].total()).astype(bf16)
        sums = sums + last_sums
    for one in gathers:
        one.forward()
    for one in gathers:
        one.forward_more()
    if beside:
        beside.middle()
    for one in gathers:
        one.finish()
    for one in sums:
        one.finish()
    for one in swaps:
        one.wait_send()
    lines.finish()
    if beside:
        beside.later()
    if mode == "last":
        total = pieces[ctx.me]
        for d, copy in enumerate(owner_copies, start=1):
            copy.wait_recv()
            total = total + gain_slots[d]
        gain_out[...] = total
        for copy in owner_copies:
            copy.wait_send()
    if beside:
        beside.end()


def backward_sum(
    mode, part, line, above, own, factor, gain, arrays, dims, modes, extra, collective_id,
    chunks=4
):
    rows, width = own.shape
    vmem = pl.BlockSpec(memory_space=pltpu.VMEM)
    hbm = pl.BlockSpec(memory_space=pl.ANY)
    whole = jax.ShapeDtypeStruct((rows, 8 * width), bf16)
    one_sum = reduce_scratch(chunks, rows // chunks, width)
    seven = [pltpu.SemaphoreType.DMA((8,)), pltpu.SemaphoreType.DMA((8,))]
    if mode == "mid":
        out_shape = (
            jax.ShapeDtypeStruct((rows, width), f32),
            jax.ShapeDtypeStruct((8, width), f32),
            whole,
        )
        out_specs = (vmem, vmem, hbm)
        scratch = [pltpu.VMEM((rows, width), bf16)]
    elif mode == "pass":
        out_shape = (jax.ShapeDtypeStruct((rows, width), bf16), whole)
        out_specs = (vmem, hbm)
        scratch = [pltpu.VMEM((rows, width), bf16)] * 2 + [
            pltpu.SemaphoreType.DMA((chunks,)),
            pltpu.SemaphoreType.DMA((chunks,)),
        ]
    else:
        out_shape = (
            jax.ShapeDtypeStruct((rows, width), bf16),
            jax.ShapeDtypeStruct((rows, width), bf16),
            jax.ShapeDtypeStruct((16, width), f32),
        )
        out_specs = (vmem, vmem, vmem)
        scratch = [pltpu.VMEM((16, width), f32), pltpu.VMEM((8, 16, width), f32)]
        scratch += seven + [pltpu.VMEM((8, 16, width), f32)] + seven + one_sum
    scratch += [pltpu.VMEM((8, 8, 128), f32)] + seven + one_sum
    if mode != "last":
        scratch += gather_scratch(chunks)
    operands = [part, line, above, own, factor, gain] + arrays + extra
    shapes = [array.shape for array in arrays]
    return pl.pallas_call(
        functools.partial(backward_kernel, mode, chunks, dims, modes),
        out_shape=out_shape
        + tuple(jax.ShapeDtypeStruct(owned(*one), f32) for one in zip(shapes, dims)),
        in_specs=[vmem] * 6 + [hbm] * len(arrays) + [vmem] * len(extra),
        out_specs=out_specs + (vmem,) * len(arrays),
        scratch_shapes=ctx_scratch(shapes, dims, modes) + scratch,
        compiler_params=pltpu.CompilerParams(
            collective_id=collective_id, has_side_effects=True,
            vmem_limit_bytes=(56 if arrays else 32) * MiB,
        ),
        name="sum_back_" + mode,
    )(*operands)


def lanes(shape):
    return lax.broadcasted_iota(jnp.int32, shape, len(shape) - 1)


def turn(u, cosine, sine):
    low_half = jnp.bitwise_and(lanes(u.shape), HD - 1) < HD // 2
    turned = jnp.where(low_half, -pltpu.roll(u, 128 - HD // 2, 1), pltpu.roll(u, HD // 2, 1))
    return u * cosine + turned * sine


def turn_back(y, cosine, sine):
    low_half = jnp.bitwise_and(lanes(y.shape), HD - 1) < HD // 2
    z = y * sine
    turned = jnp.where(low_half, pltpu.roll(z, 128 - HD // 2, 1), -pltpu.roll(z, HD // 2, 1))
    return y * cosine + turned


def visible_keys(bounds, b, key_block, me, rows, heads):
    row = lax.broadcasted_iota(jnp.int32, (1, heads * rows), 1)
    for head in range(1, heads):
        row = row - jnp.where(lanes((1, heads * rows)) >= head * rows, rows, 0)
    place = me * rows + row
    first, second = bounds[b, 0], bounds[b, 1]
    begin = jnp.where(place >= second, second, jnp.where(place >= first, first, 0))
    key = key_block * rows + lax.broadcasted_iota(jnp.int32, (rows, 1), 0)
    return (key <= place) & (key >= begin)


def stack_queries(flat, cosine, sine, b, rows, stacked):
    span = pl.ds(b * rows, rows)
    low = lanes((rows, 128)) < HD
    for pair in range(2):
        u = turn(flat[span, 128 * pair : 128 * pair + 128], cosine[span, :], sine[span, :])
        u = u.astype(bf16).astype(f32) * (HD**-0.5)
        even = jnp.where(low, u, 0.0)
        odd = jnp.where(low, pltpu.roll(u, HD, 1), 0.0)
        stacked[b, pl.ds(2 * pair * rows, rows), :] = even.astype(bf16)
        stacked[b, pl.ds((2 * pair + 1) * rows, rows), :] = odd.astype(bf16)


def later(me, d, n):
    return me + d < n


def earlier(me, d, n):
    return me - d >= 0


def greet_order(me, n, side, count):
    barrier = pltpu.get_barrier_semaphore()
    step = 1 if side is later else n - 1
    for d in range(1, n):

        @pl.when(side(me, d, n))
        def _():
            pl.semaphore_signal(
                barrier, inc=1, device_id={"ctx": lax.rem(me + d * step, n)},
                device_id_type=MESH,
            )

    def wait():
        @pl.when(count > 0)
        def _():
            pl.semaphore_wait(barrier, count)

    return wait


def attention_kernel(
    n, bounds, flat, kv_pre, cosine, sine, kv_cosine, kv_sine, mix, logs, mixed, kv,
    stacked, acc, mine, send, recv
):
    me = lax.axis_index("ctx")
    rows = kv.shape[2]
    heads = 4
    wait = greet_order(me, n, earlier, n - 1 - me)
    for b in range(2):
        span = pl.ds(b * rows, rows)
        turned = turn(kv_pre[span, :], kv_cosine[span, :], kv_sine[span, :]).astype(bf16)
        mine[b] = turned
        kv[me, b] = turned
    wait()

    def copy(d):
        return remote(mine, kv.at[me], send.at[d], recv.at[d], {"ctx": lax.rem(me + d, n)})

    for d in reversed(range(1, n)):

        @pl.when(later(me, d, n))
        def _():
            copy(d).start()

    for b in range(2):
        stack_queries(flat, cosine, sine, b, rows, stacked)
    acc[...] = jnp.zeros_like(acc)

    def block(j, carry):
        after = []
        for b in range(2):
            peak, total = carry[2 * b : 2 * b + 2]
            keys = kv[j, b]
            scores = times_transposed(keys, stacked[b])
            scores = jnp.where(visible_keys(bounds, b, j, me, rows, heads), scores, neg_big)
            new_peak = jnp.maximum(peak, jnp.max(scores, axis=0, keepdims=True))
            shrink = jnp.exp(peak - new_peak)
            weight = jnp.exp(scores - new_peak)
            total = total * shrink + jnp.sum(weight, axis=0, keepdims=True)
            acc[b] = acc[b] * shrink + contract_rows(keys, weight.astype(bf16))
            after += [new_peak, total]
        return tuple(after)

    def arrived(d, carry):
        copy(d).wait_recv()
        return block(me - d, carry)

    zero = jnp.zeros((1, heads * rows), f32)
    done = block(me, (zero + neg_big, zero) * 2)
    done = lax.fori_loop(1, me + 1, arrived, done)
    low = lanes((rows, 128)) < HD
    for b in range(2):
        peak, total = done[2 * b : 2 * b + 2]
        out = acc[b] / total
        mixed[b] = out
        logs[b] = peak + jnp.log(total)
        upright = out.T
        for pair in range(2):
            even = upright[2 * pair * rows : (2 * pair + 1) * rows]
            odd = upright[(2 * pair + 1) * rows : (2 * pair + 2) * rows]
            both = jnp.where(low, pltpu.roll(even, HD, 1), odd)
            mix[pl.ds(b * rows, rows), 128 * pair : 128 * pair + 128] = both.astype(bf16)
    for d in range(1, n):

        @pl.when(later(me, d, n))
        def _():
            copy(d).wait_send()


def attention(bounds, flat, kv_pre, cosine, sine, kv_cosine, kv_sine, collective_id):
    n = 8
    rows = flat.shape[0] // 2
    vmem = pl.BlockSpec(memory_space=pltpu.VMEM)
    return pl.pallas_call(
        functools.partial(attention_kernel, n),
        out_shape=(
            jax.ShapeDtypeStruct((2 * rows, 256), bf16),
            jax.ShapeDtypeStruct((2, 1, 4 * rows), f32),
            jax.ShapeDtypeStruct((2, 128, 4 * rows), f32),
            jax.ShapeDtypeStruct((n, 2, rows, 128), bf16),
        ),
        in_specs=[pl.BlockSpec(memory_space=pltpu.SMEM)] + [vmem] * 6,
        out_specs=(vmem,) * 4,
        scratch_shapes=[
            pltpu.VMEM((2, 4 * rows, 128), bf16),
            pltpu.VMEM((2, 128, 4 * rows), f32),
            pltpu.VMEM((2, rows, 128), bf16),
            pltpu.SemaphoreType.DMA((n,)),
            pltpu.SemaphoreType.DMA((n,)),
        ],
        compiler_params=pltpu.CompilerParams(
            collective_id=collective_id, has_side_effects=True, vmem_limit_bytes=40 * MiB
        ),
        name="attention",
    )(bounds, flat, kv_pre, cosine, sine, kv_cosine, kv_sine)


def attention_back_kernel(
    n, bounds, flat, cosine, sine, kv_cosine, kv_sine, kv, logs, mixed, grad, out, grad_kv,
    terms, slots, total, stacked, grads, acc, send, recv
):
    me = lax.axis_index("ctx")
    rows = kv.shape[2]
    heads = 4
    low = lanes((rows, 128)) < HD
    wait = greet_order(me, n, later, me)
    deltas = []
    for b in range(2):
        stack_queries(flat, cosine, sine, b, rows, stacked)
        for pair in range(2):
            u = grad[pl.ds(b * rows, rows), 128 * pair : 128 * pair + 128].astype(f32)
            even = jnp.where(low, 0.0, pltpu.roll(u, HD, 1))
            odd = jnp.where(low, 0.0, u)
            grads[b, pl.ds(2 * pair * rows, rows), :] = even.astype(bf16)
            grads[b, pl.ds((2 * pair + 1) * rows, rows), :] = odd.astype(bf16)
        deltas.append(
            jnp.sum(mixed[b] * grads[b].astype(f32).T, axis=0, keepdims=True)
        )
    acc[...] = jnp.zeros_like(acc)
    wait()

    def block(j):
        for b in range(2):
            keys = kv[j, b]
            scores = times_transposed(keys, stacked[b])
            probs = jnp.where(
                visible_keys(bounds, b, j, me, rows, heads), jnp.exp(scores - logs[b]), 0.0
            )
            grad_probs = times_transposed(keys, grads[b])
            grad_scores = (probs * (grad_probs - deltas[b])).astype(bf16)
            acc[b] += contract_rows(keys, grad_scores)
            terms[j, b] = (
                jnp.dot(grad_scores, stacked[b], preferred_element_type=f32)
                + jnp.dot(probs.astype(bf16), grads[b], preferred_element_type=f32)
            ).astype(bf16)

    def copy(d):
        back = lax.rem(me + n - d, n)
        return remote(terms.at[back], slots.at[d], send.at[d], recv.at[d], {"ctx": back})

    def block_sent(j, carry):
        block(j)
        copy(me - j).start()
        return carry

    lax.fori_loop(0, me, block_sent, 0)
    block(me)
    for b in range(2):
        span = pl.ds(b * rows, rows)
        upright = acc[b].T * (HD**-0.5)
        for pair in range(2):
            even = upright[2 * pair * rows : (2 * pair + 1) * rows]
            odd = upright[(2 * pair + 1) * rows : (2 * pair + 2) * rows]
            both = jnp.where(low, even, pltpu.roll(odd, HD, 1))
            out[span, 128 * pair : 128 * pair + 128] = turn_back(
                both, cosine[span, :], sine[span, :]
            ).astype(bf16)
    for b in range(2):
        total[b] = terms[me, b].astype(f32)
    for d in range(1, n):

        @pl.when(later(me, d, n))
        def _():
            copy(d).wait_recv()
            total[...] += slots[d].astype(f32)

    for b in range(2):
        span = pl.ds(b * rows, rows)
        grad_kv[span, :] = turn_back(
            total[b], kv_cosine[span, :], kv_sine[span, :]
        ).astype(bf16)
    for d in range(1, n):

        @pl.when(earlier(me, d, n))
        def _():
            copy(d).wait_send()


def attention_back(
    bounds, flat, cosine, sine, kv_cosine, kv_sine, kv, logs, mixed, grad, collective_id
):
    n, two, rows, width = kv.shape
    vmem = pl.BlockSpec(memory_space=pltpu.VMEM)
    return pl.pallas_call(
        functools.partial(attention_back_kernel, n),
        out_shape=(
            jax.ShapeDtypeStruct((2 * rows, 256), bf16),
            jax.ShapeDtypeStruct((2 * rows, 128), bf16),
        ),
        in_specs=[pl.BlockSpec(memory_space=pltpu.SMEM)] + [vmem] * 9,
        out_specs=(vmem, vmem),
        scratch_shapes=[
            pltpu.VMEM(kv.shape, bf16),
            pltpu.VMEM(kv.shape, bf16),
            pltpu.VMEM((2, rows, width), f32),
            pltpu.VMEM((2, 4 * rows, 128), bf16),
            pltpu.VMEM((2, 4 * rows, 128), bf16),
            pltpu.VMEM((2, 128, 4 * rows), f32),
            pltpu.SemaphoreType.DMA((n,)),
            pltpu.SemaphoreType.DMA((n,)),
        ],
        compiler_params=pltpu.CompilerParams(
            collective_id=collective_id, has_side_effects=True, vmem_limit_bytes=40 * MiB
        ),
        name="attention_back",
    )(bounds, flat, cosine, sine, kv_cosine, kv_sine, kv, logs, mixed, grad)


def per_device(
    inputs,
    cotangent,
    doc_bounds,
    attn_gain,
    w_query,
    w_key,
    w_value,
    w_out,
    mlp_gain,
    w_gate,
    w_up,
    w_down,
):
    ctx_rank = lax.axis_index("ctx")
    wt_rank = lax.axis_index("wt")
    micro_count, block_rows, share_width = inputs.shape
    rows = micro_count * block_rows
    gain_attn = attn_gain.astype(f32)
    gain_mlp = mlp_gain.astype(f32)
    own_gain_attn = lax.dynamic_slice_in_dim(gain_attn, wt_rank * share_width, share_width, 1)
    own_gain_mlp = lax.dynamic_slice_in_dim(gain_mlp, wt_rank * share_width, share_width, 1)
    w_qkv = jnp.concatenate([w_query[0], w_key[0], w_value[0]], axis=1)
    w_o, w_g, w_u, w_d = w_out[0], w_gate[0], w_up[0], w_down[0]
    begin = inputs.reshape(rows, share_width)
    cot = cotangent.reshape(rows, share_width)

    places = ctx_rank * block_rows + jnp.arange(block_rows, dtype=jnp.int32)
    offsets = jnp.concatenate(
        [places - doc_begins(doc_bounds[b], places) for b in range(micro_count)]
    )
    angles = offsets.astype(f32)[:, None] * rope_freqs(HD)[None, :]
    cos_half, sin_half = jnp.cos(angles), jnp.sin(angles)
    cosine = jnp.concatenate([cos_half] * 4, axis=1)
    sine = jnp.concatenate([sin_half] * 4, axis=1)
    key_lane = jnp.arange(128)[None, :] < HD
    kv_cosine = jnp.where(key_lane, cosine, 1.0)
    kv_sine = jnp.where(key_lane, sine, 0.0)

    def forward(whole, share, tick):
        hidden = whole.astype(f32)
        factor = lax.rsqrt(jnp.mean(hidden * hidden, axis=-1, keepdims=True) + eps)
        attn_in = (hidden * factor * gain_attn).astype(bf16)
        pre = jnp.dot(attn_in, w_qkv, preferred_element_type=f32)
        q_pre, kv_pre = pre[:, :256], pre[:, 256:]
        mix, logs, mixed, kv = attention(
            doc_bounds, q_pre, kv_pre, cosine, sine, kv_cosine, kv_sine, 1
        )
        part = jnp.dot(mix, w_o, preferred_element_type=f32).astype(bf16)
        mid, mid_whole = forward_mid(part, share, 2)
        mid_wide = mid_whole.astype(f32)
        mid_factor = lax.rsqrt(jnp.mean(mid_wide * mid_wide, axis=-1, keepdims=True) + eps)
        mlp_in = (mid_wide * mid_factor * gain_mlp).astype(bf16)
        gate = jnp.dot(mlp_in, w_g, preferred_element_type=f32)
        up = jnp.dot(mlp_in, w_u, preferred_element_type=f32)
        inner = lax.optimization_barrier((jax.nn.silu(gate) * up).astype(bf16))
        part = jnp.dot(inner, w_d, preferred_element_type=f32).astype(bf16)
        saved = dict(
            whole=whole, share=share, factor=factor, attn_in=attn_in, q_pre=q_pre, kv=kv,
            mix=mix, logs=logs, mixed=mixed, mid=mid, mid_whole=mid_whole,
            mid_factor=mid_factor, mlp_in=mlp_in, gate=gate, up=up, inner=inner,
        )
        return part, saved

    def line_of(part, whole, factor, gain):
        dots = jnp.sum(part * (whole.astype(f32) * factor * gain), axis=1)
        return jnp.concatenate(
            [dots.reshape(rows // 128, 128), jnp.zeros((8 - rows // 128, 128), f32)]
        )

    def backward(grad, grad_share, saved, last):
        gate, up = saved["gate"], saved["up"]
        grad_inner = times_transposed(grad, w_d)
        sigmoid = jax.nn.sigmoid(gate)
        grad_gate = (grad_inner * up * sigmoid * (1.0 + gate * (1.0 - sigmoid))).astype(bf16)
        grad_up = (grad_inner * gate * sigmoid).astype(bf16)
        part = times_transposed(grad_gate, w_g) + times_transposed(grad_up, w_u)
        line = line_of(part, saved["mid_whole"], saved["mid_factor"], gain_mlp)
        arrays = []
        if last:
            half = saved["inner"].shape[1] // 2
            arrays = [
                contract_rows(saved["inner"][:, :half], grad).astype(bf16),
                contract_rows(saved["inner"][:, half:], grad).astype(bf16),
            ]
        grad_mid, piece, grad_attn, *down = backward_sum(
            "mid", part.astype(bf16), line, grad_share, saved["mid"], saved["mid_factor"],
            own_gain_mlp, arrays, (1, 1)[: len(arrays)], ("x", "y")[: len(arrays)], [],
            8 if last else 3,
        )
        grad_mix = times_transposed(grad_attn, w_o).astype(bf16)
        grad_query, grad_kv = attention_back(
            doc_bounds, saved["q_pre"], cosine, sine, kv_cosine, kv_sine, saved["kv"],
            saved["logs"], saved["mixed"], grad_mix, 4,
        )
        grad_pre = jnp.concatenate([grad_query, grad_kv], axis=1)
        part = times_transposed(grad_pre, w_qkv)
        line = line_of(part, saved["whole"], saved["factor"], gain_attn)
        operands = (
            part.astype(bf16), line, grad_mid, saved["share"].astype(f32), saved["factor"],
            own_gain_attn,
        )
        return operands, dict(
            grad_gate=grad_gate, grad_up=grad_up, grad_attn=grad_attn, grad_pre=grad_pre,
            piece=piece, down=down,
        )

    whole_cot = lax.all_gather(cot, "wt", axis=1, tiled=True)
    part, saved = forward(wt_gather(begin, 6), begin, 0)
    share, whole = forward_pass(part, saved["mid"], begin, 7)
    part, saved = forward(whole, share, 1)
    last_part = part

    operands, _ = backward(whole_cot, cot, saved, False)
    section = lax.axis_index("section")
    grad_share, grad = backward_sum("pass", *operands, [], (), (), [cot], 9)
    operands, kept = backward(grad, grad_share, saved, True)
    arrays = [
        contract_rows(saved["mlp_in"], kept["grad_up"]).astype(bf16),
        contract_rows(saved["attn_in"], kept["grad_pre"]).astype(bf16),
        contract_rows(saved["mix"], kept["grad_attn"]).astype(bf16),
        contract_rows(saved["mlp_in"], kept["grad_gate"]).astype(bf16),
    ]
    first_grad, result, gains, up, pre, out, gate = backward_sum(
        "last", *operands, arrays, (0, 0, 1, 0), ("x", "x", "y", "y"),
        [kept["piece"], last_part, saved["mid"]], 10,
    )
    down = jnp.concatenate(kept["down"], axis=0)
    boundary = jnp.where(section == 0, first_grad, result)
    return (
        boundary.reshape(1, micro_count, block_rows, share_width),
        gains[0][None],
        pre[:, :256][None],
        pre[:, 256:320][None],
        pre[:, 320:][None],
        out[None],
        gains[8][None],
        gate[None],
        up[None],
        down[None],
    )


def solution(mesh):
    return jax.shard_map(
        per_device,
        mesh=mesh,
        in_specs=(
            P(None, "ctx", "wt"),
            P(None, "ctx", "wt"),
            P(),
            P("section", None),
            P("section", None, "wt"),
            P("section", None, "wt"),
            P("section", None, "wt"),
            P("section", "wt", None),
            P("section", None),
            P("section", None, "wt"),
            P("section", None, "wt"),
            P("section", "wt", None),
        ),
        out_specs=(
            P("section", None, "ctx", "wt"),
            P("section", "ctx"),
            P("section", "ctx", "wt"),
            P("section", "ctx", "wt"),
            P("section", "ctx", "wt"),
            P("section", "wt", "ctx"),
            P("section", "ctx"),
            P("section", "ctx", "wt"),
            P("section", "ctx", "wt"),
            P("section", "wt", "ctx"),
        ),
        check_vma=False,
    )
```

```python
import functools

import jax
import jax.numpy as jnp
from jax import lax
from jax.experimental import pallas as pl
from jax.experimental.pallas import tpu as pltpu
from jax.sharding import PartitionSpec as P

HD = 64
eps = 1e-05
theta = 500000.0
neg_big = -1e30
MESH = pl.DeviceIdType.MESH
f32 = jnp.float32
bf16 = jnp.bfloat16
MiB = 1024 * 1024


def rope_freqs(head_width):
    index_steps = jnp.arange(head_width // 2, dtype=jnp.float32)
    inverse = theta ** (-2.0 * index_steps / head_width)
    wavelen = 2.0 * jnp.pi / inverse
    smooth = (8192.0 / wavelen - 1.0) / 3.0
    blended = (1.0 - smooth) * inverse / 32.0 + smooth * inverse
    return jnp.where(
        wavelen < 2048.0, inverse, jnp.where(wavelen > 8192.0, inverse / 32.0, blended)
    )


def doc_begins(bounds, places):
    starts = jnp.concatenate([jnp.zeros((1,), jnp.int32), bounds])
    started = places[:, None] >= starts[None, :]
    return jnp.max(jnp.where(started, starts[None, :], 0), axis=1)


def contract_rows(left, right):
    return lax.dot_general(
        left, right, (((0,), (0,)), ((), ())), preferred_element_type=jnp.float32
    )


def times_transposed(left, right):
    return lax.dot_general(
        left, right, (((1,), (1,)), ((), ())), preferred_element_type=jnp.float32
    )


def greet(peers):
    barrier = pltpu.get_barrier_semaphore()
    for peer in peers:
        pl.semaphore_signal(barrier, inc=1, device_id=peer, device_id_type=MESH)
    pl.semaphore_wait(barrier, len(peers))


def remote(src, dst, send, recv, peer):
    return pltpu.make_async_remote_copy(
        src_ref=src, dst_ref=dst, send_sem=send, recv_sem=recv, device_id=peer,
        device_id_type=MESH,
    )


class WtPlace:
    def __init__(self, width):
        self.me = lax.axis_index("wt")
        self.z = self.me // 2
        self.core = self.me % 2
        self.sib = self.me + 1 - 2 * self.core
        self.width = width

    def peer(self, k):
        return lax.rem(self.z + k + 4, 4) * 2 + self.core

    def cols(self, index):
        return pl.ds(pl.multiple_of(index * self.width, self.width), self.width)


def way(chunk):
    return 1 if chunk % 2 == 0 else -1


class Gather:
    def __init__(self, place, out, sems, chunk, rows):
        self.place, self.out, self.chunk, self.rows = place, out, chunk, rows
        self.send, self.recv, self.fsend, self.frecv, self.local = sems
        self.s = way(chunk)

    def piece(self, index):
        return self.out.at[self.rows, self.place.cols(index)]

    def aside(self, k):
        p, q = self.place, self.chunk
        got = self.piece(p.peer(-k))
        return remote(got, got, self.fsend.at[q, k % 4], self.frecv.at[q, k % 4], {"wt": p.sib})

    def start(self, src):
        p, q = self.place, self.chunk
        mine = self.piece(p.me)
        self.own = pltpu.make_async_copy(src, mine, self.local.at[q])
        self.sent = []
        for hop in (self.s, -self.s):
            k = hop % 4
            copy = remote(
                src, mine, self.send.at[q, k], self.recv.at[q, k], {"wt": p.peer(hop)}
            )
            copy.start()
            self.sent.append(copy)
        copy = remote(src, mine, self.fsend.at[q, 0], self.frecv.at[q, 0], {"wt": p.sib})
        copy.start()
        self.sent.append(copy)
        self.own.start()

    def forward(self):
        p, q, s = self.place, self.chunk, self.s
        self.passed = []
        self.sent[0].wait_recv()
        got = self.piece(p.peer(-s))
        copy = remote(got, got, self.send.at[q, 2], self.recv.at[q, 2], {"wt": p.peer(s)})
        copy.start()
        self.sent.append(copy)
        near = self.aside(s)
        near.start()
        self.passed.append(near)

    def forward_more(self):
        s = self.s
        self.sent[1].wait_recv()
        near = self.aside(-s)
        near.start()
        self.passed.append(near)
        self.sent[3].wait_recv()
        near = self.aside(2)
        near.start()
        self.passed.append(near)

    def finish(self):
        for copy in self.passed:
            copy.wait()
        self.sent[2].wait_recv()
        for copy in self.sent:
            copy.wait_send()
        self.own.wait()


def gather_all(gathers):
    for one in gathers:
        one.forward()
    for one in gathers:
        one.forward_more()
    for one in gathers:
        one.finish()


def gather_scratch(chunks):
    return [pltpu.SemaphoreType.DMA((chunks, 4)) for _ in range(4)] + [
        pltpu.SemaphoreType.DMA((chunks,))
    ]


def greet_wt(place, more=()):
    greet([{"wt": place.sib}] + [{"wt": place.peer(k)} for k in (1, -1)] + list(more))


def gather_kernel(chunks, x, out, *sems):
    place = WtPlace(x.shape[1])
    greet_wt(place)
    rows = x.shape[0] // chunks
    parts = []
    for q in range(chunks):
        chunk_rows = pl.ds(q * rows, rows)
        part = Gather(place, out, sems, q, chunk_rows)
        part.start(x.at[chunk_rows])
        parts.append(part)
    gather_all(parts)


def wt_gather(x, collective_id, chunks=4):
    rows, width = x.shape
    return pl.pallas_call(
        functools.partial(gather_kernel, chunks),
        out_shape=jax.ShapeDtypeStruct((rows, 8 * width), x.dtype),
        in_specs=[pl.BlockSpec(memory_space=pltpu.VMEM)],
        out_specs=pl.BlockSpec(memory_space=pl.ANY),
        scratch_shapes=gather_scratch(chunks),
        compiler_params=pltpu.CompilerParams(
            collective_id=collective_id, has_side_effects=True, vmem_limit_bytes=32 * MiB
        ),
        name="gather_wt",
    )(x)


class Reduce:
    def __init__(self, place, part, bufs, chunk, rows):
        self.place, self.part, self.chunk, self.rows = place, part, chunk, rows
        (self.pair, self.out, self.landed, self.s1, self.r1, self.s2, self.r2) = bufs
        self.s = way(chunk)

    def start(self):
        p, q, s = self.place, self.chunk, self.s
        self.first = {}
        for k in (2, -s, s, 0):
            target = lax.rem(p.z + k + 4, 4) * 2 + 1 - p.core
            copy = remote(
                self.part.at[self.rows, p.cols(target)], self.pair.at[q, k % 4],
                self.s1.at[q, k % 4], self.r1.at[q, k % 4], {"wt": p.sib},
            )
            copy.start()
            self.first[k] = copy

    def both(self, k):
        p, q = self.place, self.chunk
        self.first[k].wait_recv()
        own = self.part[self.rows, p.cols(p.peer(k))]
        return own.astype(f32) + self.pair[q, k % 4].astype(f32)

    def onward(self, k, value, hop):
        p, q = self.place, self.chunk
        self.out[q, k % 4] = value.astype(bf16)
        copy = remote(
            self.out.at[q, k % 4], self.landed.at[q, k % 4], self.s2.at[q, k % 4],
            self.r2.at[q, k % 4], {"wt": p.peer(hop)},
        )
        copy.start()
        self.second[k] = copy

    def pass_on(self):
        self.second = {}
        self.onward(2, self.both(2), self.s)
        self.onward(-self.s, self.both(-self.s), -self.s)

    def pass_more(self):
        q, s = self.chunk, self.s
        value = self.both(s)
        self.second[2].wait_recv()
        self.onward(s, value + self.landed[q, 2].astype(f32), s)

    def total(self):
        q = self.chunk
        total = self.both(0)
        for k in (-self.s, self.s):
            self.second[k].wait_recv()
            total = total + self.landed[q, k % 4].astype(f32)
        return total

    def finish(self):
        for copy in self.first.values():
            copy.wait_send()
        for copy in self.second.values():
            copy.wait_send()


def sum_in_turn(sums, use):
    for one in sums:
        one.start()
    for one in sums:
        one.pass_on()
    for one in sums:
        one.pass_more()
    for q in range(len(sums)):
        use(q)


def reduce_scratch(chunks, rows, width):
    return [pltpu.VMEM((chunks, 4, rows, width), bf16) for _ in range(3)] + [
        pltpu.SemaphoreType.DMA((chunks, 4)) for _ in range(4)
    ]


def column(line, blocks):
    eye = lax.broadcasted_iota(jnp.int32, (128, 128), 0) == lax.broadcasted_iota(
        jnp.int32, (128, 128), 1
    )
    parts = [
        jnp.sum(
            jnp.where(eye, jnp.broadcast_to(line[j : j + 1, :], (128, 128)), 0.0),
            axis=1, keepdims=True,
        )
        for j in range(blocks)
    ]
    return jnp.concatenate(parts, axis=0)


def swap_sections(src, dst, send, recv):
    return remote(src, dst, send, recv, {"section": 1 - lax.axis_index("section")})


def forward_mid_kernel(chunks, part, skip, mid, whole, agsrc, *scratch):
    bufs, sems = scratch[:7], scratch[7:]
    place = WtPlace(skip.shape[1])
    greet_wt(place)
    rows = skip.shape[0] // chunks
    spans = [pl.ds(q * rows, rows) for q in range(chunks)]
    sums = [Reduce(place, part, bufs, q, spans[q]) for q in range(chunks)]
    gathers = [Gather(place, whole, sems, q, spans[q]) for q in range(chunks)]

    def use(q):
        value = skip[spans[q], :].astype(f32) + sums[q].total()
        mid[spans[q], :] = value
        agsrc[spans[q], :] = value.astype(bf16)
        gathers[q].start(agsrc.at[spans[q]])

    sum_in_turn(sums, use)
    gather_all(gathers)
    for one in sums:
        one.finish()


def forward_mid(part, skip, collective_id, chunks=4):
    rows, width = skip.shape
    return pl.pallas_call(
        functools.partial(forward_mid_kernel, chunks),
        out_shape=(
            jax.ShapeDtypeStruct((rows, width), f32),
            jax.ShapeDtypeStruct((rows, 8 * width), bf16),
        ),
        in_specs=[pl.BlockSpec(memory_space=pltpu.VMEM)] * 2,
        out_specs=(
            pl.BlockSpec(memory_space=pltpu.VMEM),
            pl.BlockSpec(memory_space=pl.ANY),
        ),
        scratch_shapes=[pltpu.VMEM((rows, width), bf16)]
        + reduce_scratch(chunks, rows // chunks, width)
        + gather_scratch(chunks),
        compiler_params=pltpu.CompilerParams(
            collective_id=collective_id, has_side_effects=True, vmem_limit_bytes=32 * MiB
        ),
        name="sum_mid_gather",
    )(part, skip)


def forward_pass_kernel(
    chunks, part, mid, begin, share, whole, agsrc, arrived, xsend, xrecv, *scratch
):
    bufs, sems = scratch[:7], scratch[7:]
    place = WtPlace(mid.shape[1])
    section = lax.axis_index("section")
    greet_wt(place, [{"section": 1 - section}])
    rows = mid.shape[0] // chunks
    spans = [pl.ds(q * rows, rows) for q in range(chunks)]
    sums = [Reduce(place, part, bufs, q, spans[q]) for q in range(chunks)]
    gathers = [Gather(place, whole, sems, q, spans[q]) for q in range(chunks)]
    swaps = []

    def use(q):
        agsrc[spans[q], :] = (mid[spans[q], :] + sums[q].total()).astype(bf16)
        swap = swap_sections(
            agsrc.at[spans[q]], arrived.at[spans[q]], xsend.at[q], xrecv.at[q]
        )
        swap.start()
        swaps.append(swap)

    sum_in_turn(sums, use)
    for q in range(chunks):
        swaps[q].wait_recv()
        share[spans[q], :] = jnp.where(
            section == 0, begin[spans[q], :].astype(f32), arrived[spans[q], :].astype(f32)
        ).astype(bf16)
        gathers[q].start(share.at[spans[q]])
    gather_all(gathers)
    for one in sums:
        one.finish()
    for one in swaps:
        one.wait_send()


def forward_pass(part, mid, begin, collective_id, chunks=4):
    rows, width = mid.shape
    return pl.pallas_call(
        functools.partial(forward_pass_kernel, chunks),
        out_shape=(
            jax.ShapeDtypeStruct((rows, width), bf16),
            jax.ShapeDtypeStruct((rows, 8 * width), bf16),
        ),
        in_specs=[pl.BlockSpec(memory_space=pltpu.VMEM)] * 3,
        out_specs=(
            pl.BlockSpec(memory_space=pltpu.VMEM),
            pl.BlockSpec(memory_space=pl.ANY),
        ),
        scratch_shapes=[
            pltpu.VMEM((rows, width), bf16),
            pltpu.VMEM((rows, width), bf16),
            pltpu.SemaphoreType.DMA((chunks,)),
            pltpu.SemaphoreType.DMA((chunks,)),
        ]
        + reduce_scratch(chunks, rows // chunks, width)
        + gather_scratch(chunks),
        compiler_params=pltpu.CompilerParams(
            collective_id=collective_id, has_side_effects=True, vmem_limit_bytes=32 * MiB
        ),
        name="sum_pass_gather",
    )(part, mid, begin)


def add_up(dst, sources, step=64):
    def some(i, carry):
        span = pl.ds(pl.multiple_of(i * step, step), step)
        total = sources[0][span, :].astype(f32)
        for source in sources[1:]:
            total = total + source[span, :].astype(f32)
        dst[span, :] = total.astype(dst.dtype)
        return carry

    lax.fori_loop(0, dst.shape[0] // step, some, 0)


class CtxPlace:
    def __init__(self):
        self.me = lax.axis_index("ctx")
        self.x = self.me // 2
        self.y = self.me % 2

    def at(self, k, y):
        return lax.rem(self.x + k + 4, 4) * 2 + y

    def x_peer(self, hop):
        return {"ctx": self.at(hop, self.y)}

    def y_peer(self):
        return {"ctx": self.at(0, 1 - self.y)}

    def near(self):
        return [self.x_peer(1), self.x_peer(-1), self.y_peer()]

    def all(self):
        return [{"ctx": lax.rem(self.me + d, 8)} for d in range(1, 8)]


class XRing:
    def __init__(self, place, s, loaded, bufs, sems):
        self.place, self.s, self.loaded = place, s, loaded
        self.via, self.near, self.joined, self.summed = bufs
        self.send, self.recv = sems
        self.copies = {}

    def go(self, i, src, dst, hop):
        copy = remote(src, dst, self.send.at[i], self.recv.at[i], self.place.x_peer(hop))
        copy.start()
        self.copies[i] = copy

    def start(self, k):
        if k == 2:
            self.go(0, self.loaded(2), self.via, self.s)
        elif k == -self.s:
            self.go(1, self.loaded(k), self.near, k)

    def join(self):
        self.copies[0].wait_recv()
        add_up(self.summed, [self.loaded(self.s), self.via])
        self.go(2, self.summed, self.joined, self.s)

    def total(self, dst):
        self.copies[1].wait_recv()
        self.copies[2].wait_recv()
        add_up(dst, [self.loaded(0), self.near, self.joined])

    def finish(self):
        for copy in self.copies.values():
            copy.wait_send()


def cut(array, dim, owner):
    length = array.shape[dim] // 8
    span = pl.ds(pl.multiple_of(owner * length, length), length)
    return array.at[span] if dim == 0 else array.at[:, span]


BLOCKS = (2, -1, 1, 0)


class XFirst:
    def __init__(self, place, array, dim, out, scratch):
        self.place, self.out = place, out
        bufs, summed, self.swapped, sems, self.ssend, self.srecv, *held = scratch
        self.held, self.lsem = held if held else (None, None)

        def block(k, y):
            return cut(array, dim, place.at(k, y))

        def loaded(k, y):
            if held and k in (0, way(y)):
                return self.held.at[abs(k), y]
            return block(k, y)

        self.block = block
        self.rings = [
            XRing(
                place, way(y), lambda k, y=y: loaded(k, y),
                [bufs.at[y, j] for j in range(3)] + [summed.at[y]],
                [sems.at[0, y], sems.at[1, y]],
            )
            for y in (0, 1)
        ]

    def start(self):
        self.loads = []
        for y, ring in enumerate(self.rings):
            ring.start(2)
            ring.start(-ring.s)
        if self.held is not None:
            for y in (0, 1):
                for k in (way(y), 0):
                    copy = pltpu.make_async_copy(
                        self.block(k, y), self.held.at[abs(k), y], self.lsem.at[abs(k), y]
                    )
                    copy.start()
                    self.loads.append(copy)

    def join(self):
        for copy in self.loads:
            copy.wait()
        for ring in self.rings:
            ring.join()

    def swap(self):
        for y in (0, 1):
            self.rings[y].total(self.swapped.at[1 + y])
        self.across = remote(
            self.swapped.at[1 + (1 - self.place.y)], self.swapped.at[0], self.ssend.at[0],
            self.srecv.at[0], self.place.y_peer(),
        )
        self.across.start()

    def total(self):
        self.across.wait_recv()
        add_up(self.out, [self.swapped.at[1 + self.place.y], self.swapped.at[0]])

    def finish(self):
        for ring in self.rings:
            ring.finish()
        self.across.wait_send()


class YFirst:
    def __init__(self, place, array, dim, out, scratch):
        self.place, self.array, self.dim, self.out = place, array, dim, out
        (bufs, summed, self.swapped, sems, self.ssend, self.srecv, self.held, self.lsem) = scratch
        swapped = self.swapped
        self.half = half = self.held.shape[1] // 2
        self.rings = [
            XRing(
                place, way(h), lambda k, h=h: swapped.at[k % 4, pl.ds(h * half, half)],
                [bufs.at[h, j] for j in range(3)] + [summed.at[h]],
                [sems.at[0, h], sems.at[1, h]],
            )
            for h in (0, 1)
        ]

    def start(self):
        self.swaps, self.loads = {}, {}
        for k in BLOCKS:
            copy = remote(
                cut(self.array, self.dim, self.place.at(k, 1 - self.place.y)),
                self.swapped.at[k % 4], self.ssend.at[k % 4], self.srecv.at[k % 4],
                self.place.y_peer(),
            )
            copy.start()
            self.swaps[k] = copy
        for k in BLOCKS:
            copy = pltpu.make_async_copy(
                cut(self.array, self.dim, self.place.at(k, self.place.y)),
                self.held.at[k % 4], self.lsem.at[k % 4],
            )
            copy.start()
            self.loads[k] = copy

    def first(self):
        for k in BLOCKS:
            self.loads[k].wait()
            self.swaps[k].wait_recv()
            block = self.swapped.at[k % 4]
            add_up(block, [block, self.held.at[k % 4]])
            for ring in self.rings:
                ring.start(k)

    def join(self):
        for ring in self.rings:
            ring.join()

    def total(self):
        for h, ring in enumerate(self.rings):
            ring.total(self.out.at[pl.ds(h * self.half, self.half)])

    def finish(self):
        for ring in self.rings:
            ring.finish()
        for copy in self.swaps.values():
            copy.wait_send()


def owned(shape, dim):
    return tuple(n // 8 if i == dim else n for i, n in enumerate(shape))


def ctx_scratch(shape, dim, mode):
    rows, width = owned(shape, dim)
    ring = (rows // 2 if mode == "y" else rows, width)
    scratch = [
        pltpu.VMEM((2, 3, *ring), bf16),
        pltpu.VMEM((2, *ring), bf16),
        pltpu.VMEM((4 if mode == "y" else 3, rows, width), bf16),
        pltpu.SemaphoreType.DMA((2, 2, 3)),
        pltpu.SemaphoreType.DMA((4,)),
        pltpu.SemaphoreType.DMA((4,)),
    ]
    if mode == "y":
        scratch += [pltpu.VMEM((4, rows, width), bf16), pltpu.SemaphoreType.DMA((4,))]
    elif mode == "x":
        scratch += [pltpu.VMEM((2, 2, rows, width), bf16), pltpu.SemaphoreType.DMA((2, 2))]
    return scratch


def everyone(place):
    return [lax.rem(place.me + d, 8) for d in range(1, 8)]


class Lines:
    def __init__(self, place, line, slots, send, recv):
        self.line, self.slots = line, slots
        self.copies = [
            remote(line, slots.at[d], send.at[d], recv.at[d], {"wt": lax.rem(place.me + d, 8)})
            for d in range(1, 8)
        ]

    def start(self):
        for copy in self.copies:
            copy.start()

    def total(self):
        total = self.line[...]
        for d, copy in enumerate(self.copies, start=1):
            copy.wait_recv()
            total = total + self.slots[d]
        return total

    def finish(self):
        for copy in self.copies:
            copy.wait_send()


def norm_back(total, above, own, scale, gain, mean):
    normed = own * scale
    grad = above.astype(f32) + scale * (total * gain - normed * mean)
    return grad, jnp.sum(total * normed, axis=0, keepdims=True)


def backward_kernel(mode, chunks, part, line, above, own, factor, gain, *rest):
    if mode == "mid":
        share, whole, agsrc, *rest = rest
    else:
        begin, share, whole, agsrc, arrived, xsend, xrecv, *rest = rest
    slots, lsend, lrecv, *rest = rest
    bufs, sems = rest[:7], rest[7:]
    place = WtPlace(own.shape[1])
    section = lax.axis_index("section")
    greet(
        [{"wt": peer} for peer in everyone(place)]
        + ([{"section": 1 - section}] if mode == "pass" else [])
    )
    rows = own.shape[0] // chunks
    depth = 8 * own.shape[1]
    spans = [pl.ds(q * rows, rows) for q in range(chunks)]
    sums = [Reduce(place, part, bufs, q, spans[q]) for q in range(chunks)]
    gathers = [Gather(place, whole, sems, q, spans[q]) for q in range(chunks)]
    lines = Lines(place, line, slots, lsend, lrecv)
    lines.start()
    for one in sums:
        one.start()
    for one in sums:
        one.pass_on()
    for one in sums:
        one.pass_more()
    mean = column(lines.total(), own.shape[0] // 128) * (1.0 / depth)
    swaps = []
    for q in range(chunks):
        span = spans[q]
        grad, _ = norm_back(
            sums[q].total(), above[span, :], own[span, :], factor[span, :], gain[...],
            mean[q * rows : (q + 1) * rows],
        )
        agsrc[span, :] = grad.astype(bf16)
        if mode == "mid":
            share[span, :] = grad
            gathers[q].start(agsrc.at[span])
        else:
            swap = swap_sections(agsrc.at[span], arrived.at[span], xsend.at[q], xrecv.at[q])
            swap.start()
            swaps.append(swap)
    if mode == "pass":
        for q in range(chunks):
            span = spans[q]
            swaps[q].wait_recv()
            share[span, :] = jnp.where(
                section == 1, begin[span, :].astype(f32), arrived[span, :].astype(f32)
            ).astype(bf16)
            gathers[q].start(share.at[span])
    gather_all(gathers)
    for one in sums:
        one.finish()
    for one in swaps:
        one.wait_send()
    lines.finish()


def seven():
    return [pltpu.SemaphoreType.DMA((8,)), pltpu.SemaphoreType.DMA((8,))]


def backward_sum(mode, part, line, above, own, factor, gain, extra, collective_id, chunks=4):
    rows, width = own.shape
    vmem = pl.BlockSpec(memory_space=pltpu.VMEM)
    hbm = pl.BlockSpec(memory_space=pl.ANY)
    scratch = [pltpu.VMEM((rows, width), bf16)]
    if mode == "pass":
        scratch += [
            pltpu.VMEM((rows, width), bf16),
            pltpu.SemaphoreType.DMA((chunks,)),
            pltpu.SemaphoreType.DMA((chunks,)),
        ]
    scratch += [pltpu.VMEM((8, 8, 128), f32)] + seven()
    scratch += reduce_scratch(chunks, rows // chunks, width) + gather_scratch(chunks)
    operands = [part, line, above, own, factor, gain] + extra
    return pl.pallas_call(
        functools.partial(backward_kernel, mode, chunks),
        out_shape=(
            jax.ShapeDtypeStruct((rows, width), f32 if mode == "mid" else bf16),
            jax.ShapeDtypeStruct((rows, 8 * width), bf16),
        ),
        in_specs=[vmem] * len(operands),
        out_specs=(vmem, hbm),
        scratch_shapes=scratch,
        compiler_params=pltpu.CompilerParams(
            collective_id=collective_id, has_side_effects=True, vmem_limit_bytes=32 * MiB
        ),
        name="sum_back_" + mode,
    )(*operands)


def lanes(shape):
    return lax.broadcasted_iota(jnp.int32, shape, len(shape) - 1)


def turn(u, cosine, sine):
    low_half = jnp.bitwise_and(lanes(u.shape), HD - 1) < HD // 2
    turned = jnp.where(low_half, -pltpu.roll(u, 128 - HD // 2, 1), pltpu.roll(u, HD // 2, 1))
    return u * cosine + turned * sine


def turn_back(y, cosine, sine):
    low_half = jnp.bitwise_and(lanes(y.shape), HD - 1) < HD // 2
    z = y * sine
    turned = jnp.where(low_half, pltpu.roll(z, 128 - HD // 2, 1), -pltpu.roll(z, HD // 2, 1))
    return y * cosine + turned


def visible_keys(bounds, b, key_block, me, rows, heads):
    row = lax.broadcasted_iota(jnp.int32, (1, heads * rows), 1)
    for head in range(1, heads):
        row = row - jnp.where(lanes((1, heads * rows)) >= head * rows, rows, 0)
    place = me * rows + row
    first, second = bounds[b, 0], bounds[b, 1]
    begin = jnp.where(place >= second, second, jnp.where(place >= first, first, 0))
    key = key_block * rows + lax.broadcasted_iota(jnp.int32, (rows, 1), 0)
    return (key <= place) & (key >= begin)


def stack_queries(flat, cosine, sine, b, rows, stacked):
    span = pl.ds(b * rows, rows)
    low = lanes((rows, 128)) < HD
    for pair in range(2):
        u = turn(flat[span, 128 * pair : 128 * pair + 128], cosine[span, :], sine[span, :])
        u = u.astype(bf16).astype(f32) * (HD**-0.5)
        even = jnp.where(low, u, 0.0)
        odd = jnp.where(low, pltpu.roll(u, HD, 1), 0.0)
        stacked[b, pl.ds(2 * pair * rows, rows), :] = even.astype(bf16)
        stacked[b, pl.ds((2 * pair + 1) * rows, rows), :] = odd.astype(bf16)


def later(me, d, n):
    return me + d < n


def earlier(me, d, n):
    return me - d >= 0


def greet_order(me, n, side, count):
    barrier = pltpu.get_barrier_semaphore()
    step = 1 if side is later else n - 1
    for d in range(1, n):

        @pl.when(side(me, d, n))
        def _():
            pl.semaphore_signal(
                barrier, inc=1, device_id={"ctx": lax.rem(me + d * step, n)},
                device_id_type=MESH,
            )

    def wait():
        @pl.when(count > 0)
        def _():
            pl.semaphore_wait(barrier, count)

    return wait


def attention_kernel(
    n, bounds, flat, kv_pre, cosine, sine, kv_cosine, kv_sine, mix, logs, mixed, kv,
    stacked, acc, mine, send, recv
):
    me = lax.axis_index("ctx")
    rows = kv.shape[2]
    heads = 4
    wait = greet_order(me, n, earlier, n - 1 - me)
    for b in range(2):
        span = pl.ds(b * rows, rows)
        turned = turn(kv_pre[span, :], kv_cosine[span, :], kv_sine[span, :]).astype(bf16)
        mine[b] = turned
        kv[me, b] = turned
    wait()

    def copy(d):
        return remote(mine, kv.at[me], send.at[d], recv.at[d], {"ctx": lax.rem(me + d, n)})

    for d in reversed(range(1, n)):

        @pl.when(later(me, d, n))
        def _():
            copy(d).start()

    for b in range(2):
        stack_queries(flat, cosine, sine, b, rows, stacked)
    acc[...] = jnp.zeros_like(acc)

    def block(j, carry):
        after = []
        for b in range(2):
            peak, total = carry[2 * b : 2 * b + 2]
            keys = kv[j, b]
            scores = times_transposed(keys, stacked[b])
            scores = jnp.where(visible_keys(bounds, b, j, me, rows, heads), scores, neg_big)
            new_peak = jnp.maximum(peak, jnp.max(scores, axis=0, keepdims=True))
            shrink = jnp.exp(peak - new_peak)
            weight = jnp.exp(scores - new_peak)
            total = total * shrink + jnp.sum(weight, axis=0, keepdims=True)
            acc[b] = acc[b] * shrink + contract_rows(keys, weight.astype(bf16))
            after += [new_peak, total]
        return tuple(after)

    def arrived(d, carry):
        copy(d).wait_recv()
        return block(me - d, carry)

    zero = jnp.zeros((1, heads * rows), f32)
    done = block(me, (zero + neg_big, zero) * 2)
    done = lax.fori_loop(1, me + 1, arrived, done)
    low = lanes((rows, 128)) < HD
    for b in range(2):
        peak, total = done[2 * b : 2 * b + 2]
        out = acc[b] / total
        mixed[b] = out
        logs[b] = peak + jnp.log(total)
        upright = out.T
        for pair in range(2):
            even = upright[2 * pair * rows : (2 * pair + 1) * rows]
            odd = upright[(2 * pair + 1) * rows : (2 * pair + 2) * rows]
            both = jnp.where(low, pltpu.roll(even, HD, 1), odd)
            mix[pl.ds(b * rows, rows), 128 * pair : 128 * pair + 128] = both.astype(bf16)
    for d in range(1, n):

        @pl.when(later(me, d, n))
        def _():
            copy(d).wait_send()


def attention(bounds, flat, kv_pre, cosine, sine, kv_cosine, kv_sine, collective_id):
    n = 8
    rows = flat.shape[0] // 2
    vmem = pl.BlockSpec(memory_space=pltpu.VMEM)
    return pl.pallas_call(
        functools.partial(attention_kernel, n),
        out_shape=(
            jax.ShapeDtypeStruct((2 * rows, 256), bf16),
            jax.ShapeDtypeStruct((2, 1, 4 * rows), f32),
            jax.ShapeDtypeStruct((2, 128, 4 * rows), f32),
            jax.ShapeDtypeStruct((n, 2, rows, 128), bf16),
        ),
        in_specs=[pl.BlockSpec(memory_space=pltpu.SMEM)] + [vmem] * 6,
        out_specs=(vmem,) * 4,
        scratch_shapes=[
            pltpu.VMEM((2, 4 * rows, 128), bf16),
            pltpu.VMEM((2, 128, 4 * rows), f32),
            pltpu.VMEM((2, rows, 128), bf16),
            pltpu.SemaphoreType.DMA((n,)),
            pltpu.SemaphoreType.DMA((n,)),
        ],
        compiler_params=pltpu.CompilerParams(
            collective_id=collective_id, has_side_effects=True, vmem_limit_bytes=40 * MiB
        ),
        name="attention",
    )(bounds, flat, kv_pre, cosine, sine, kv_cosine, kv_sine)


def attention_back_kernel(n, *refs):
    me = lax.axis_index("ctx")
    attention_back_steps(n, me, greet_order(me, n, later, me), *refs)


def attention_back_steps(
    n, me, wait, bounds, flat, cosine, sine, kv_cosine, kv_sine, kv, logs, mixed, grad, out,
    grad_kv, terms, slots, total, stacked, grads, acc, send, recv
):
    rows = kv.shape[2]
    heads = 4
    low = lanes((rows, 128)) < HD
    deltas = []
    for b in range(2):
        stack_queries(flat, cosine, sine, b, rows, stacked)
        for pair in range(2):
            u = grad[pl.ds(b * rows, rows), 128 * pair : 128 * pair + 128].astype(f32)
            even = jnp.where(low, 0.0, pltpu.roll(u, HD, 1))
            odd = jnp.where(low, 0.0, u)
            grads[b, pl.ds(2 * pair * rows, rows), :] = even.astype(bf16)
            grads[b, pl.ds((2 * pair + 1) * rows, rows), :] = odd.astype(bf16)
        deltas.append(
            jnp.sum(mixed[b] * grads[b].astype(f32).T, axis=0, keepdims=True)
        )
    acc[...] = jnp.zeros_like(acc)
    wait()

    def block(j):
        for b in range(2):
            keys = kv[j, b]
            scores = times_transposed(keys, stacked[b])
            probs = jnp.where(
                visible_keys(bounds, b, j, me, rows, heads), jnp.exp(scores - logs[b]), 0.0
            )
            grad_probs = times_transposed(keys, grads[b])
            grad_scores = (probs * (grad_probs - deltas[b])).astype(bf16)
            acc[b] += contract_rows(keys, grad_scores)
            terms[j, b] = (
                jnp.dot(grad_scores, stacked[b], preferred_element_type=f32)
                + jnp.dot(probs.astype(bf16), grads[b], preferred_element_type=f32)
            ).astype(bf16)

    def copy(d):
        back = lax.rem(me + n - d, n)
        return remote(terms.at[back], slots.at[d], send.at[d], recv.at[d], {"ctx": back})

    def block_sent(j, carry):
        block(j)
        copy(me - j).start()
        return carry

    lax.fori_loop(0, me, block_sent, 0)
    block(me)
    for b in range(2):
        span = pl.ds(b * rows, rows)
        upright = acc[b].T * (HD**-0.5)
        for pair in range(2):
            even = upright[2 * pair * rows : (2 * pair + 1) * rows]
            odd = upright[(2 * pair + 1) * rows : (2 * pair + 2) * rows]
            both = jnp.where(low, even, pltpu.roll(odd, HD, 1))
            out[span, 128 * pair : 128 * pair + 128] = turn_back(
                both, cosine[span, :], sine[span, :]
            ).astype(bf16)
    for b in range(2):
        total[b] = terms[me, b].astype(f32)
    for d in range(1, n):

        @pl.when(later(me, d, n))
        def _():
            copy(d).wait_recv()
            total[...] += slots[d].astype(f32)

    for b in range(2):
        span = pl.ds(b * rows, rows)
        grad_kv[span, :] = turn_back(
            total[b], kv_cosine[span, :], kv_sine[span, :]
        ).astype(bf16)
    for d in range(1, n):

        @pl.when(earlier(me, d, n))
        def _():
            copy(d).wait_send()


def attention_back_scratch(shape):
    n, two, rows, width = shape
    return [
        pltpu.VMEM(shape, bf16),
        pltpu.VMEM(shape, bf16),
        pltpu.VMEM((2, rows, width), f32),
        pltpu.VMEM((2, 4 * rows, 128), bf16),
        pltpu.VMEM((2, 4 * rows, 128), bf16),
        pltpu.VMEM((2, 128, 4 * rows), f32),
        pltpu.SemaphoreType.DMA((n,)),
        pltpu.SemaphoreType.DMA((n,)),
    ]


def attention_back(
    bounds, flat, cosine, sine, kv_cosine, kv_sine, kv, logs, mixed, grad, collective_id
):
    n, two, rows, width = kv.shape
    vmem = pl.BlockSpec(memory_space=pltpu.VMEM)
    return pl.pallas_call(
        functools.partial(attention_back_kernel, n),
        out_shape=(
            jax.ShapeDtypeStruct((2 * rows, 256), bf16),
            jax.ShapeDtypeStruct((2 * rows, 128), bf16),
        ),
        in_specs=[pl.BlockSpec(memory_space=pltpu.SMEM)] + [vmem] * 9,
        out_specs=(vmem, vmem),
        scratch_shapes=attention_back_scratch(kv.shape),
        compiler_params=pltpu.CompilerParams(
            collective_id=collective_id, has_side_effects=True, vmem_limit_bytes=40 * MiB
        ),
        name="attention_back",
    )(bounds, flat, cosine, sine, kv_cosine, kv_sine, kv, logs, mixed, grad)


def as_line(column_values, line):
    eye = lax.broadcasted_iota(jnp.int32, (128, 128), 0) == lax.broadcasted_iota(
        jnp.int32, (128, 128), 1
    )
    line[...] = jnp.zeros_like(line)
    for j in range(column_values.shape[0] // 128):
        block = column_values[128 * j : 128 * j + 128]
        line[j : j + 1, :] = jnp.sum(
            jnp.where(eye, jnp.broadcast_to(block, (128, 128)), 0.0), axis=0, keepdims=True
        )


CTX_NAMES = ("down_a", "up", "down_b", "gate", "pre", "out")
CTX_DIMS = dict(down_a=1, up=0, down_b=1, gate=0, pre=0, out=1)
CTX_MODES = dict(down_a="x", up="x", down_b="y", gate="y", pre="local", out="local")


def end_kernel(n, chunks, names, *refs):
    r, at = {}, 0
    for name, count in names:
        r[name] = refs[at] if count == 1 else refs[at : at + count]
        at += count
    place, ctx = WtPlace(r["mid"].shape[1]), CtxPlace()
    greet([{"wt": peer} for peer in everyone(place)] + ctx.all())
    width = r["mid"].shape[1]
    all_rows = r["mid"].shape[0]
    rows = all_rows // chunks
    depth = 8 * width
    spans = [pl.ds(q * rows, rows) for q in range(chunks)]
    blocks = [pl.ds(width * c, width) for c in range(8)]
    inner_sums = {
        name: (YFirst if CTX_MODES[name] == "y" else XFirst)(
            ctx, r[name], CTX_DIMS[name], r["own_" + name], r["sum_" + name]
        )
        for name in CTX_NAMES
    }
    down_a, up, down_b, gate, pre, out = (inner_sums[name] for name in CTX_NAMES)

    sums = [Reduce(place, r["part"], r["reduce"], q, spans[q]) for q in range(chunks)]
    gathers = [Gather(place, r["whole"], r["gather"], q, spans[q]) for q in range(chunks)]
    lines = Lines(place, r["line"], *r["slots"])
    lines.start()
    for one in sums:
        one.start()
    for one in (down_a, up, down_b, gate):
        one.start()
    for one in sums:
        one.pass_on()
    for one in sums:
        one.pass_more()
    mean = column(lines.total(), all_rows // 128) * (1.0 / depth)
    terms = jnp.zeros((1, width), f32)
    for q in range(chunks):
        span = spans[q]
        grad, term = norm_back(
            sums[q].total(), r["above"][span, :], r["mid"][span, :], r["mid_factor"][span, :],
            r["mid_gain"][...], mean[q * rows : (q + 1) * rows],
        )
        terms = terms + term
        r["grad_mid"][span, :] = grad
        r["agsrc"][span, :] = grad.astype(bf16)
        gathers[q].start(r["agsrc"].at[span])
    r["piece"][8:16, :] = jnp.broadcast_to(terms, (8, width))
    for one in gathers:
        one.forward()
    for one in gathers:
        one.forward_more()
    down_a.join()
    for one in gathers:
        one.finish()
    last_sums = [
        Reduce(place, r["last_part"], r["last_reduce"], q, spans[q]) for q in range(chunks)
    ]
    for one in last_sums:
        one.start()
    r["grad_mix"][...] = times_transposed(r["whole"][...], r["w_out"][...]).astype(bf16)
    for one in last_sums:
        one.pass_on()
    down_b.first()

    grad_pre = r["grad_pre"]
    attention_back_steps(
        n, ctx.me, lambda: None, r["bounds"], r["flat"], r["cosine"], r["sine"],
        r["kv_cosine"], r["kv_sine"], r["kv"], r["logs"], r["mixed"], r["grad_mix"],
        grad_pre.at[:, pl.ds(0, 256)], grad_pre.at[:, pl.ds(256, 128)], *r["attention"]
    )
    up.join()
    for one in last_sums:
        one.pass_more()

    dots = jnp.zeros((all_rows, 1), f32)
    for block in blocks:
        partial_sum = times_transposed(grad_pre[...], r["w_qkv"][block, :])
        dots = dots + jnp.sum(
            partial_sum * r["attn_in"][:, block].astype(f32), axis=1, keepdims=True
        )
        r["part_in"][:, block] = partial_sum.astype(bf16)
    as_line(dots, r["line_in"])
    lines_in = Lines(place, r["line_in"], *r["slots_in"])
    lines_in.start()
    sums_in = [Reduce(place, r["part_in"], r["reduce_in"], q, spans[q]) for q in range(chunks)]
    for one in sums_in:
        one.start()
    for one in sums_in:
        one.pass_on()
    down_b.join()
    for block in blocks:
        r["pre"][block, :] = contract_rows(r["attn_in"][:, block], grad_pre[...]).astype(bf16)
    pre.start()
    for one in sums_in:
        one.pass_more()
    for block in blocks:
        r["out"][:, block] = contract_rows(r["mix"][...], r["whole"][:, block]).astype(bf16)
    out.start()
    mean = column(lines_in.total(), all_rows // 128) * (1.0 / depth)
    terms = jnp.zeros((1, width), f32)
    for q in range(chunks):
        span = spans[q]
        grad, term = norm_back(
            sums_in[q].total(), r["grad_mid"][span, :], r["hidden"][span, :],
            r["factor"][span, :], r["gain"][...], mean[q * rows : (q + 1) * rows],
        )
        terms = terms + term
        r["first_grad"][span, :] = grad.astype(bf16)
    r["piece"][0:8, :] = jnp.broadcast_to(terms, (8, width))
    piece, pieces = r["piece"], r["pieces"]
    gsend, grecv = r["piece_sems"]
    piece_copies = [
        remote(
            piece, pieces.at[place.me], gsend.at[d], grecv.at[d],
            {"wt": lax.rem(place.me + d, 8)},
        )
        for d in range(1, 8)
    ]
    for copy in piece_copies:
        copy.start()
    pieces[place.me] = piece[...]
    down_a.swap()
    up.swap()
    for q in range(chunks):
        span = spans[q]
        r["result"][span, :] = (r["last_mid"][span, :] + last_sums[q].total()).astype(bf16)
    for copy in piece_copies:
        copy.wait()
    osend, orecv = r["owner_sems"]
    owner_copies = []
    for d in range(1, 8):
        owner = lax.rem(ctx.me + d, 8)
        copy = remote(
            pieces.at[owner], r["gain_slots"].at[d], osend.at[d], orecv.at[d], {"ctx": owner}
        )
        copy.start()
        owner_copies.append(copy)
    pre.join()
    out.join()
    down_b.total()
    gate.first()
    pre.swap()
    out.swap()
    gate.join()
    down_a.total()
    up.total()
    total = pieces[ctx.me]
    for d, copy in enumerate(owner_copies, start=1):
        copy.wait_recv()
        total = total + r["gain_slots"][d]
    r["gains"][...] = total
    pre.total()
    out.total()
    gate.total()
    for one in sums + sums_in + last_sums + list(inner_sums.values()):
        one.finish()
    for copy in owner_copies:
        copy.wait_send()
    lines.finish()
    lines_in.finish()


def end_of_backward(operands, hbm_names, out_shapes, collective_id, chunks=4):
    n = 8
    rows, width = operands["mid"].shape
    vmem = pl.BlockSpec(memory_space=pltpu.VMEM)
    kinds = {name: pl.BlockSpec(memory_space=pl.ANY) for name in hbm_names}
    kinds["bounds"] = pl.BlockSpec(memory_space=pltpu.SMEM)
    shapes = {name: operands[name].shape for name in hbm_names}
    shapes |= dict(pre=(8 * width, 384), out=(width, 8 * width))
    outs = dict(out_shapes)
    for name in CTX_NAMES:
        outs["own_" + name] = (owned(shapes[name], CTX_DIMS[name]), bf16)
    reduce = reduce_scratch(chunks, rows // chunks, width)
    slots = [pltpu.VMEM((8, 8, 128), f32)] + seven()
    scratch = dict(
        whole=[pltpu.VMEM((rows, 8 * width), bf16)],
        part_in=[pltpu.VMEM((rows, 8 * width), bf16)],
        pre=[pltpu.VMEM(shapes["pre"], bf16)],
        out=[pltpu.VMEM(shapes["out"], bf16)],
        grad_mid=[pltpu.VMEM((rows, width), f32)],
        agsrc=[pltpu.VMEM((rows, width), bf16)],
        grad_mix=[pltpu.VMEM((rows, width), bf16)],
        grad_pre=[pltpu.VMEM((rows, 384), bf16)],
        line_in=[pltpu.VMEM((8, 128), f32)],
        piece=[pltpu.VMEM((16, width), f32)],
        pieces=[pltpu.VMEM((8, 16, width), f32)],
        gain_slots=[pltpu.VMEM((8, 16, width), f32)],
        piece_sems=seven(),
        owner_sems=seven(),
        slots=slots,
        slots_in=slots,
        reduce=reduce,
        reduce_in=reduce,
        last_reduce=reduce,
        gather=gather_scratch(chunks),
        attention=attention_back_scratch(operands["kv"].shape),
    )
    for name in CTX_NAMES:
        scratch["sum_" + name] = ctx_scratch(shapes[name], CTX_DIMS[name], CTX_MODES[name])
    names = (
        [(name, 1) for name in operands] + [(name, 1) for name in outs]
        + [(name, len(specs)) for name, specs in scratch.items()]
    )
    results = pl.pallas_call(
        functools.partial(end_kernel, n, chunks, names),
        out_shape=tuple(jax.ShapeDtypeStruct(*one) for one in outs.values()),
        in_specs=[kinds.get(name, vmem) for name in operands],
        out_specs=(vmem,) * len(outs),
        scratch_shapes=[spec for specs in scratch.values() for spec in specs],
        compiler_params=pltpu.CompilerParams(
            collective_id=collective_id, has_side_effects=True, vmem_limit_bytes=60 * MiB
        ),
        name="end_of_backward",
    )(*operands.values())
    return dict(zip(outs, results))


def per_device(
    inputs,
    cotangent,
    doc_bounds,
    attn_gain,
    w_query,
    w_key,
    w_value,
    w_out,
    mlp_gain,
    w_gate,
    w_up,
    w_down,
):
    ctx_rank = lax.axis_index("ctx")
    wt_rank = lax.axis_index("wt")
    micro_count, block_rows, share_width = inputs.shape
    rows = micro_count * block_rows
    gain_attn = attn_gain.astype(f32)
    gain_mlp = mlp_gain.astype(f32)
    own_gain_attn = lax.dynamic_slice_in_dim(gain_attn, wt_rank * share_width, share_width, 1)
    own_gain_mlp = lax.dynamic_slice_in_dim(gain_mlp, wt_rank * share_width, share_width, 1)
    w_qkv = jnp.concatenate([w_query[0], w_key[0], w_value[0]], axis=1)
    w_o, w_g, w_u, w_d = w_out[0], w_gate[0], w_up[0], w_down[0]
    begin = inputs.reshape(rows, share_width)
    cot = cotangent.reshape(rows, share_width)

    places = ctx_rank * block_rows + jnp.arange(block_rows, dtype=jnp.int32)
    offsets = jnp.concatenate(
        [places - doc_begins(doc_bounds[b], places) for b in range(micro_count)]
    )
    angles = offsets.astype(f32)[:, None] * rope_freqs(HD)[None, :]
    cos_half, sin_half = jnp.cos(angles), jnp.sin(angles)
    cosine = jnp.concatenate([cos_half] * 4, axis=1)
    sine = jnp.concatenate([sin_half] * 4, axis=1)
    key_lane = jnp.arange(128)[None, :] < HD
    kv_cosine = jnp.where(key_lane, cosine, 1.0)
    kv_sine = jnp.where(key_lane, sine, 0.0)

    def forward(whole, share, tick):
        hidden = whole.astype(f32)
        factor = lax.rsqrt(jnp.mean(hidden * hidden, axis=-1, keepdims=True) + eps)
        attn_in = (hidden * factor * gain_attn).astype(bf16)
        pre = jnp.dot(attn_in, w_qkv, preferred_element_type=f32)
        q_pre, kv_pre = pre[:, :256], pre[:, 256:]
        mix, logs, mixed, kv = attention(
            doc_bounds, q_pre, kv_pre, cosine, sine, kv_cosine, kv_sine, 1
        )
        part = jnp.dot(mix, w_o, preferred_element_type=f32).astype(bf16)
        mid, mid_whole = forward_mid(part, share, 2)
        mid_wide = mid_whole.astype(f32)
        mid_factor = lax.rsqrt(jnp.mean(mid_wide * mid_wide, axis=-1, keepdims=True) + eps)
        mlp_in = (mid_wide * mid_factor * gain_mlp).astype(bf16)
        gate = jnp.dot(mlp_in, w_g, preferred_element_type=f32)
        up = jnp.dot(mlp_in, w_u, preferred_element_type=f32)
        inner = lax.optimization_barrier((jax.nn.silu(gate) * up).astype(bf16))
        part = jnp.dot(inner, w_d, preferred_element_type=f32).astype(bf16)
        saved = dict(
            whole=whole, share=share, factor=factor, attn_in=attn_in, q_pre=q_pre, kv=kv,
            mix=mix, logs=logs, mixed=mixed, mid=mid, mid_whole=mid_whole,
            mid_factor=mid_factor, mlp_in=mlp_in, gate=gate, up=up, inner=inner,
        )
        return part, saved

    def line_of(part, whole, factor, gain):
        dots = jnp.sum(part * (whole.astype(f32) * factor * gain), axis=1)
        return jnp.concatenate(
            [dots.reshape(rows // 128, 128), jnp.zeros((8 - rows // 128, 128), f32)]
        )

    def behind_mlp(grad, saved):
        gate, up = saved["gate"], saved["up"]
        grad_inner = times_transposed(grad, w_d)
        sigmoid = jax.nn.sigmoid(gate)
        grad_gate = (grad_inner * up * sigmoid * (1.0 + gate * (1.0 - sigmoid))).astype(bf16)
        grad_up = (grad_inner * gate * sigmoid).astype(bf16)
        part = times_transposed(grad_gate, w_g) + times_transposed(grad_up, w_u)
        line = line_of(part, saved["mid_whole"], saved["mid_factor"], gain_mlp)
        return part.astype(bf16), line, grad_gate, grad_up

    def backward(grad, grad_share, saved):
        part, line, _, _ = behind_mlp(grad, saved)
        grad_mid, grad_attn = backward_sum(
            "mid", part, line, grad_share, saved["mid"], saved["mid_factor"], own_gain_mlp,
            [], 3,
        )
        grad_mix = times_transposed(grad_attn, w_o).astype(bf16)
        grad_query, grad_kv = attention_back(
            doc_bounds, saved["q_pre"], cosine, sine, kv_cosine, kv_sine, saved["kv"],
            saved["logs"], saved["mixed"], grad_mix, 4,
        )
        grad_pre = jnp.concatenate([grad_query, grad_kv], axis=1)
        part = times_transposed(grad_pre, w_qkv)
        line = line_of(part, saved["whole"], saved["factor"], gain_attn)
        return (
            part.astype(bf16), line, grad_mid, saved["share"].astype(f32), saved["factor"],
            own_gain_attn,
        )

    whole_cot = lax.all_gather(cot, "wt", axis=1, tiled=True)
    part, saved = forward(wt_gather(begin, 6), begin, 0)
    share, whole = forward_pass(part, saved["mid"], begin, 7)
    part, saved = forward(whole, share, 1)
    last_part = part

    operands = backward(whole_cot, cot, saved)
    section = lax.axis_index("section")
    grad_share, grad = backward_sum("pass", *operands, [cot], 9)
    part, line, grad_gate, grad_up = behind_mlp(grad, saved)
    half = saved["inner"].shape[1] // 2
    operands = dict(
        bounds=doc_bounds, part=part, line=line, above=grad_share, mid=saved["mid"],
        mid_factor=saved["mid_factor"], mid_gain=own_gain_mlp, flat=saved["q_pre"],
        cosine=cosine, sine=sine, kv_cosine=kv_cosine, kv_sine=kv_sine, kv=saved["kv"],
        logs=saved["logs"], mixed=saved["mixed"], w_out=w_o, w_qkv=w_qkv,
        attn_in=saved["attn_in"], mix=saved["mix"], hidden=saved["share"].astype(f32),
        factor=saved["factor"], gain=own_gain_attn, last_part=last_part,
        last_mid=saved["mid"],
        down_a=contract_rows(saved["inner"][:, :half], grad).astype(bf16),
        up=contract_rows(saved["mlp_in"], grad_up).astype(bf16),
        down_b=contract_rows(saved["inner"][:, half:], grad).astype(bf16),
        gate=contract_rows(saved["mlp_in"], grad_gate).astype(bf16),
    )
    out_shapes = dict(
        first_grad=((rows, share_width), bf16), result=((rows, share_width), bf16),
        gains=((16, share_width), f32),
    )
    ends = end_of_backward(operands, ("down_a", "up", "down_b", "gate"), out_shapes, 10)
    first_grad, result, gains = ends["first_grad"], ends["result"], ends["gains"]
    up, gate, pre, out = (ends["own_" + name].astype(f32) for name in ("up", "gate", "pre", "out"))
    down = jnp.concatenate([ends["own_down_a"], ends["own_down_b"]], axis=0).astype(f32)
    boundary = jnp.where(section == 0, first_grad, result)
    return (
        boundary.reshape(1, micro_count, block_rows, share_width),
        gains[0][None],
        pre[:, :256][None],
        pre[:, 256:320][None],
        pre[:, 320:][None],
        out[None],
        gains[8][None],
        gate[None],
        up[None],
        down[None],
    )


def solution(mesh):
    return jax.shard_map(
        per_device,
        mesh=mesh,
        in_specs=(
            P(None, "ctx", "wt"),
            P(None, "ctx", "wt"),
            P(),
            P("section", None),
            P("section", None, "wt"),
            P("section", None, "wt"),
            P("section", None, "wt"),
            P("section", "wt", None),
            P("section", None),
            P("section", None, "wt"),
            P("section", None, "wt"),
            P("section", "wt", None),
        ),
        out_specs=(
            P("section", None, "ctx", "wt"),
            P("section", "ctx"),
            P("section", "ctx", "wt"),
            P("section", "ctx", "wt"),
            P("section", "ctx", "wt"),
            P("section", "wt", "ctx"),
            P("section", "ctx"),
            P("section", "ctx", "wt"),
            P("section", "ctx", "wt"),
            P("section", "wt", "ctx"),
        ),
        check_vma=False,
    )
```

```python
import functools
from types import SimpleNamespace

import jax
import jax.numpy as jnp
from jax import lax
from jax.experimental import pallas as pl
from jax.experimental.pallas import tpu as pltpu
from jax.sharding import PartitionSpec as P

HD = 64
eps = 1e-05
theta = 500000.0
neg_big = -1e30
MESH = pl.DeviceIdType.MESH
f32 = jnp.float32
bf16 = jnp.bfloat16
MiB = 1024 * 1024


def rope_freqs(head_width):
    index_steps = jnp.arange(head_width // 2, dtype=jnp.float32)
    inverse = theta ** (-2.0 * index_steps / head_width)
    wavelen = 2.0 * jnp.pi / inverse
    smooth = (8192.0 / wavelen - 1.0) / 3.0
    blended = (1.0 - smooth) * inverse / 32.0 + smooth * inverse
    return jnp.where(
        wavelen < 2048.0, inverse, jnp.where(wavelen > 8192.0, inverse / 32.0, blended)
    )


def doc_begins(bounds, places):
    starts = jnp.concatenate([jnp.zeros((1,), jnp.int32), bounds])
    started = places[:, None] >= starts[None, :]
    return jnp.max(jnp.where(started, starts[None, :], 0), axis=1)


def contract_rows(left, right):
    return lax.dot_general(
        left, right, (((0,), (0,)), ((), ())), preferred_element_type=jnp.float32
    )


def times_transposed(left, right):
    return lax.dot_general(
        left, right, (((1,), (1,)), ((), ())), preferred_element_type=jnp.float32
    )


def greet(peers):
    barrier = pltpu.get_barrier_semaphore()
    for peer in peers:
        pl.semaphore_signal(barrier, inc=1, device_id=peer, device_id_type=MESH)
    pl.semaphore_wait(barrier, len(peers))


def remote(src, dst, send, recv, peer):
    return pltpu.make_async_remote_copy(
        src_ref=src, dst_ref=dst, send_sem=send, recv_sem=recv, device_id=peer,
        device_id_type=MESH,
    )


class WtPlace:
    def __init__(self, width):
        self.me = lax.axis_index("wt")
        self.z = self.me // 2
        self.core = self.me % 2
        self.sib = self.me + 1 - 2 * self.core
        self.width = width

    def peer(self, k):
        return lax.rem(self.z + k + 4, 4) * 2 + self.core

    def cols(self, index):
        return pl.ds(pl.multiple_of(index * self.width, self.width), self.width)


def way(chunk):
    return 1 if chunk % 2 == 0 else -1


class Gather:
    def __init__(self, place, out, sems, chunk, rows):
        self.place, self.out, self.chunk, self.rows = place, out, chunk, rows
        self.send, self.recv, self.fsend, self.frecv, self.local = sems
        self.s = way(chunk)

    def piece(self, index):
        return self.out.at[self.rows, self.place.cols(index)]

    def aside(self, k):
        p, q = self.place, self.chunk
        got = self.piece(p.peer(-k))
        return remote(got, got, self.fsend.at[q, k % 4], self.frecv.at[q, k % 4], {"wt": p.sib})

    def start(self, src):
        p, q = self.place, self.chunk
        mine = self.piece(p.me)
        self.own = pltpu.make_async_copy(src, mine, self.local.at[q])
        self.sent = []
        for hop in (self.s, -self.s):
            k = hop % 4
            copy = remote(
                src, mine, self.send.at[q, k], self.recv.at[q, k], {"wt": p.peer(hop)}
            )
            copy.start()
            self.sent.append(copy)
        copy = remote(src, mine, self.fsend.at[q, 0], self.frecv.at[q, 0], {"wt": p.sib})
        copy.start()
        self.sent.append(copy)
        self.own.start()

    def forward(self):
        p, q, s = self.place, self.chunk, self.s
        self.passed = []
        self.sent[0].wait_recv()
        got = self.piece(p.peer(-s))
        copy = remote(got, got, self.send.at[q, 2], self.recv.at[q, 2], {"wt": p.peer(s)})
        copy.start()
        self.sent.append(copy)
        near = self.aside(s)
        near.start()
        self.passed.append(near)

    def forward_more(self):
        s = self.s
        self.sent[1].wait_recv()
        near = self.aside(-s)
        near.start()
        self.passed.append(near)
        self.sent[3].wait_recv()
        near = self.aside(2)
        near.start()
        self.passed.append(near)

    def finish(self):
        for copy in self.passed:
            copy.wait()
        self.sent[2].wait_recv()
        for copy in self.sent:
            copy.wait_send()
        self.own.wait()


def gather_all(gathers):
    for one in gathers:
        one.forward()
    for one in gathers:
        one.forward_more()
    for one in gathers:
        one.finish()


def gather_scratch(chunks):
    return [pltpu.SemaphoreType.DMA((chunks, 4)) for _ in range(4)] + [
        pltpu.SemaphoreType.DMA((chunks,))
    ]


def greet_wt(place, more=()):
    greet([{"wt": place.sib}] + [{"wt": place.peer(k)} for k in (1, -1)] + list(more))


def gather_kernel(chunks, x, out, *sems):
    place = WtPlace(x.shape[1])
    greet_wt(place)
    rows = x.shape[0] // chunks
    parts = []
    for q in range(chunks):
        chunk_rows = pl.ds(q * rows, rows)
        part = Gather(place, out, sems, q, chunk_rows)
        part.start(x.at[chunk_rows])
        parts.append(part)
    gather_all(parts)


def wt_gather(x, collective_id, chunks=4):
    rows, width = x.shape
    return pl.pallas_call(
        functools.partial(gather_kernel, chunks),
        out_shape=jax.ShapeDtypeStruct((rows, 8 * width), x.dtype),
        in_specs=[pl.BlockSpec(memory_space=pltpu.VMEM)],
        out_specs=pl.BlockSpec(memory_space=pl.ANY),
        scratch_shapes=gather_scratch(chunks),
        compiler_params=pltpu.CompilerParams(
            collective_id=collective_id, has_side_effects=True, vmem_limit_bytes=4 * MiB
        ),
        name="gather_wt",
    )(x)


class Reduce:
    def __init__(self, place, part, bufs, chunk, rows):
        self.place, self.part, self.chunk, self.rows = place, part, chunk, rows
        (self.pair, self.out, self.landed, self.s1, self.r1, self.s2, self.r2) = bufs
        self.s = way(chunk)

    def start(self):
        p, q, s = self.place, self.chunk, self.s
        self.first = {}
        for k in (2, -s, s, 0):
            target = lax.rem(p.z + k + 4, 4) * 2 + 1 - p.core
            copy = remote(
                self.part.at[self.rows, p.cols(target)], self.pair.at[q, k % 4],
                self.s1.at[q, k % 4], self.r1.at[q, k % 4], {"wt": p.sib},
            )
            copy.start()
            self.first[k] = copy

    def both(self, k):
        p, q = self.place, self.chunk
        self.first[k].wait_recv()
        own = self.part[self.rows, p.cols(p.peer(k))]
        return own.astype(f32) + self.pair[q, k % 4].astype(f32)

    def onward(self, k, value, hop):
        p, q = self.place, self.chunk
        self.out[q, k % 4] = value.astype(bf16)
        copy = remote(
            self.out.at[q, k % 4], self.landed.at[q, k % 4], self.s2.at[q, k % 4],
            self.r2.at[q, k % 4], {"wt": p.peer(hop)},
        )
        copy.start()
        self.second[k] = copy

    def pass_on(self):
        self.second = {}
        self.onward(2, self.both(2), self.s)
        self.onward(-self.s, self.both(-self.s), -self.s)

    def pass_more(self):
        q, s = self.chunk, self.s
        value = self.both(s)
        self.second[2].wait_recv()
        self.onward(s, value + self.landed[q, 2].astype(f32), s)

    def total(self):
        q = self.chunk
        total = self.both(0)
        for k in (-self.s, self.s):
            self.second[k].wait_recv()
            total = total + self.landed[q, k % 4].astype(f32)
        return total

    def finish(self):
        for copy in self.first.values():
            copy.wait_send()
        for copy in self.second.values():
            copy.wait_send()


def sum_in_turn(sums, use):
    for one in sums:
        one.start()
    for one in sums:
        one.pass_on()
    for one in sums:
        one.pass_more()
    for q in range(len(sums)):
        use(q)


def reduce_scratch(chunks, rows, width):
    return [pltpu.VMEM((chunks, 4, rows, width), bf16) for _ in range(3)] + [
        pltpu.SemaphoreType.DMA((chunks, 4)) for _ in range(4)
    ]


def column(line, blocks):
    eye = lax.broadcasted_iota(jnp.int32, (128, 128), 0) == lax.broadcasted_iota(
        jnp.int32, (128, 128), 1
    )
    parts = [
        jnp.sum(
            jnp.where(eye, jnp.broadcast_to(line[j : j + 1, :], (128, 128)), 0.0),
            axis=1, keepdims=True,
        )
        for j in range(blocks)
    ]
    return jnp.concatenate(parts, axis=0)


def swap_sections(src, dst, send, recv):
    return remote(src, dst, send, recv, {"section": 1 - lax.axis_index("section")})


def forward_mid_kernel(chunks, part, skip, mid, whole, agsrc, *scratch):
    bufs, sems = scratch[:7], scratch[7:]
    place = WtPlace(skip.shape[1])
    greet_wt(place)
    rows = skip.shape[0] // chunks
    spans = [pl.ds(q * rows, rows) for q in range(chunks)]
    sums = [Reduce(place, part, bufs, q, spans[q]) for q in range(chunks)]
    gathers = [Gather(place, whole, sems, q, spans[q]) for q in range(chunks)]

    def use(q):
        value = skip[spans[q], :].astype(f32) + sums[q].total()
        mid[spans[q], :] = value
        agsrc[spans[q], :] = value.astype(bf16)
        gathers[q].start(agsrc.at[spans[q]])

    sum_in_turn(sums, use)
    gather_all(gathers)
    for one in sums:
        one.finish()


def forward_mid(part, skip, collective_id, chunks=4):
    rows, width = skip.shape
    return pl.pallas_call(
        functools.partial(forward_mid_kernel, chunks),
        out_shape=(
            jax.ShapeDtypeStruct((rows, width), f32),
            jax.ShapeDtypeStruct((rows, 8 * width), bf16),
        ),
        in_specs=[pl.BlockSpec(memory_space=pltpu.VMEM)] * 2,
        out_specs=(
            pl.BlockSpec(memory_space=pltpu.VMEM),
            pl.BlockSpec(memory_space=pl.ANY),
        ),
        scratch_shapes=[pltpu.VMEM((rows, width), bf16)]
        + reduce_scratch(chunks, rows // chunks, width)
        + gather_scratch(chunks),
        compiler_params=pltpu.CompilerParams(
            collective_id=collective_id, has_side_effects=True, vmem_limit_bytes=10 * MiB
        ),
        name="sum_mid_gather",
    )(part, skip)


def forward_pass_kernel(
    chunks, part, mid, begin, share, whole, agsrc, arrived, xsend, xrecv, *scratch
):
    bufs, sems = scratch[:7], scratch[7:]
    place = WtPlace(mid.shape[1])
    section = lax.axis_index("section")
    greet_wt(place, [{"section": 1 - section}])
    rows = mid.shape[0] // chunks
    spans = [pl.ds(q * rows, rows) for q in range(chunks)]
    sums = [Reduce(place, part, bufs, q, spans[q]) for q in range(chunks)]
    gathers = [Gather(place, whole, sems, q, spans[q]) for q in range(chunks)]
    swaps = []

    def use(q):
        agsrc[spans[q], :] = (mid[spans[q], :] + sums[q].total()).astype(bf16)
        swap = swap_sections(
            agsrc.at[spans[q]], arrived.at[spans[q]], xsend.at[q], xrecv.at[q]
        )
        swap.start()
        swaps.append(swap)

    sum_in_turn(sums, use)
    for q in range(chunks):
        swaps[q].wait_recv()
        share[spans[q], :] = jnp.where(
            section == 0, begin[spans[q], :].astype(f32), arrived[spans[q], :].astype(f32)
        ).astype(bf16)
        gathers[q].start(share.at[spans[q]])
    gather_all(gathers)
    for one in sums:
        one.finish()
    for one in swaps:
        one.wait_send()


def forward_pass(part, mid, begin, collective_id, chunks=4):
    rows, width = mid.shape
    return pl.pallas_call(
        functools.partial(forward_pass_kernel, chunks),
        out_shape=(
            jax.ShapeDtypeStruct((rows, width), bf16),
            jax.ShapeDtypeStruct((rows, 8 * width), bf16),
        ),
        in_specs=[pl.BlockSpec(memory_space=pltpu.VMEM)] * 3,
        out_specs=(
            pl.BlockSpec(memory_space=pltpu.VMEM),
            pl.BlockSpec(memory_space=pl.ANY),
        ),
        scratch_shapes=[
            pltpu.VMEM((rows, width), bf16),
            pltpu.VMEM((rows, width), bf16),
            pltpu.SemaphoreType.DMA((chunks,)),
            pltpu.SemaphoreType.DMA((chunks,)),
        ]
        + reduce_scratch(chunks, rows // chunks, width)
        + gather_scratch(chunks),
        compiler_params=pltpu.CompilerParams(
            collective_id=collective_id, has_side_effects=True, vmem_limit_bytes=10 * MiB
        ),
        name="sum_pass_gather",
    )(part, mid, begin)


def add_up(dst, sources, step=64):
    def some(i, carry):
        span = pl.ds(pl.multiple_of(i * step, step), step)
        total = sources[0][span, :].astype(f32)
        for source in sources[1:]:
            total = total + source[span, :].astype(f32)
        dst[span, :] = total.astype(dst.dtype)
        return carry

    lax.fori_loop(0, dst.shape[0] // step, some, 0)


class CtxPlace:
    def __init__(self):
        self.me = lax.axis_index("ctx")
        self.x = self.me // 2
        self.y = self.me % 2

    def at(self, k, y):
        return lax.rem(self.x + k + 4, 4) * 2 + y

    def x_peer(self, hop):
        return {"ctx": self.at(hop, self.y)}

    def y_peer(self):
        return {"ctx": self.at(0, 1 - self.y)}

    def near(self):
        return [self.x_peer(1), self.x_peer(-1), self.y_peer()]

    def all(self):
        return [{"ctx": lax.rem(self.me + d, 8)} for d in range(1, 8)]


class XRing:
    def __init__(self, place, s, loaded, bufs, sems):
        self.place, self.s, self.loaded = place, s, loaded
        self.via, self.near, self.joined, self.summed = bufs
        self.send, self.recv = sems
        self.copies = {}

    def go(self, i, src, dst, hop):
        copy = remote(src, dst, self.send.at[i], self.recv.at[i], self.place.x_peer(hop))
        copy.start()
        self.copies[i] = copy

    def start(self, k):
        if k == 2:
            self.go(0, self.loaded(2), self.via, self.s)
        elif k == -self.s:
            self.go(1, self.loaded(k), self.near, k)

    def join(self):
        self.copies[0].wait_recv()
        add_up(self.summed, [self.loaded(self.s), self.via])
        self.go(2, self.summed, self.joined, self.s)

    def total(self, dst):
        self.copies[1].wait_recv()
        self.copies[2].wait_recv()
        add_up(dst, [self.loaded(0), self.near, self.joined])

    def finish(self):
        for copy in self.copies.values():
            copy.wait_send()


def cut(array, dim, owner):
    length = array.shape[dim] // 8
    span = pl.ds(pl.multiple_of(owner * length, length), length)
    return array.at[span] if dim == 0 else array.at[:, span]


BLOCKS = (2, -1, 1, 0)


class XFirst:
    def __init__(self, place, array, dim, out, scratch):
        self.place, self.out = place, out
        bufs, summed, self.swapped, sems, self.ssend, self.srecv, *held = scratch
        self.held, self.lsem = held if held else (None, None)

        def block(k, y):
            return cut(array, dim, place.at(k, y))

        def loaded(k, y):
            if held and k in (0, way(y)):
                return self.held.at[abs(k), y]
            return block(k, y)

        self.block = block
        self.rings = [
            XRing(
                place, way(y), lambda k, y=y: loaded(k, y),
                [bufs.at[y, j] for j in range(3)] + [summed.at[y]],
                [sems.at[0, y], sems.at[1, y]],
            )
            for y in (0, 1)
        ]

    def start(self):
        self.loads = []
        for y, ring in enumerate(self.rings):
            ring.start(2)
            ring.start(-ring.s)
        if self.held is not None:
            for y in (0, 1):
                for k in (way(y), 0):
                    copy = pltpu.make_async_copy(
                        self.block(k, y), self.held.at[abs(k), y], self.lsem.at[abs(k), y]
                    )
                    copy.start()
                    self.loads.append(copy)

    def join(self):
        for copy in self.loads:
            copy.wait()
        for ring in self.rings:
            ring.join()

    def swap(self):
        for y in (0, 1):
            self.rings[y].total(self.swapped.at[1 + y])
        self.across = remote(
            self.swapped.at[1 + (1 - self.place.y)], self.swapped.at[0], self.ssend.at[0],
            self.srecv.at[0], self.place.y_peer(),
        )
        self.across.start()

    def total(self):
        self.across.wait_recv()
        add_up(self.out, [self.swapped.at[1 + self.place.y], self.swapped.at[0]])

    def finish(self):
        for ring in self.rings:
            ring.finish()
        self.across.wait_send()


class YFirst:
    def __init__(self, place, array, dim, out, scratch):
        self.place, self.array, self.dim, self.out = place, array, dim, out
        (bufs, summed, self.swapped, sems, self.ssend, self.srecv, self.held, self.lsem) = scratch
        swapped = self.swapped
        self.half = half = self.held.shape[1] // 2
        self.rings = [
            XRing(
                place, way(h), lambda k, h=h: swapped.at[k % 4, pl.ds(h * half, half)],
                [bufs.at[h, j] for j in range(3)] + [summed.at[h]],
                [sems.at[0, h], sems.at[1, h]],
            )
            for h in (0, 1)
        ]

    def start(self):
        self.swaps, self.loads = {}, {}
        for k in BLOCKS:
            copy = remote(
                cut(self.array, self.dim, self.place.at(k, 1 - self.place.y)),
                self.swapped.at[k % 4], self.ssend.at[k % 4], self.srecv.at[k % 4],
                self.place.y_peer(),
            )
            copy.start()
            self.swaps[k] = copy
        for k in BLOCKS:
            copy = pltpu.make_async_copy(
                cut(self.array, self.dim, self.place.at(k, self.place.y)),
                self.held.at[k % 4], self.lsem.at[k % 4],
            )
            copy.start()
            self.loads[k] = copy

    def first(self):
        for k in BLOCKS:
            self.loads[k].wait()
            self.swaps[k].wait_recv()
            block = self.swapped.at[k % 4]
            add_up(block, [block, self.held.at[k % 4]])
            for ring in self.rings:
                ring.start(k)

    def join(self):
        for ring in self.rings:
            ring.join()

    def total(self):
        for h, ring in enumerate(self.rings):
            ring.total(self.out.at[pl.ds(h * self.half, self.half)])

    def finish(self):
        for ring in self.rings:
            ring.finish()
        for copy in self.swaps.values():
            copy.wait_send()


def owned(shape, dim):
    return tuple(n // 8 if i == dim else n for i, n in enumerate(shape))


def ctx_scratch(shape, dim, mode):
    rows, width = owned(shape, dim)
    ring = (rows // 2 if mode == "y" else rows, width)
    scratch = [
        pltpu.VMEM((2, 3, *ring), bf16),
        pltpu.VMEM((2, *ring), bf16),
        pltpu.VMEM((4 if mode == "y" else 3, rows, width), bf16),
        pltpu.SemaphoreType.DMA((2, 2, 3)),
        pltpu.SemaphoreType.DMA((4,)),
        pltpu.SemaphoreType.DMA((4,)),
    ]
    if mode == "y":
        scratch += [pltpu.VMEM((4, rows, width), bf16), pltpu.SemaphoreType.DMA((4,))]
    elif mode == "x":
        scratch += [pltpu.VMEM((2, 2, rows, width), bf16), pltpu.SemaphoreType.DMA((2, 2))]
    return scratch


def everyone(place):
    return [lax.rem(place.me + d, 8) for d in range(1, 8)]


class Lines:
    def __init__(self, place, line, slots, send, recv):
        self.line, self.slots = line, slots
        self.copies = [
            remote(line, slots.at[d], send.at[d], recv.at[d], {"wt": lax.rem(place.me + d, 8)})
            for d in range(1, 8)
        ]

    def start(self):
        for copy in self.copies:
            copy.start()

    def total(self):
        total = self.line[...]
        for d, copy in enumerate(self.copies, start=1):
            copy.wait_recv()
            total = total + self.slots[d]
        return total

    def finish(self):
        for copy in self.copies:
            copy.wait_send()


def norm_back(total, above, own, scale, gain, mean):
    normed = own * scale
    grad = above.astype(f32) + scale * (total * gain - normed * mean)
    return grad, jnp.sum(total * normed, axis=0, keepdims=True)


def backward_kernel(mode, chunks, part, line, above, own, factor, gain, *rest):
    if mode == "mid":
        share, whole, agsrc, *rest = rest
    else:
        begin, share, whole, agsrc, arrived, xsend, xrecv, *rest = rest
    slots, lsend, lrecv, *rest = rest
    bufs, sems = rest[:7], rest[7:]
    place = WtPlace(own.shape[1])
    section = lax.axis_index("section")
    greet(
        [{"wt": peer} for peer in everyone(place)]
        + ([{"section": 1 - section}] if mode == "pass" else [])
    )
    rows = own.shape[0] // chunks
    depth = 8 * own.shape[1]
    spans = [pl.ds(q * rows, rows) for q in range(chunks)]
    sums = [Reduce(place, part, bufs, q, spans[q]) for q in range(chunks)]
    gathers = [Gather(place, whole, sems, q, spans[q]) for q in range(chunks)]
    lines = Lines(place, line, slots, lsend, lrecv)
    lines.start()
    for one in sums:
        one.start()
    for one in sums:
        one.pass_on()
    for one in sums:
        one.pass_more()
    mean = column(lines.total(), own.shape[0] // 128) * (1.0 / depth)
    swaps = []
    for q in range(chunks):
        span = spans[q]
        grad, _ = norm_back(
            sums[q].total(), above[span, :], own[span, :], factor[span, :], gain[...],
            mean[q * rows : (q + 1) * rows],
        )
        agsrc[span, :] = grad.astype(bf16)
        if mode == "mid":
            share[span, :] = grad
            gathers[q].start(agsrc.at[span])
        else:
            swap = swap_sections(agsrc.at[span], arrived.at[span], xsend.at[q], xrecv.at[q])
            swap.start()
            swaps.append(swap)
    if mode == "pass":
        for q in range(chunks):
            span = spans[q]
            swaps[q].wait_recv()
            share[span, :] = jnp.where(
                section == 1, begin[span, :].astype(f32), arrived[span, :].astype(f32)
            ).astype(bf16)
            gathers[q].start(share.at[span])
    gather_all(gathers)
    for one in sums:
        one.finish()
    for one in swaps:
        one.wait_send()
    lines.finish()


def seven():
    return [pltpu.SemaphoreType.DMA((8,)), pltpu.SemaphoreType.DMA((8,))]


def backward_sum(mode, part, line, above, own, factor, gain, extra, collective_id, chunks=4):
    rows, width = own.shape
    vmem = pl.BlockSpec(memory_space=pltpu.VMEM)
    hbm = pl.BlockSpec(memory_space=pl.ANY)
    scratch = [pltpu.VMEM((rows, width), bf16)]
    if mode == "pass":
        scratch += [
            pltpu.VMEM((rows, width), bf16),
            pltpu.SemaphoreType.DMA((chunks,)),
            pltpu.SemaphoreType.DMA((chunks,)),
        ]
    scratch += [pltpu.VMEM((8, 8, 128), f32)] + seven()
    scratch += reduce_scratch(chunks, rows // chunks, width) + gather_scratch(chunks)
    operands = [part, line, above, own, factor, gain] + extra
    return pl.pallas_call(
        functools.partial(backward_kernel, mode, chunks),
        out_shape=(
            jax.ShapeDtypeStruct((rows, width), f32 if mode == "mid" else bf16),
            jax.ShapeDtypeStruct((rows, 8 * width), bf16),
        ),
        in_specs=[vmem] * len(operands),
        out_specs=(vmem, hbm),
        scratch_shapes=scratch,
        compiler_params=pltpu.CompilerParams(
            collective_id=collective_id, has_side_effects=True, vmem_limit_bytes=12 * MiB
        ),
        name="sum_back_" + mode,
    )(*operands)


def lanes(shape):
    return lax.broadcasted_iota(jnp.int32, shape, len(shape) - 1)


def turn(u, cosine, sine):
    low_half = jnp.bitwise_and(lanes(u.shape), HD - 1) < HD // 2
    turned = jnp.where(low_half, -pltpu.roll(u, 128 - HD // 2, 1), pltpu.roll(u, HD // 2, 1))
    return u * cosine + turned * sine


def turn_back(y, cosine, sine):
    low_half = jnp.bitwise_and(lanes(y.shape), HD - 1) < HD // 2
    z = y * sine
    turned = jnp.where(low_half, pltpu.roll(z, 128 - HD // 2, 1), -pltpu.roll(z, HD // 2, 1))
    return y * cosine + turned


def visible_keys(bounds, b, key_block, me, rows, heads):
    row = lax.broadcasted_iota(jnp.int32, (1, heads * rows), 1)
    for head in range(1, heads):
        row = row - jnp.where(lanes((1, heads * rows)) >= head * rows, rows, 0)
    place = me * rows + row
    first, second = bounds[b, 0], bounds[b, 1]
    begin = jnp.where(place >= second, second, jnp.where(place >= first, first, 0))
    key = key_block * rows + lax.broadcasted_iota(jnp.int32, (rows, 1), 0)
    return (key <= place) & (key >= begin)


def stack_queries(flat, cosine, sine, b, rows, stacked):
    span = pl.ds(b * rows, rows)
    low = lanes((rows, 128)) < HD
    for pair in range(2):
        u = turn(flat[span, 128 * pair : 128 * pair + 128], cosine[span, :], sine[span, :])
        u = u.astype(bf16).astype(f32) * (HD**-0.5)
        even = jnp.where(low, u, 0.0)
        odd = jnp.where(low, pltpu.roll(u, HD, 1), 0.0)
        stacked[b, pl.ds(2 * pair * rows, rows), :] = even.astype(bf16)
        stacked[b, pl.ds((2 * pair + 1) * rows, rows), :] = odd.astype(bf16)


def later(me, d, n):
    return me + d < n


def earlier(me, d, n):
    return me - d >= 0


def greet_order(me, n, side, count):
    barrier = pltpu.get_barrier_semaphore()
    step = 1 if side is later else n - 1
    for d in range(1, n):

        @pl.when(side(me, d, n))
        def _():
            pl.semaphore_signal(
                barrier, inc=1, device_id={"ctx": lax.rem(me + d * step, n)},
                device_id_type=MESH,
            )

    def wait():
        @pl.when(count > 0)
        def _():
            pl.semaphore_wait(barrier, count)

    return wait


def attention_kernel(
    n, bounds, flat, kv_pre, cosine, sine, kv_cosine, kv_sine, mix, logs, mixed, kv,
    stacked, acc, mine, send, recv
):
    me = lax.axis_index("ctx")
    rows = kv.shape[2]
    heads = 4
    wait = greet_order(me, n, earlier, n - 1 - me)
    for b in range(2):
        span = pl.ds(b * rows, rows)
        turned = turn(kv_pre[span, :], kv_cosine[span, :], kv_sine[span, :]).astype(bf16)
        mine[b] = turned
        kv[me, b] = turned
    wait()

    def copy(d):
        return remote(mine, kv.at[me], send.at[d], recv.at[d], {"ctx": lax.rem(me + d, n)})

    for d in reversed(range(1, n)):

        @pl.when(later(me, d, n))
        def _():
            copy(d).start()

    for b in range(2):
        stack_queries(flat, cosine, sine, b, rows, stacked)
    acc[...] = jnp.zeros_like(acc)

    def block(j, carry):
        after = []
        for b in range(2):
            peak, total = carry[2 * b : 2 * b + 2]
            keys = kv[j, b]
            scores = times_transposed(keys, stacked[b])
            scores = jnp.where(visible_keys(bounds, b, j, me, rows, heads), scores, neg_big)
            new_peak = jnp.maximum(peak, jnp.max(scores, axis=0, keepdims=True))
            shrink = jnp.exp(peak - new_peak)
            weight = jnp.exp(scores - new_peak)
            total = total * shrink + jnp.sum(weight, axis=0, keepdims=True)
            acc[b] = acc[b] * shrink + contract_rows(keys, weight.astype(bf16))
            after += [new_peak, total]
        return tuple(after)

    def arrived(d, carry):
        copy(d).wait_recv()
        return block(me - d, carry)

    zero = jnp.zeros((1, heads * rows), f32)
    done = block(me, (zero + neg_big, zero) * 2)
    done = lax.fori_loop(1, me + 1, arrived, done)
    low = lanes((rows, 128)) < HD
    for b in range(2):
        peak, total = done[2 * b : 2 * b + 2]
        out = acc[b] / total
        mixed[b] = out
        logs[b] = peak + jnp.log(total)
        upright = out.T
        for pair in range(2):
            even = upright[2 * pair * rows : (2 * pair + 1) * rows]
            odd = upright[(2 * pair + 1) * rows : (2 * pair + 2) * rows]
            both = jnp.where(low, pltpu.roll(even, HD, 1), odd)
            mix[pl.ds(b * rows, rows), 128 * pair : 128 * pair + 128] = both.astype(bf16)
    for d in range(1, n):

        @pl.when(later(me, d, n))
        def _():
            copy(d).wait_send()


def attention(bounds, flat, kv_pre, cosine, sine, kv_cosine, kv_sine, collective_id):
    n = 8
    rows = flat.shape[0] // 2
    vmem = pl.BlockSpec(memory_space=pltpu.VMEM)
    return pl.pallas_call(
        functools.partial(attention_kernel, n),
        out_shape=(
            jax.ShapeDtypeStruct((2 * rows, 256), bf16),
            jax.ShapeDtypeStruct((2, 1, 4 * rows), f32),
            jax.ShapeDtypeStruct((2, 128, 4 * rows), f32),
            jax.ShapeDtypeStruct((n, 2, rows, 128), bf16),
        ),
        in_specs=[pl.BlockSpec(memory_space=pltpu.SMEM)] + [vmem] * 6,
        out_specs=(vmem,) * 4,
        scratch_shapes=[
            pltpu.VMEM((2, 4 * rows, 128), bf16),
            pltpu.VMEM((2, 128, 4 * rows), f32),
            pltpu.VMEM((2, rows, 128), bf16),
            pltpu.SemaphoreType.DMA((n,)),
            pltpu.SemaphoreType.DMA((n,)),
        ],
        compiler_params=pltpu.CompilerParams(
            collective_id=collective_id, has_side_effects=True, vmem_limit_bytes=20 * MiB
        ),
        name="attention",
    )(bounds, flat, kv_pre, cosine, sine, kv_cosine, kv_sine)


def attention_back_kernel(n, *refs):
    me = lax.axis_index("ctx")
    attention_back_steps(n, me, greet_order(me, n, later, me), *refs)


def attention_back_steps(
    n, me, wait, bounds, flat, cosine, sine, kv_cosine, kv_sine, kv, logs, mixed, grad, out,
    grad_kv, terms, slots, total, stacked, grads, acc, send, recv
):
    rows = kv.shape[2]
    heads = 4
    low = lanes((rows, 128)) < HD
    deltas = []
    for b in range(2):
        stack_queries(flat, cosine, sine, b, rows, stacked)
        for pair in range(2):
            u = grad[pl.ds(b * rows, rows), 128 * pair : 128 * pair + 128].astype(f32)
            even = jnp.where(low, 0.0, pltpu.roll(u, HD, 1))
            odd = jnp.where(low, 0.0, u)
            grads[b, pl.ds(2 * pair * rows, rows), :] = even.astype(bf16)
            grads[b, pl.ds((2 * pair + 1) * rows, rows), :] = odd.astype(bf16)
        deltas.append(
            jnp.sum(mixed[b] * grads[b].astype(f32).T, axis=0, keepdims=True)
        )
    acc[...] = jnp.zeros_like(acc)
    wait()

    def block(j):
        for b in range(2):
            keys = kv[j, b]
            scores = times_transposed(keys, stacked[b])
            probs = jnp.where(
                visible_keys(bounds, b, j, me, rows, heads), jnp.exp(scores - logs[b]), 0.0
            )
            grad_probs = times_transposed(keys, grads[b])
            grad_scores = (probs * (grad_probs - deltas[b])).astype(bf16)
            acc[b] += contract_rows(keys, grad_scores)
            terms[j, b] = (
                jnp.dot(grad_scores, stacked[b], preferred_element_type=f32)
                + jnp.dot(probs.astype(bf16), grads[b], preferred_element_type=f32)
            ).astype(bf16)

    def copy(d):
        back = lax.rem(me + n - d, n)
        return remote(terms.at[back], slots.at[d], send.at[d], recv.at[d], {"ctx": back})

    def block_sent(j, carry):
        block(j)
        copy(me - j).start()
        return carry

    lax.fori_loop(0, me, block_sent, 0)
    block(me)
    for b in range(2):
        span = pl.ds(b * rows, rows)
        upright = acc[b].T * (HD**-0.5)
        for pair in range(2):
            even = upright[2 * pair * rows : (2 * pair + 1) * rows]
            odd = upright[(2 * pair + 1) * rows : (2 * pair + 2) * rows]
            both = jnp.where(low, even, pltpu.roll(odd, HD, 1))
            out[span, 128 * pair : 128 * pair + 128] = turn_back(
                both, cosine[span, :], sine[span, :]
            ).astype(bf16)
    for b in range(2):
        total[b] = terms[me, b].astype(f32)
    for d in range(1, n):

        @pl.when(later(me, d, n))
        def _():
            copy(d).wait_recv()
            total[...] += slots[d].astype(f32)

    for b in range(2):
        span = pl.ds(b * rows, rows)
        grad_kv[span, :] = turn_back(
            total[b], kv_cosine[span, :], kv_sine[span, :]
        ).astype(bf16)
    for d in range(1, n):

        @pl.when(earlier(me, d, n))
        def _():
            copy(d).wait_send()


def attention_back_scratch(shape):
    n, two, rows, width = shape
    return [
        pltpu.VMEM(shape, bf16),
        pltpu.VMEM(shape, bf16),
        pltpu.VMEM((2, rows, width), f32),
        pltpu.VMEM((2, 4 * rows, 128), bf16),
        pltpu.VMEM((2, 4 * rows, 128), bf16),
        pltpu.VMEM((2, 128, 4 * rows), f32),
        pltpu.SemaphoreType.DMA((n,)),
        pltpu.SemaphoreType.DMA((n,)),
    ]


def attention_back(
    bounds, flat, cosine, sine, kv_cosine, kv_sine, kv, logs, mixed, grad, collective_id
):
    n, two, rows, width = kv.shape
    vmem = pl.BlockSpec(memory_space=pltpu.VMEM)
    return pl.pallas_call(
        functools.partial(attention_back_kernel, n),
        out_shape=(
            jax.ShapeDtypeStruct((2 * rows, 256), bf16),
            jax.ShapeDtypeStruct((2 * rows, 128), bf16),
        ),
        in_specs=[pl.BlockSpec(memory_space=pltpu.SMEM)] + [vmem] * 9,
        out_specs=(vmem, vmem),
        scratch_shapes=attention_back_scratch(kv.shape),
        compiler_params=pltpu.CompilerParams(
            collective_id=collective_id, has_side_effects=True, vmem_limit_bytes=24 * MiB
        ),
        name="attention_back",
    )(bounds, flat, cosine, sine, kv_cosine, kv_sine, kv, logs, mixed, grad)


def as_line(column_values, line):
    eye = lax.broadcasted_iota(jnp.int32, (128, 128), 0) == lax.broadcasted_iota(
        jnp.int32, (128, 128), 1
    )
    line[...] = jnp.zeros_like(line)
    for j in range(column_values.shape[0] // 128):
        block = column_values[128 * j : 128 * j + 128]
        line[j : j + 1, :] = jnp.sum(
            jnp.where(eye, jnp.broadcast_to(block, (128, 128)), 0.0), axis=0, keepdims=True
        )


CTX_DIMS = dict(down_a=1, up=0, down_b=1, gate=0, pre=0, out=1)
CTX_MODES = dict(down_a="x", up="x", down_b="y", gate="y", pre="local", out="local")


class Call:
    def __init__(self, chunks, names, ctx_names, refs):
        given, at = {}, 0
        for name, count in names:
            given[name] = refs[at] if count == 1 else refs[at : at + count]
            at += count
        self.r = SimpleNamespace(**given)
        self.place, self.ctx = WtPlace(given["gain"].shape[1]), CtxPlace()
        greet([{"wt": peer} for peer in everyone(self.place)] + self.ctx.all())
        self.width = self.place.width
        self.all_rows = given["factor"].shape[0]
        self.rows = self.all_rows // chunks
        self.spans = [pl.ds(q * self.rows, self.rows) for q in range(chunks)]
        self.blocks = [pl.ds(self.width * c, self.width) for c in range(8)]
        self.beside = [
            (YFirst if CTX_MODES[name] == "y" else XFirst)(
                self.ctx, given[name], CTX_DIMS[name], given["own_" + name],
                given["sum_" + name],
            )
            for name in ctx_names
        ]

    def sums(self, part, bufs):
        return [Reduce(self.place, part, bufs, q, span) for q, span in enumerate(self.spans)]

    def behind_norm(self, sums, lines, above, own, use):
        r = self.r
        mean = column(lines.total(), self.all_rows // 128) * (1.0 / (8 * self.width))
        terms = jnp.zeros((1, self.width), f32)
        for q, span in enumerate(self.spans):
            grad, term = norm_back(
                sums[q].total(), above[span, :], own[span, :], r.factor[span, :], r.gain[...],
                mean[q * self.rows : (q + 1) * self.rows],
            )
            terms = terms + term
            use(q, span, grad)
        return jnp.broadcast_to(terms, (8, self.width))


def middle_kernel(n, chunks, names, ctx_names, *refs):
    call = Call(chunks, names, ctx_names, refs)
    r, place, ctx = call.r, call.place, call.ctx
    down_a, down_b = call.beside
    sums = call.sums(r.part, r.reduce)
    gathers = [
        Gather(place, r.whole, r.gather, q, span) for q, span in enumerate(call.spans)
    ]
    lines = Lines(place, r.line, *r.slots)
    lines.start()
    for one in sums:
        one.start()
    for one in call.beside:
        one.start()
    for one in sums:
        one.pass_on()
    for one in sums:
        one.pass_more()

    def use(q, span, grad):
        r.grad_mid[span, :] = grad
        r.agsrc[span, :] = grad.astype(bf16)
        gathers[q].start(r.agsrc.at[span])

    r.piece[...] = call.behind_norm(sums, lines, r.above, r.mid, use)
    for one in gathers:
        one.forward()
    for one in gathers:
        one.forward_more()
    down_a.join()
    for one in gathers:
        one.finish()
    r.grad_mix[...] = times_transposed(r.whole[...], r.w_out[...]).astype(bf16)
    down_b.first()
    attention_back_steps(
        n, ctx.me, lambda: None, r.bounds, r.flat, r.cosine, r.sine, r.kv_cosine, r.kv_sine,
        r.kv, r.logs, r.mixed, r.grad_mix, r.grad_pre.at[:, pl.ds(0, 256)],
        r.grad_pre.at[:, pl.ds(256, 128)], *r.attention
    )
    down_b.join()
    down_a.swap()
    down_b.total()
    down_a.total()
    for one in sums + call.beside:
        one.finish()
    lines.finish()


def last_kernel(n, chunks, names, ctx_names, *refs):
    call = Call(chunks, names, ctx_names, refs)
    r, place, ctx = call.r, call.place, call.ctx
    up, gate, pre, out = call.beside
    grad_pre = r.grad_pre
    up.start()
    gate.start()
    dots = jnp.zeros((call.all_rows, 1), f32)
    for block in call.blocks:
        partial_sum = times_transposed(grad_pre[...], r.w_qkv[block, :])
        dots = dots + jnp.sum(
            partial_sum * r.attn_in[:, block].astype(f32), axis=1, keepdims=True
        )
        r.part[:, block] = partial_sum.astype(bf16)
    as_line(dots, r.line)
    lines = Lines(place, r.line, *r.slots)
    lines.start()
    sums = call.sums(r.part, r.reduce)
    last_sums = call.sums(r.last_part, r.last_reduce)
    for one in sums:
        one.start()
    for one in sums:
        one.pass_on()
    for block in call.blocks:
        r.pre[block, :] = contract_rows(r.attn_in[:, block], grad_pre[...]).astype(bf16)
    pre.start()
    for one in sums:
        one.pass_more()
    for one in last_sums:
        one.start()
    for block in call.blocks:
        r.out[:, block] = contract_rows(r.mix[...], r.whole[:, block]).astype(bf16)
    out.start()
    for one in last_sums:
        one.pass_on()

    def use(q, span, grad):
        r.first_grad[span, :] = grad.astype(bf16)

    r.both_pieces[0:8, :] = call.behind_norm(sums, lines, r.grad_mid, r.hidden, use)
    r.both_pieces[8:16, :] = r.piece[...]
    piece, pieces = r.both_pieces, r.pieces
    gsend, grecv = r.piece_sems
    piece_copies = [
        remote(
            piece, pieces.at[place.me], gsend.at[d], grecv.at[d],
            {"wt": lax.rem(place.me + d, 8)},
        )
        for d in range(1, 8)
    ]
    for copy in piece_copies:
        copy.start()
    for one in last_sums:
        one.pass_more()
    pieces[place.me] = piece[...]
    for copy in piece_copies:
        copy.wait()
    osend, orecv = r.owner_sems
    owner_copies = []
    for d in range(1, 8):
        owner = lax.rem(ctx.me + d, 8)
        copy = remote(
            pieces.at[owner], r.gain_slots.at[d], osend.at[d], orecv.at[d], {"ctx": owner}
        )
        copy.start()
        owner_copies.append(copy)
    up.join()
    pre.join()
    out.join()
    for q, span in enumerate(call.spans):
        r.result[span, :] = (r.last_mid[span, :] + last_sums[q].total()).astype(bf16)
    total = pieces[ctx.me]
    for d, copy in enumerate(owner_copies, start=1):
        copy.wait_recv()
        total = total + r.gain_slots[d]
    r.gains[...] = total
    up.swap()
    gate.first()
    pre.swap()
    out.swap()
    gate.join()
    up.total()
    pre.total()
    out.total()
    gate.total()
    for one in sums + last_sums + call.beside:
        one.finish()
    for copy in owner_copies:
        copy.wait_send()
    lines.finish()


def call_with_ctx(
    kernel, operands, outs, scratch, ctx_shapes, hbm_names, collective_id, vmem_mib, name,
    chunks=4
):
    vmem = pl.BlockSpec(memory_space=pltpu.VMEM)
    kinds = {one: pl.BlockSpec(memory_space=pl.ANY) for one in hbm_names}
    kinds["bounds"] = pl.BlockSpec(memory_space=pltpu.SMEM)
    outs, scratch = dict(outs), dict(scratch)
    for one, shape in ctx_shapes.items():
        outs["own_" + one] = (owned(shape, CTX_DIMS[one]), bf16)
        scratch["sum_" + one] = ctx_scratch(shape, CTX_DIMS[one], CTX_MODES[one])
    names = (
        [(one, 1) for one in operands] + [(one, 1) for one in outs]
        + [(one, len(specs)) for one, specs in scratch.items()]
    )
    results = pl.pallas_call(
        functools.partial(kernel, 8, chunks, names, tuple(ctx_shapes)),
        out_shape=tuple(jax.ShapeDtypeStruct(*one) for one in outs.values()),
        in_specs=[kinds.get(one, vmem) for one in operands],
        out_specs=(vmem,) * len(outs),
        scratch_shapes=[spec for specs in scratch.values() for spec in specs],
        compiler_params=pltpu.CompilerParams(
            collective_id=collective_id, has_side_effects=True,
            vmem_limit_bytes=vmem_mib * MiB,
        ),
        name=name,
    )(*operands.values())
    return SimpleNamespace(**dict(zip(outs, results)))


def middle_of_backward(operands, collective_id, chunks=4):
    rows, width = operands["mid"].shape
    shape = operands["down_a"].shape
    return call_with_ctx(
        middle_kernel, operands,
        dict(
            grad_mid=((rows, width), f32), piece=((8, width), f32),
            whole=((rows, 8 * width), bf16), grad_pre=((rows, 384), bf16),
        ),
        dict(
            agsrc=[pltpu.VMEM((rows, width), bf16)],
            grad_mix=[pltpu.VMEM((rows, width), bf16)],
            slots=[pltpu.VMEM((8, 8, 128), f32)] + seven(),
            reduce=reduce_scratch(chunks, rows // chunks, width),
            gather=gather_scratch(chunks),
            attention=attention_back_scratch(operands["kv"].shape),
        ),
        dict(down_a=shape, down_b=shape), ("down_a", "down_b"), collective_id, 30,
        "middle_of_backward", chunks,
    )


def end_of_backward(operands, collective_id, chunks=4):
    rows, width = operands["grad_mid"].shape
    wide = operands["up"].shape
    pre, out = (8 * width, 384), (width, 8 * width)
    reduce = reduce_scratch(chunks, rows // chunks, width)
    return call_with_ctx(
        last_kernel, operands,
        dict(
            first_grad=((rows, width), bf16), result=((rows, width), bf16),
            gains=((16, width), f32),
        ),
        dict(
            part=[pltpu.VMEM((rows, 8 * width), bf16)],
            pre=[pltpu.VMEM(pre, bf16)],
            out=[pltpu.VMEM(out, bf16)],
            line=[pltpu.VMEM((8, 128), f32)],
            both_pieces=[pltpu.VMEM((16, width), f32)],
            pieces=[pltpu.VMEM((8, 16, width), f32)],
            gain_slots=[pltpu.VMEM((8, 16, width), f32)],
            piece_sems=seven(),
            owner_sems=seven(),
            slots=[pltpu.VMEM((8, 8, 128), f32)] + seven(),
            reduce=reduce,
            last_reduce=reduce,
        ),
        dict(up=wide, gate=wide, pre=pre, out=out), ("up", "gate"), collective_id, 48,
        "end_of_backward", chunks,
    )


def per_device(
    inputs,
    cotangent,
    doc_bounds,
    attn_gain,
    w_query,
    w_key,
    w_value,
    w_out,
    mlp_gain,
    w_gate,
    w_up,
    w_down,
):
    ctx_rank = lax.axis_index("ctx")
    wt_rank = lax.axis_index("wt")
    micro_count, block_rows, share_width = inputs.shape
    rows = micro_count * block_rows
    gain_attn = attn_gain.astype(f32)
    gain_mlp = mlp_gain.astype(f32)
    own_gain_attn = lax.dynamic_slice_in_dim(gain_attn, wt_rank * share_width, share_width, 1)
    own_gain_mlp = lax.dynamic_slice_in_dim(gain_mlp, wt_rank * share_width, share_width, 1)
    w_qkv = jnp.concatenate([w_query[0], w_key[0], w_value[0]], axis=1)
    w_o, w_g, w_u, w_d = w_out[0], w_gate[0], w_up[0], w_down[0]
    begin = inputs.reshape(rows, share_width)
    cot = cotangent.reshape(rows, share_width)

    places = ctx_rank * block_rows + jnp.arange(block_rows, dtype=jnp.int32)
    offsets = jnp.concatenate(
        [places - doc_begins(doc_bounds[b], places) for b in range(micro_count)]
    )
    angles = offsets.astype(f32)[:, None] * rope_freqs(HD)[None, :]
    cos_half, sin_half = jnp.cos(angles), jnp.sin(angles)
    cosine = jnp.concatenate([cos_half] * 4, axis=1)
    sine = jnp.concatenate([sin_half] * 4, axis=1)
    key_lane = jnp.arange(128)[None, :] < HD
    kv_cosine = jnp.where(key_lane, cosine, 1.0)
    kv_sine = jnp.where(key_lane, sine, 0.0)

    def forward(whole, share, tick):
        hidden = whole.astype(f32)
        factor = lax.rsqrt(jnp.mean(hidden * hidden, axis=-1, keepdims=True) + eps)
        attn_in = (hidden * factor * gain_attn).astype(bf16)
        pre = jnp.dot(attn_in, w_qkv, preferred_element_type=f32)
        q_pre, kv_pre = pre[:, :256], pre[:, 256:]
        mix, logs, mixed, kv = attention(
            doc_bounds, q_pre, kv_pre, cosine, sine, kv_cosine, kv_sine, 1
        )
        part = jnp.dot(mix, w_o, preferred_element_type=f32).astype(bf16)
        mid, mid_whole = forward_mid(part, share, 2)
        mid_wide = mid_whole.astype(f32)
        mid_factor = lax.rsqrt(jnp.mean(mid_wide * mid_wide, axis=-1, keepdims=True) + eps)
        mlp_in = (mid_wide * mid_factor * gain_mlp).astype(bf16)
        gate = jnp.dot(mlp_in, w_g, preferred_element_type=f32)
        up = jnp.dot(mlp_in, w_u, preferred_element_type=f32)
        inner = lax.optimization_barrier((jax.nn.silu(gate) * up).astype(bf16))
        part = jnp.dot(inner, w_d, preferred_element_type=f32).astype(bf16)
        saved = SimpleNamespace(
            whole=whole, share=share, factor=factor, attn_in=attn_in, q_pre=q_pre, kv=kv,
            mix=mix, logs=logs, mixed=mixed, mid=mid, mid_whole=mid_whole,
            mid_factor=mid_factor, mlp_in=mlp_in, gate=gate, up=up, inner=inner,
        )
        return part, saved

    def line_of(part, whole, factor, gain):
        dots = jnp.sum(part * (whole.astype(f32) * factor * gain), axis=1)
        return jnp.concatenate(
            [dots.reshape(rows // 128, 128), jnp.zeros((8 - rows // 128, 128), f32)]
        )

    def behind_mlp(grad, saved):
        gate, up = saved.gate, saved.up
        grad_inner = times_transposed(grad, w_d)
        sigmoid = jax.nn.sigmoid(gate)
        grad_gate = (grad_inner * up * sigmoid * (1.0 + gate * (1.0 - sigmoid))).astype(bf16)
        grad_up = (grad_inner * gate * sigmoid).astype(bf16)
        part = times_transposed(grad_gate, w_g) + times_transposed(grad_up, w_u)
        line = line_of(part, saved.mid_whole, saved.mid_factor, gain_mlp)
        return part.astype(bf16), line, grad_gate, grad_up

    def backward(grad, grad_share, saved):
        part, line, _, _ = behind_mlp(grad, saved)
        grad_mid, grad_attn = backward_sum(
            "mid", part, line, grad_share, saved.mid, saved.mid_factor, own_gain_mlp,
            [], 3,
        )
        grad_mix = times_transposed(grad_attn, w_o).astype(bf16)
        grad_query, grad_kv = attention_back(
            doc_bounds, saved.q_pre, cosine, sine, kv_cosine, kv_sine, saved.kv,
            saved.logs, saved.mixed, grad_mix, 4,
        )
        grad_pre = jnp.concatenate([grad_query, grad_kv], axis=1)
        part = times_transposed(grad_pre, w_qkv)
        line = line_of(part, saved.whole, saved.factor, gain_attn)
        return (
            part.astype(bf16), line, grad_mid, saved.share.astype(f32), saved.factor,
            own_gain_attn,
        )

    whole_cot = lax.all_gather(cot, "wt", axis=1, tiled=True)
    part, saved = forward(wt_gather(begin, 6), begin, 0)
    share, whole = forward_pass(part, saved.mid, begin, 7)
    part, saved = forward(whole, share, 1)
    last_part = part

    operands = backward(whole_cot, cot, saved)
    section = lax.axis_index("section")
    grad_share, grad = backward_sum("pass", *operands, [cot], 9)
    part, line, grad_gate, grad_up = behind_mlp(grad, saved)
    half = saved.inner.shape[1] // 2
    mids = middle_of_backward(
        dict(
            bounds=doc_bounds, part=part, line=line, above=grad_share, mid=saved.mid,
            factor=saved.mid_factor, gain=own_gain_mlp, flat=saved.q_pre, cosine=cosine,
            sine=sine, kv_cosine=kv_cosine, kv_sine=kv_sine, kv=saved.kv, logs=saved.logs,
            mixed=saved.mixed, w_out=w_o,
            down_a=contract_rows(saved.inner[:, :half], grad).astype(bf16),
            down_b=contract_rows(saved.inner[:, half:], grad).astype(bf16),
        ),
        8,
    )
    ends = end_of_backward(
        dict(
            grad_pre=mids.grad_pre, w_qkv=w_qkv, attn_in=saved.attn_in, mix=saved.mix,
            whole=mids.whole, grad_mid=mids.grad_mid, hidden=saved.share.astype(f32),
            factor=saved.factor, gain=own_gain_attn, piece=mids.piece, last_part=last_part,
            last_mid=saved.mid,
            up=contract_rows(saved.mlp_in, grad_up).astype(bf16),
            gate=contract_rows(saved.mlp_in, grad_gate).astype(bf16),
        ),
        10,
    )
    first_grad, result, gains = ends.first_grad, ends.result, ends.gains
    up, gate, pre, out = (
        one.astype(f32) for one in (ends.own_up, ends.own_gate, ends.own_pre, ends.own_out)
    )
    down = jnp.concatenate([mids.own_down_a, mids.own_down_b], axis=0).astype(f32)
    boundary = jnp.where(section == 0, first_grad, result)
    return (
        boundary.reshape(1, micro_count, block_rows, share_width),
        gains[0][None],
        pre[:, :256][None],
        pre[:, 256:320][None],
        pre[:, 320:][None],
        out[None],
        gains[8][None],
        gate[None],
        up[None],
        down[None],
    )


def solution(mesh):
    return jax.shard_map(
        per_device,
        mesh=mesh,
        in_specs=(
            P(None, "ctx", "wt"),
            P(None, "ctx", "wt"),
            P(),
            P("section", None),
            P("section", None, "wt"),
            P("section", None, "wt"),
            P("section", None, "wt"),
            P("section", "wt", None),
            P("section", None),
            P("section", None, "wt"),
            P("section", None, "wt"),
            P("section", "wt", None),
        ),
        out_specs=(
            P("section", None, "ctx", "wt"),
            P("section", "ctx"),
            P("section", "ctx", "wt"),
            P("section", "ctx", "wt"),
            P("section", "ctx", "wt"),
            P("section", "wt", "ctx"),
            P("section", "ctx"),
            P("section", "ctx", "wt"),
            P("section", "ctx", "wt"),
            P("section", "wt", "ctx"),
        ),
        check_vma=False,
    )
```

```python
import functools
from types import SimpleNamespace

import jax
import jax.numpy as jnp
from jax import lax
from jax.experimental import pallas as pl
from jax.experimental.pallas import tpu as pltpu
from jax.sharding import PartitionSpec as P

HD = 64
eps = 1e-05
theta = 500000.0
neg_big = -1e30
MESH = pl.DeviceIdType.MESH
f32 = jnp.float32
bf16 = jnp.bfloat16
MiB = 1024 * 1024


def rope_freqs(head_width):
    index_steps = jnp.arange(head_width // 2, dtype=jnp.float32)
    inverse = theta ** (-2.0 * index_steps / head_width)
    wavelen = 2.0 * jnp.pi / inverse
    smooth = (8192.0 / wavelen - 1.0) / 3.0
    blended = (1.0 - smooth) * inverse / 32.0 + smooth * inverse
    return jnp.where(
        wavelen < 2048.0, inverse, jnp.where(wavelen > 8192.0, inverse / 32.0, blended)
    )


def doc_begins(bounds, places):
    starts = jnp.concatenate([jnp.zeros((1,), jnp.int32), bounds])
    started = places[:, None] >= starts[None, :]
    return jnp.max(jnp.where(started, starts[None, :], 0), axis=1)


def contract_rows(left, right):
    return lax.dot_general(
        left, right, (((0,), (0,)), ((), ())), preferred_element_type=jnp.float32
    )


def times_transposed(left, right):
    return lax.dot_general(
        left, right, (((1,), (1,)), ((), ())), preferred_element_type=jnp.float32
    )


def greet(peers):
    barrier = pltpu.get_barrier_semaphore()
    for peer in peers:
        pl.semaphore_signal(barrier, inc=1, device_id=peer, device_id_type=MESH)
    pl.semaphore_wait(barrier, len(peers))


def remote(src, dst, send, recv, peer):
    return pltpu.make_async_remote_copy(
        src_ref=src, dst_ref=dst, send_sem=send, recv_sem=recv, device_id=peer,
        device_id_type=MESH,
    )


class WtPlace:
    def __init__(self, width):
        self.me = lax.axis_index("wt")
        self.z = self.me // 2
        self.core = self.me % 2
        self.sib = self.me + 1 - 2 * self.core
        self.width = width

    def peer(self, k):
        return lax.rem(self.z + k + 4, 4) * 2 + self.core

    def cols(self, index):
        return pl.ds(pl.multiple_of(index * self.width, self.width), self.width)


def way(chunk):
    return 1 if chunk % 2 == 0 else -1


class Gather:
    def __init__(self, place, out, sems, chunk, rows):
        self.place, self.out, self.chunk, self.rows = place, out, chunk, rows
        self.send, self.recv, self.fsend, self.frecv, self.local = sems
        self.s = way(chunk)

    def piece(self, index):
        return self.out.at[self.rows, self.place.cols(index)]

    def aside(self, k):
        p, q = self.place, self.chunk
        got = self.piece(p.peer(-k))
        return remote(got, got, self.fsend.at[q, k % 4], self.frecv.at[q, k % 4], {"wt": p.sib})

    def start(self, src):
        p, q = self.place, self.chunk
        mine = self.piece(p.me)
        self.own = pltpu.make_async_copy(src, mine, self.local.at[q])
        self.sent = []
        for hop in (self.s, -self.s):
            k = hop % 4
            copy = remote(
                src, mine, self.send.at[q, k], self.recv.at[q, k], {"wt": p.peer(hop)}
            )
            copy.start()
            self.sent.append(copy)
        copy = remote(src, mine, self.fsend.at[q, 0], self.frecv.at[q, 0], {"wt": p.sib})
        copy.start()
        self.sent.append(copy)
        self.own.start()

    def forward(self):
        p, q, s = self.place, self.chunk, self.s
        self.passed = []
        self.sent[0].wait_recv()
        got = self.piece(p.peer(-s))
        copy = remote(got, got, self.send.at[q, 2], self.recv.at[q, 2], {"wt": p.peer(s)})
        copy.start()
        self.sent.append(copy)
        near = self.aside(s)
        near.start()
        self.passed.append(near)

    def forward_more(self):
        s = self.s
        self.sent[1].wait_recv()
        near = self.aside(-s)
        near.start()
        self.passed.append(near)
        self.sent[3].wait_recv()
        near = self.aside(2)
        near.start()
        self.passed.append(near)

    def finish(self):
        for copy in self.passed:
            copy.wait()
        self.sent[2].wait_recv()
        for copy in self.sent:
            copy.wait_send()
        self.own.wait()


def gather_all(gathers):
    for one in gathers:
        one.forward()
    for one in gathers:
        one.forward_more()
    for one in gathers:
        one.finish()


def gather_scratch(chunks):
    return [pltpu.SemaphoreType.DMA((chunks, 4)) for _ in range(4)] + [
        pltpu.SemaphoreType.DMA((chunks,))
    ]


def greet_wt(place, more=()):
    greet([{"wt": place.sib}] + [{"wt": place.peer(k)} for k in (1, -1)] + list(more))


def gather_kernel(chunks, x, out, *sems):
    place = WtPlace(x.shape[1])
    greet_wt(place)
    rows = x.shape[0] // chunks
    parts = []
    for q in range(chunks):
        chunk_rows = pl.ds(q * rows, rows)
        part = Gather(place, out, sems, q, chunk_rows)
        part.start(x.at[chunk_rows])
        parts.append(part)
    gather_all(parts)


def wt_gather(x, collective_id, chunks=4):
    rows, width = x.shape
    return pl.pallas_call(
        functools.partial(gather_kernel, chunks),
        out_shape=jax.ShapeDtypeStruct((rows, 8 * width), x.dtype),
        in_specs=[pl.BlockSpec(memory_space=pltpu.VMEM)],
        out_specs=pl.BlockSpec(memory_space=pl.ANY),
        scratch_shapes=gather_scratch(chunks),
        compiler_params=pltpu.CompilerParams(
            collective_id=collective_id, has_side_effects=True, vmem_limit_bytes=4 * MiB
        ),
        name="gather_wt",
    )(x)


class Reduce:
    def __init__(self, place, part, bufs, chunk, rows):
        self.place, self.part, self.chunk, self.rows = place, part, chunk, rows
        (self.pair, self.out, self.landed, self.s1, self.r1, self.s2, self.r2) = bufs
        self.s = way(chunk)

    def start(self):
        p, q, s = self.place, self.chunk, self.s
        self.first = {}
        for k in (2, -s, s, 0):
            target = lax.rem(p.z + k + 4, 4) * 2 + 1 - p.core
            copy = remote(
                self.part.at[self.rows, p.cols(target)], self.pair.at[q, k % 4],
                self.s1.at[q, k % 4], self.r1.at[q, k % 4], {"wt": p.sib},
            )
            copy.start()
            self.first[k] = copy

    def both(self, k):
        p, q = self.place, self.chunk
        self.first[k].wait_recv()
        own = self.part[self.rows, p.cols(p.peer(k))]
        return own.astype(f32) + self.pair[q, k % 4].astype(f32)

    def onward(self, k, value, hop):
        p, q = self.place, self.chunk
        self.out[q, k % 4] = value.astype(bf16)
        copy = remote(
            self.out.at[q, k % 4], self.landed.at[q, k % 4], self.s2.at[q, k % 4],
            self.r2.at[q, k % 4], {"wt": p.peer(hop)},
        )
        copy.start()
        self.second[k] = copy

    def pass_on(self):
        self.second = {}
        self.onward(2, self.both(2), self.s)
        self.onward(-self.s, self.both(-self.s), -self.s)

    def pass_more(self):
        q, s = self.chunk, self.s
        value = self.both(s)
        self.second[2].wait_recv()
        self.onward(s, value + self.landed[q, 2].astype(f32), s)

    def total(self):
        q = self.chunk
        total = self.both(0)
        for k in (-self.s, self.s):
            self.second[k].wait_recv()
            total = total + self.landed[q, k % 4].astype(f32)
        return total

    def finish(self):
        for copy in self.first.values():
            copy.wait_send()
        for copy in self.second.values():
            copy.wait_send()


def sum_in_turn(sums, use):
    for one in sums:
        one.start()
    for one in sums:
        one.pass_on()
    for one in sums:
        one.pass_more()
    for q in range(len(sums)):
        use(q)


def reduce_scratch(chunks, rows, width):
    return [pltpu.VMEM((chunks, 4, rows, width), bf16) for _ in range(3)] + [
        pltpu.SemaphoreType.DMA((chunks, 4)) for _ in range(4)
    ]


def column(line, blocks):
    eye = lax.broadcasted_iota(jnp.int32, (128, 128), 0) == lax.broadcasted_iota(
        jnp.int32, (128, 128), 1
    )
    parts = [
        jnp.sum(
            jnp.where(eye, jnp.broadcast_to(line[j : j + 1, :], (128, 128)), 0.0),
            axis=1, keepdims=True,
        )
        for j in range(blocks)
    ]
    return jnp.concatenate(parts, axis=0)


def swap_sections(src, dst, send, recv):
    return remote(src, dst, send, recv, {"section": 1 - lax.axis_index("section")})


def forward_mid_kernel(chunks, part, skip, mid, whole, agsrc, *scratch):
    bufs, sems = scratch[:7], scratch[7:]
    place = WtPlace(skip.shape[1])
    greet_wt(place)
    rows = skip.shape[0] // chunks
    spans = [pl.ds(q * rows, rows) for q in range(chunks)]
    sums = [Reduce(place, part, bufs, q, spans[q]) for q in range(chunks)]
    gathers = [Gather(place, whole, sems, q, spans[q]) for q in range(chunks)]

    def use(q):
        value = skip[spans[q], :].astype(f32) + sums[q].total()
        mid[spans[q], :] = value
        agsrc[spans[q], :] = value.astype(bf16)
        gathers[q].start(agsrc.at[spans[q]])

    sum_in_turn(sums, use)
    gather_all(gathers)
    for one in sums:
        one.finish()


def forward_mid(part, skip, collective_id, chunks=4):
    rows, width = skip.shape
    return pl.pallas_call(
        functools.partial(forward_mid_kernel, chunks),
        out_shape=(
            jax.ShapeDtypeStruct((rows, width), f32),
            jax.ShapeDtypeStruct((rows, 8 * width), bf16),
        ),
        in_specs=[pl.BlockSpec(memory_space=pltpu.VMEM)] * 2,
        out_specs=(
            pl.BlockSpec(memory_space=pltpu.VMEM),
            pl.BlockSpec(memory_space=pl.ANY),
        ),
        scratch_shapes=[pltpu.VMEM((rows, width), bf16)]
        + reduce_scratch(chunks, rows // chunks, width)
        + gather_scratch(chunks),
        compiler_params=pltpu.CompilerParams(
            collective_id=collective_id, has_side_effects=True, vmem_limit_bytes=10 * MiB
        ),
        name="sum_mid_gather",
    )(part, skip)


def forward_pass_kernel(
    chunks, part, mid, begin, share, whole, agsrc, arrived, xsend, xrecv, *scratch
):
    bufs, sems = scratch[:7], scratch[7:]
    place = WtPlace(mid.shape[1])
    section = lax.axis_index("section")
    greet_wt(place, [{"section": 1 - section}])
    rows = mid.shape[0] // chunks
    spans = [pl.ds(q * rows, rows) for q in range(chunks)]
    sums = [Reduce(place, part, bufs, q, spans[q]) for q in range(chunks)]
    gathers = [Gather(place, whole, sems, q, spans[q]) for q in range(chunks)]
    swaps = []

    def use(q):
        agsrc[spans[q], :] = (mid[spans[q], :] + sums[q].total()).astype(bf16)
        swap = swap_sections(
            agsrc.at[spans[q]], arrived.at[spans[q]], xsend.at[q], xrecv.at[q]
        )
        swap.start()
        swaps.append(swap)

    sum_in_turn(sums, use)
    for q in range(chunks):
        swaps[q].wait_recv()
        share[spans[q], :] = jnp.where(
            section == 0, begin[spans[q], :].astype(f32), arrived[spans[q], :].astype(f32)
        ).astype(bf16)
        gathers[q].start(share.at[spans[q]])
    gather_all(gathers)
    for one in sums:
        one.finish()
    for one in swaps:
        one.wait_send()


def forward_pass(part, mid, begin, collective_id, chunks=4):
    rows, width = mid.shape
    return pl.pallas_call(
        functools.partial(forward_pass_kernel, chunks),
        out_shape=(
            jax.ShapeDtypeStruct((rows, width), bf16),
            jax.ShapeDtypeStruct((rows, 8 * width), bf16),
        ),
        in_specs=[pl.BlockSpec(memory_space=pltpu.VMEM)] * 3,
        out_specs=(
            pl.BlockSpec(memory_space=pltpu.VMEM),
            pl.BlockSpec(memory_space=pl.ANY),
        ),
        scratch_shapes=[
            pltpu.VMEM((rows, width), bf16),
            pltpu.VMEM((rows, width), bf16),
            pltpu.SemaphoreType.DMA((chunks,)),
            pltpu.SemaphoreType.DMA((chunks,)),
        ]
        + reduce_scratch(chunks, rows // chunks, width)
        + gather_scratch(chunks),
        compiler_params=pltpu.CompilerParams(
            collective_id=collective_id, has_side_effects=True, vmem_limit_bytes=10 * MiB
        ),
        name="sum_pass_gather",
    )(part, mid, begin)


def add_up(dst, sources, step=64):
    def some(i, carry):
        span = pl.ds(pl.multiple_of(i * step, step), step)
        total = sources[0][span, :].astype(f32)
        for source in sources[1:]:
            total = total + source[span, :].astype(f32)
        dst[span, :] = total.astype(dst.dtype)
        return carry

    lax.fori_loop(0, dst.shape[0] // step, some, 0)


class CtxPlace:
    def __init__(self):
        self.me = lax.axis_index("ctx")
        self.x = self.me // 2
        self.y = self.me % 2

    def at(self, k, y):
        return lax.rem(self.x + k + 4, 4) * 2 + y

    def x_peer(self, hop):
        return {"ctx": self.at(hop, self.y)}

    def y_peer(self):
        return {"ctx": self.at(0, 1 - self.y)}

    def near(self):
        return [self.x_peer(1), self.x_peer(-1), self.y_peer()]

    def all(self):
        return [{"ctx": lax.rem(self.me + d, 8)} for d in range(1, 8)]


class XRing:
    def __init__(self, place, s, loaded, bufs, sems):
        self.place, self.s, self.loaded = place, s, loaded
        self.via, self.near, self.joined, self.summed = bufs
        self.send, self.recv = sems
        self.copies = {}

    def go(self, i, src, dst, hop):
        copy = remote(src, dst, self.send.at[i], self.recv.at[i], self.place.x_peer(hop))
        copy.start()
        self.copies[i] = copy

    def start(self, k):
        if k == 2:
            self.go(0, self.loaded(2), self.via, self.s)
        elif k == -self.s:
            self.go(1, self.loaded(k), self.near, k)

    def join(self):
        self.copies[0].wait_recv()
        add_up(self.summed, [self.loaded(self.s), self.via])
        self.go(2, self.summed, self.joined, self.s)

    def total(self, dst):
        self.copies[1].wait_recv()
        self.copies[2].wait_recv()
        add_up(dst, [self.loaded(0), self.near, self.joined])

    def finish(self):
        for copy in self.copies.values():
            copy.wait_send()


def cut(array, dim, owner):
    length = array.shape[dim] // 8
    span = pl.ds(pl.multiple_of(owner * length, length), length)
    return array.at[span] if dim == 0 else array.at[:, span]


BLOCKS = (2, -1, 1, 0)


class XFirst:
    def __init__(self, place, array, dim, out, scratch):
        self.place, self.out = place, out
        bufs, summed, self.swapped, sems, self.ssend, self.srecv, *held = scratch
        self.held, self.lsem = held if held else (None, None)

        def block(k, y):
            return cut(array, dim, place.at(k, y))

        def loaded(k, y):
            if held and k in (0, way(y)):
                return self.held.at[abs(k), y]
            return block(k, y)

        self.block = block
        self.rings = [
            XRing(
                place, way(y), lambda k, y=y: loaded(k, y),
                [bufs.at[y, j] for j in range(3)] + [summed.at[y]],
                [sems.at[0, y], sems.at[1, y]],
            )
            for y in (0, 1)
        ]

    def start(self):
        self.loads = []
        for y, ring in enumerate(self.rings):
            ring.start(2)
            ring.start(-ring.s)
        if self.held is not None:
            for y in (0, 1):
                for k in (way(y), 0):
                    copy = pltpu.make_async_copy(
                        self.block(k, y), self.held.at[abs(k), y], self.lsem.at[abs(k), y]
                    )
                    copy.start()
                    self.loads.append(copy)

    def join(self):
        for copy in self.loads:
            copy.wait()
        for ring in self.rings:
            ring.join()

    def swap(self):
        for y in (0, 1):
            self.rings[y].total(self.swapped.at[1 + y])
        self.across = remote(
            self.swapped.at[1 + (1 - self.place.y)], self.swapped.at[0], self.ssend.at[0],
            self.srecv.at[0], self.place.y_peer(),
        )
        self.across.start()

    def total(self):
        self.across.wait_recv()
        add_up(self.out, [self.swapped.at[1 + self.place.y], self.swapped.at[0]])

    def finish(self):
        for ring in self.rings:
            ring.finish()
        self.across.wait_send()


class YFirst:
    def __init__(self, place, array, dim, out, scratch):
        self.place, self.array, self.dim, self.out = place, array, dim, out
        (bufs, summed, self.swapped, sems, self.ssend, self.srecv, self.held, self.lsem) = scratch
        swapped = self.swapped
        self.half = half = self.held.shape[1] // 2
        self.rings = [
            XRing(
                place, way(h), lambda k, h=h: swapped.at[k % 4, pl.ds(h * half, half)],
                [bufs.at[h, j] for j in range(3)] + [summed.at[h]],
                [sems.at[0, h], sems.at[1, h]],
            )
            for h in (0, 1)
        ]

    def start(self):
        self.swaps, self.loads = {}, {}
        for k in BLOCKS:
            copy = remote(
                cut(self.array, self.dim, self.place.at(k, 1 - self.place.y)),
                self.swapped.at[k % 4], self.ssend.at[k % 4], self.srecv.at[k % 4],
                self.place.y_peer(),
            )
            copy.start()
            self.swaps[k] = copy
        for k in BLOCKS:
            copy = pltpu.make_async_copy(
                cut(self.array, self.dim, self.place.at(k, self.place.y)),
                self.held.at[k % 4], self.lsem.at[k % 4],
            )
            copy.start()
            self.loads[k] = copy

    def first(self):
        for k in BLOCKS:
            self.loads[k].wait()
            self.swaps[k].wait_recv()
            block = self.swapped.at[k % 4]
            add_up(block, [block, self.held.at[k % 4]])
            for ring in self.rings:
                ring.start(k)

    def join(self):
        for ring in self.rings:
            ring.join()

    def total(self):
        for h, ring in enumerate(self.rings):
            ring.total(self.out.at[pl.ds(h * self.half, self.half)])

    def finish(self):
        for ring in self.rings:
            ring.finish()
        for copy in self.swaps.values():
            copy.wait_send()


def owned(shape, dim):
    return tuple(n // 8 if i == dim else n for i, n in enumerate(shape))


def ctx_scratch(shape, dim, mode):
    rows, width = owned(shape, dim)
    ring = (rows // 2 if mode == "y" else rows, width)
    scratch = [
        pltpu.VMEM((2, 3, *ring), bf16),
        pltpu.VMEM((2, *ring), bf16),
        pltpu.VMEM((4 if mode == "y" else 3, rows, width), bf16),
        pltpu.SemaphoreType.DMA((2, 2, 3)),
        pltpu.SemaphoreType.DMA((4,)),
        pltpu.SemaphoreType.DMA((4,)),
    ]
    if mode == "y":
        scratch += [pltpu.VMEM((4, rows, width), bf16), pltpu.SemaphoreType.DMA((4,))]
    elif mode == "x":
        scratch += [pltpu.VMEM((2, 2, rows, width), bf16), pltpu.SemaphoreType.DMA((2, 2))]
    return scratch


def everyone(place):
    return [lax.rem(place.me + d, 8) for d in range(1, 8)]


class Lines:
    def __init__(self, place, line, slots, send, recv):
        self.line, self.slots = line, slots
        self.copies = [
            remote(line, slots.at[d], send.at[d], recv.at[d], {"wt": lax.rem(place.me + d, 8)})
            for d in range(1, 8)
        ]

    def start(self):
        for copy in self.copies:
            copy.start()

    def total(self):
        total = self.line[...]
        for d, copy in enumerate(self.copies, start=1):
            copy.wait_recv()
            total = total + self.slots[d]
        return total

    def finish(self):
        for copy in self.copies:
            copy.wait_send()


def norm_back(total, above, own, scale, gain, mean):
    normed = own.astype(f32) * scale
    grad = above.astype(f32) + scale * (total * gain - normed * mean)
    return grad, jnp.sum(total * normed, axis=0, keepdims=True)


def backward_kernel(mode, chunks, part, line, above, own, factor, gain, *rest):
    if mode == "mid":
        share, whole, agsrc, *rest = rest
    else:
        begin, share, whole, agsrc, arrived, xsend, xrecv, *rest = rest
    slots, lsend, lrecv, *rest = rest
    bufs, sems = rest[:7], rest[7:]
    place = WtPlace(own.shape[1])
    section = lax.axis_index("section")
    greet(
        [{"wt": peer} for peer in everyone(place)]
        + ([{"section": 1 - section}] if mode == "pass" else [])
    )
    rows = own.shape[0] // chunks
    depth = 8 * own.shape[1]
    spans = [pl.ds(q * rows, rows) for q in range(chunks)]
    sums = [Reduce(place, part, bufs, q, spans[q]) for q in range(chunks)]
    gathers = [Gather(place, whole, sems, q, spans[q]) for q in range(chunks)]
    lines = Lines(place, line, slots, lsend, lrecv)
    lines.start()
    for one in sums:
        one.start()
    for one in sums:
        one.pass_on()
    for one in sums:
        one.pass_more()
    mean = column(lines.total(), own.shape[0] // 128) * (1.0 / depth)
    swaps = []
    for q in range(chunks):
        span = spans[q]
        grad, _ = norm_back(
            sums[q].total(), above[span, :], own[span, :], factor[span, :], gain[...],
            mean[q * rows : (q + 1) * rows],
        )
        agsrc[span, :] = grad.astype(bf16)
        if mode == "mid":
            share[span, :] = grad
            gathers[q].start(agsrc.at[span])
        else:
            swap = swap_sections(agsrc.at[span], arrived.at[span], xsend.at[q], xrecv.at[q])
            swap.start()
            swaps.append(swap)
    if mode == "pass":
        for q in range(chunks):
            span = spans[q]
            swaps[q].wait_recv()
            share[span, :] = jnp.where(
                section == 1, begin[span, :].astype(f32), arrived[span, :].astype(f32)
            ).astype(bf16)
            gathers[q].start(share.at[span])
    gather_all(gathers)
    for one in sums:
        one.finish()
    for one in swaps:
        one.wait_send()
    lines.finish()


def seven():
    return [pltpu.SemaphoreType.DMA((8,)), pltpu.SemaphoreType.DMA((8,))]


def backward_sum(mode, part, line, above, own, factor, gain, extra, collective_id, chunks=4):
    rows, width = own.shape
    vmem = pl.BlockSpec(memory_space=pltpu.VMEM)
    hbm = pl.BlockSpec(memory_space=pl.ANY)
    scratch = [pltpu.VMEM((rows, width), bf16)]
    if mode == "pass":
        scratch += [
            pltpu.VMEM((rows, width), bf16),
            pltpu.SemaphoreType.DMA((chunks,)),
            pltpu.SemaphoreType.DMA((chunks,)),
        ]
    scratch += [pltpu.VMEM((8, 8, 128), f32)] + seven()
    scratch += reduce_scratch(chunks, rows // chunks, width) + gather_scratch(chunks)
    operands = [part, line, above, own, factor, gain] + extra
    return pl.pallas_call(
        functools.partial(backward_kernel, mode, chunks),
        out_shape=(
            jax.ShapeDtypeStruct((rows, width), f32 if mode == "mid" else bf16),
            jax.ShapeDtypeStruct((rows, 8 * width), bf16),
        ),
        in_specs=[vmem] * len(operands),
        out_specs=(vmem, hbm),
        scratch_shapes=scratch,
        compiler_params=pltpu.CompilerParams(
            collective_id=collective_id, has_side_effects=True, vmem_limit_bytes=12 * MiB
        ),
        name="sum_back_" + mode,
    )(*operands)


def lanes(shape):
    return lax.broadcasted_iota(jnp.int32, shape, len(shape) - 1)


def turn(u, cosine, sine):
    low_half = jnp.bitwise_and(lanes(u.shape), HD - 1) < HD // 2
    turned = jnp.where(low_half, -pltpu.roll(u, 128 - HD // 2, 1), pltpu.roll(u, HD // 2, 1))
    return u * cosine + turned * sine


def turn_back(y, cosine, sine):
    low_half = jnp.bitwise_and(lanes(y.shape), HD - 1) < HD // 2
    z = y * sine
    turned = jnp.where(low_half, pltpu.roll(z, 128 - HD // 2, 1), -pltpu.roll(z, HD // 2, 1))
    return y * cosine + turned


def visible_keys(bounds, b, key_block, me, rows, heads):
    row = lax.broadcasted_iota(jnp.int32, (1, heads * rows), 1)
    for head in range(1, heads):
        row = row - jnp.where(lanes((1, heads * rows)) >= head * rows, rows, 0)
    place = me * rows + row
    first, second = bounds[b, 0], bounds[b, 1]
    begin = jnp.where(place >= second, second, jnp.where(place >= first, first, 0))
    key = key_block * rows + lax.broadcasted_iota(jnp.int32, (rows, 1), 0)
    return (key <= place) & (key >= begin)


def stack_queries(flat, cosine, sine, b, rows, stacked):
    span = pl.ds(b * rows, rows)
    low = lanes((rows, 128)) < HD
    for pair in range(2):
        u = turn(flat[span, 128 * pair : 128 * pair + 128], cosine[span, :], sine[span, :])
        u = u.astype(bf16).astype(f32) * (HD**-0.5)
        even = jnp.where(low, u, 0.0)
        odd = jnp.where(low, pltpu.roll(u, HD, 1), 0.0)
        stacked[b, pl.ds(2 * pair * rows, rows), :] = even.astype(bf16)
        stacked[b, pl.ds((2 * pair + 1) * rows, rows), :] = odd.astype(bf16)


def later(me, d, n):
    return me + d < n


def earlier(me, d, n):
    return me - d >= 0


def greet_order(me, n, side, count):
    barrier = pltpu.get_barrier_semaphore()
    step = 1 if side is later else n - 1
    for d in range(1, n):

        @pl.when(side(me, d, n))
        def _():
            pl.semaphore_signal(
                barrier, inc=1, device_id={"ctx": lax.rem(me + d * step, n)},
                device_id_type=MESH,
            )

    def wait():
        @pl.when(count > 0)
        def _():
            pl.semaphore_wait(barrier, count)

    return wait


def attention_kernel(
    n, bounds, flat, kv_pre, cosine, sine, kv_cosine, kv_sine, mix, logs, mixed, kv,
    stacked, acc, mine, send, recv
):
    me = lax.axis_index("ctx")
    rows = kv.shape[2]
    heads = 4
    wait = greet_order(me, n, earlier, n - 1 - me)
    for b in range(2):
        span = pl.ds(b * rows, rows)
        turned = turn(kv_pre[span, :], kv_cosine[span, :], kv_sine[span, :]).astype(bf16)
        mine[b] = turned
        kv[me, b] = turned
    wait()

    def copy(d):
        return remote(mine, kv.at[me], send.at[d], recv.at[d], {"ctx": lax.rem(me + d, n)})

    for d in reversed(range(1, n)):

        @pl.when(later(me, d, n))
        def _():
            copy(d).start()

    for b in range(2):
        stack_queries(flat, cosine, sine, b, rows, stacked)
    acc[...] = jnp.zeros_like(acc)

    def block(j, carry):
        after = []
        for b in range(2):
            peak, total = carry[2 * b : 2 * b + 2]
            keys = kv[j, b]
            scores = times_transposed(keys, stacked[b])
            scores = jnp.where(visible_keys(bounds, b, j, me, rows, heads), scores, neg_big)
            new_peak = jnp.maximum(peak, jnp.max(scores, axis=0, keepdims=True))
            shrink = jnp.exp(peak - new_peak)
            weight = jnp.exp(scores - new_peak)
            total = total * shrink + jnp.sum(weight, axis=0, keepdims=True)
            acc[b] = acc[b] * shrink + contract_rows(keys, weight.astype(bf16))
            after += [new_peak, total]
        return tuple(after)

    def arrived(d, carry):
        copy(d).wait_recv()
        return block(me - d, carry)

    zero = jnp.zeros((1, heads * rows), f32)
    done = block(me, (zero + neg_big, zero) * 2)
    done = lax.fori_loop(1, me + 1, arrived, done)
    low = lanes((rows, 128)) < HD
    for b in range(2):
        peak, total = done[2 * b : 2 * b + 2]
        out = acc[b] / total
        mixed[b] = out
        logs[b] = peak + jnp.log(total)
        upright = out.T
        for pair in range(2):
            even = upright[2 * pair * rows : (2 * pair + 1) * rows]
            odd = upright[(2 * pair + 1) * rows : (2 * pair + 2) * rows]
            both = jnp.where(low, pltpu.roll(even, HD, 1), odd)
            mix[pl.ds(b * rows, rows), 128 * pair : 128 * pair + 128] = both.astype(bf16)
    for d in range(1, n):

        @pl.when(later(me, d, n))
        def _():
            copy(d).wait_send()


def attention(bounds, flat, kv_pre, cosine, sine, kv_cosine, kv_sine, collective_id):
    n = 8
    rows = flat.shape[0] // 2
    vmem = pl.BlockSpec(memory_space=pltpu.VMEM)
    return pl.pallas_call(
        functools.partial(attention_kernel, n),
        out_shape=(
            jax.ShapeDtypeStruct((2 * rows, 256), bf16),
            jax.ShapeDtypeStruct((2, 1, 4 * rows), f32),
            jax.ShapeDtypeStruct((2, 128, 4 * rows), f32),
            jax.ShapeDtypeStruct((n, 2, rows, 128), bf16),
        ),
        in_specs=[pl.BlockSpec(memory_space=pltpu.SMEM)] + [vmem] * 6,
        out_specs=(vmem,) * 4,
        scratch_shapes=[
            pltpu.VMEM((2, 4 * rows, 128), bf16),
            pltpu.VMEM((2, 128, 4 * rows), f32),
            pltpu.VMEM((2, rows, 128), bf16),
            pltpu.SemaphoreType.DMA((n,)),
            pltpu.SemaphoreType.DMA((n,)),
        ],
        compiler_params=pltpu.CompilerParams(
            collective_id=collective_id, has_side_effects=True, vmem_limit_bytes=20 * MiB
        ),
        name="attention",
    )(bounds, flat, kv_pre, cosine, sine, kv_cosine, kv_sine)


def attention_back_kernel(n, *refs):
    me = lax.axis_index("ctx")
    attention_back_steps(n, me, greet_order(me, n, later, me), *refs)


def attention_back_steps(
    n, me, wait, bounds, flat, cosine, sine, kv_cosine, kv_sine, kv, logs, mixed, grad, out,
    grad_kv, terms, slots, total, stacked, grads, acc, send, recv
):
    rows = kv.shape[2]
    heads = 4
    low = lanes((rows, 128)) < HD
    deltas = []
    for b in range(2):
        stack_queries(flat, cosine, sine, b, rows, stacked)
        for pair in range(2):
            u = grad[pl.ds(b * rows, rows), 128 * pair : 128 * pair + 128].astype(f32)
            even = jnp.where(low, 0.0, pltpu.roll(u, HD, 1))
            odd = jnp.where(low, 0.0, u)
            grads[b, pl.ds(2 * pair * rows, rows), :] = even.astype(bf16)
            grads[b, pl.ds((2 * pair + 1) * rows, rows), :] = odd.astype(bf16)
        deltas.append(
            jnp.sum(mixed[b] * grads[b].astype(f32).T, axis=0, keepdims=True)
        )
    acc[...] = jnp.zeros_like(acc)
    wait()

    def block(j):
        for b in range(2):
            keys = kv[j, b]
            scores = times_transposed(keys, stacked[b])
            probs = jnp.where(
                visible_keys(bounds, b, j, me, rows, heads), jnp.exp(scores - logs[b]), 0.0
            )
            grad_probs = times_transposed(keys, grads[b])
            grad_scores = (probs * (grad_probs - deltas[b])).astype(bf16)
            acc[b] += contract_rows(keys, grad_scores)
            terms[j, b] = (
                jnp.dot(grad_scores, stacked[b], preferred_element_type=f32)
                + jnp.dot(probs.astype(bf16), grads[b], preferred_element_type=f32)
            ).astype(bf16)

    def copy(d):
        back = lax.rem(me + n - d, n)
        return remote(terms.at[back], slots.at[d], send.at[d], recv.at[d], {"ctx": back})

    def block_sent(j, carry):
        block(j)
        copy(me - j).start()
        return carry

    lax.fori_loop(0, me, block_sent, 0)
    block(me)
    for b in range(2):
        span = pl.ds(b * rows, rows)
        upright = acc[b].T * (HD**-0.5)
        for pair in range(2):
            even = upright[2 * pair * rows : (2 * pair + 1) * rows]
            odd = upright[(2 * pair + 1) * rows : (2 * pair + 2) * rows]
            both = jnp.where(low, even, pltpu.roll(odd, HD, 1))
            out[span, 128 * pair : 128 * pair + 128] = turn_back(
                both, cosine[span, :], sine[span, :]
            ).astype(bf16)
    for b in range(2):
        total[b] = terms[me, b].astype(f32)
    for d in range(1, n):

        @pl.when(later(me, d, n))
        def _():
            copy(d).wait_recv()
            total[...] += slots[d].astype(f32)

    for b in range(2):
        span = pl.ds(b * rows, rows)
        grad_kv[span, :] = turn_back(
            total[b], kv_cosine[span, :], kv_sine[span, :]
        ).astype(bf16)
    for d in range(1, n):

        @pl.when(earlier(me, d, n))
        def _():
            copy(d).wait_send()


def attention_back_scratch(shape):
    n, two, rows, width = shape
    return [
        pltpu.VMEM(shape, bf16),
        pltpu.VMEM(shape, bf16),
        pltpu.VMEM((2, rows, width), f32),
        pltpu.VMEM((2, 4 * rows, 128), bf16),
        pltpu.VMEM((2, 4 * rows, 128), bf16),
        pltpu.VMEM((2, 128, 4 * rows), f32),
        pltpu.SemaphoreType.DMA((n,)),
        pltpu.SemaphoreType.DMA((n,)),
    ]


def attention_back(
    bounds, flat, cosine, sine, kv_cosine, kv_sine, kv, logs, mixed, grad, collective_id
):
    n, two, rows, width = kv.shape
    vmem = pl.BlockSpec(memory_space=pltpu.VMEM)
    return pl.pallas_call(
        functools.partial(attention_back_kernel, n),
        out_shape=(
            jax.ShapeDtypeStruct((2 * rows, 256), bf16),
            jax.ShapeDtypeStruct((2 * rows, 128), bf16),
        ),
        in_specs=[pl.BlockSpec(memory_space=pltpu.SMEM)] + [vmem] * 9,
        out_specs=(vmem, vmem),
        scratch_shapes=attention_back_scratch(kv.shape),
        compiler_params=pltpu.CompilerParams(
            collective_id=collective_id, has_side_effects=True, vmem_limit_bytes=24 * MiB
        ),
        name="attention_back",
    )(bounds, flat, cosine, sine, kv_cosine, kv_sine, kv, logs, mixed, grad)


def as_line(column_values, line):
    eye = lax.broadcasted_iota(jnp.int32, (128, 128), 0) == lax.broadcasted_iota(
        jnp.int32, (128, 128), 1
    )
    line[...] = jnp.zeros_like(line)
    for j in range(column_values.shape[0] // 128):
        block = column_values[128 * j : 128 * j + 128]
        line[j : j + 1, :] = jnp.sum(
            jnp.where(eye, jnp.broadcast_to(block, (128, 128)), 0.0), axis=0, keepdims=True
        )


CTX_DIMS = dict(down_a=1, up=0, down_b=1, gate=0, pre=0, out=1)
CTX_MODES = dict(down_a="x", up="x", down_b="y", gate="y", pre="local", out="local")


class Call:
    def __init__(self, chunks, names, ctx_names, refs):
        given, at = {}, 0
        for name, count in names:
            given[name] = refs[at] if count == 1 else refs[at : at + count]
            at += count
        self.r = SimpleNamespace(**given)
        self.place, self.ctx = WtPlace(given["gain"].shape[1]), CtxPlace()
        greet([{"wt": peer} for peer in everyone(self.place)] + self.ctx.all())
        self.width = self.place.width
        self.all_rows = given["factor"].shape[0]
        self.rows = self.all_rows // chunks
        self.spans = [pl.ds(q * self.rows, self.rows) for q in range(chunks)]
        self.blocks = [pl.ds(self.width * c, self.width) for c in range(8)]
        self.beside = [
            (YFirst if CTX_MODES[name] == "y" else XFirst)(
                self.ctx, given[name], CTX_DIMS[name], given["own_" + name],
                given["sum_" + name],
            )
            for name in ctx_names
        ]

    def sums(self, part, bufs):
        return [Reduce(self.place, part, bufs, q, span) for q, span in enumerate(self.spans)]

    def behind_norm(self, sums, lines, above, own, use):
        r = self.r
        mean = column(lines.total(), self.all_rows // 128) * (1.0 / (8 * self.width))
        terms = jnp.zeros((1, self.width), f32)
        for q, span in enumerate(self.spans):
            grad, term = norm_back(
                sums[q].total(), above[span, :], own[span, :], r.factor[span, :], r.gain[...],
                mean[q * self.rows : (q + 1) * self.rows],
            )
            terms = terms + term
            use(q, span, grad)
        return jnp.broadcast_to(terms, (8, self.width))


def middle_kernel(n, chunks, names, ctx_names, *refs):
    call = Call(chunks, names, ctx_names, refs)
    r, place, ctx = call.r, call.place, call.ctx
    down_a, down_b = call.beside
    sums = call.sums(r.part, r.reduce)
    gathers = [
        Gather(place, r.whole, r.gather, q, span) for q, span in enumerate(call.spans)
    ]
    lines = Lines(place, r.line, *r.slots)
    lines.start()
    for one in sums:
        one.start()
    for one in call.beside:
        one.start()
    for one in sums:
        one.pass_on()
    for one in sums:
        one.pass_more()

    def use(q, span, grad):
        r.grad_mid[span, :] = grad
        r.agsrc[span, :] = grad.astype(bf16)
        gathers[q].start(r.agsrc.at[span])

    r.piece[...] = call.behind_norm(sums, lines, r.above, r.mid, use)
    for one in gathers:
        one.forward()
    for one in gathers:
        one.forward_more()
    down_a.join()
    for one in gathers:
        one.finish()
    r.grad_mix[...] = times_transposed(r.whole[...], r.w_out[...]).astype(bf16)
    down_b.first()
    down_a.swap()
    attention_back_steps(
        n, ctx.me, lambda: None, r.bounds, r.flat, r.cosine, r.sine, r.kv_cosine, r.kv_sine,
        r.kv, r.logs, r.mixed, r.grad_mix, r.grad_pre.at[:, pl.ds(0, 256)],
        r.grad_pre.at[:, pl.ds(256, 128)], *r.attention
    )
    down_b.join()
    down_a.total()
    down_b.total()
    for one in sums + call.beside:
        one.finish()
    lines.finish()


def last_kernel(n, chunks, names, ctx_names, *refs):
    call = Call(chunks, names, ctx_names, refs)
    r, place, ctx = call.r, call.place, call.ctx
    up, gate, pre, out = call.beside
    grad_pre = r.grad_pre
    up.start()
    gate.start()
    dots = jnp.zeros((call.all_rows, 1), f32)
    for block in call.blocks:
        partial_sum = times_transposed(grad_pre[...], r.w_qkv[block, :])
        dots = dots + jnp.sum(
            partial_sum * r.attn_in[:, block].astype(f32), axis=1, keepdims=True
        )
        r.part[:, block] = partial_sum.astype(bf16)
    as_line(dots, r.line)
    lines = Lines(place, r.line, *r.slots)
    lines.start()
    sums = call.sums(r.part, r.reduce)
    last_sums = call.sums(r.last_part, r.last_reduce)
    for one in sums:
        one.start()
    for one in sums:
        one.pass_on()
    for block in call.blocks:
        r.pre[block, :] = contract_rows(r.attn_in[:, block], grad_pre[...]).astype(bf16)
    pre.start()
    for one in sums:
        one.pass_more()
    for one in last_sums:
        one.start()
    for block in call.blocks:
        r.out[:, block] = contract_rows(r.mix[...], r.whole[:, block]).astype(bf16)
    out.start()
    for one in last_sums:
        one.pass_on()

    def use(q, span, grad):
        r.first_grad[span, :] = grad.astype(bf16)

    r.both_pieces[0:8, :] = call.behind_norm(sums, lines, r.grad_mid, r.hidden, use)
    r.both_pieces[8:16, :] = r.piece[...]
    piece, pieces = r.both_pieces, r.pieces
    gsend, grecv = r.piece_sems
    piece_copies = [
        remote(
            piece, pieces.at[place.me], gsend.at[d], grecv.at[d],
            {"wt": lax.rem(place.me + d, 8)},
        )
        for d in range(1, 8)
    ]
    for copy in piece_copies:
        copy.start()
    for one in last_sums:
        one.pass_more()
    pieces[place.me] = piece[...]
    for copy in piece_copies:
        copy.wait()
    osend, orecv = r.owner_sems
    owner_copies = []
    for d in range(1, 8):
        owner = lax.rem(ctx.me + d, 8)
        copy = remote(
            pieces.at[owner], r.gain_slots.at[d], osend.at[d], orecv.at[d], {"ctx": owner}
        )
        copy.start()
        owner_copies.append(copy)
    up.join()
    pre.join()
    out.join()
    for q, span in enumerate(call.spans):
        r.result[span, :] = (r.last_mid[span, :] + last_sums[q].total()).astype(bf16)
    total = pieces[ctx.me]
    for d, copy in enumerate(owner_copies, start=1):
        copy.wait_recv()
        total = total + r.gain_slots[d]
    r.gains[...] = total
    up.swap()
    gate.first()
    pre.swap()
    out.swap()
    gate.join()
    up.total()
    pre.total()
    out.total()
    gate.total()
    for one in sums + last_sums + call.beside:
        one.finish()
    for copy in owner_copies:
        copy.wait_send()
    lines.finish()


def call_with_ctx(
    kernel, operands, outs, scratch, ctx_shapes, hbm_names, collective_id, vmem_mib, name,
    chunks=4
):
    vmem = pl.BlockSpec(memory_space=pltpu.VMEM)
    kinds = {one: pl.BlockSpec(memory_space=pl.ANY) for one in hbm_names}
    kinds["bounds"] = pl.BlockSpec(memory_space=pltpu.SMEM)
    outs, scratch = dict(outs), dict(scratch)
    for one, shape in ctx_shapes.items():
        outs["own_" + one] = (owned(shape, CTX_DIMS[one]), bf16)
        scratch["sum_" + one] = ctx_scratch(shape, CTX_DIMS[one], CTX_MODES[one])
    names = (
        [(one, 1) for one in operands] + [(one, 1) for one in outs]
        + [(one, len(specs)) for one, specs in scratch.items()]
    )
    results = pl.pallas_call(
        functools.partial(kernel, 8, chunks, names, tuple(ctx_shapes)),
        out_shape=tuple(jax.ShapeDtypeStruct(*one) for one in outs.values()),
        in_specs=[kinds.get(one, vmem) for one in operands],
        out_specs=(vmem,) * len(outs),
        scratch_shapes=[spec for specs in scratch.values() for spec in specs],
        compiler_params=pltpu.CompilerParams(
            collective_id=collective_id, has_side_effects=True,
            vmem_limit_bytes=vmem_mib * MiB,
        ),
        name=name,
    )(*operands.values())
    return SimpleNamespace(**dict(zip(outs, results)))


def middle_of_backward(operands, collective_id, chunks=4):
    rows, width = operands["mid"].shape
    shape = operands["down_a"].shape
    return call_with_ctx(
        middle_kernel, operands,
        dict(
            grad_mid=((rows, width), f32), piece=((8, width), f32),
            whole=((rows, 8 * width), bf16), grad_pre=((rows, 384), bf16),
        ),
        dict(
            agsrc=[pltpu.VMEM((rows, width), bf16)],
            grad_mix=[pltpu.VMEM((rows, width), bf16)],
            slots=[pltpu.VMEM((8, 8, 128), f32)] + seven(),
            reduce=reduce_scratch(chunks, rows // chunks, width),
            gather=gather_scratch(chunks),
            attention=attention_back_scratch(operands["kv"].shape),
        ),
        dict(down_a=shape, down_b=shape), ("down_a", "down_b"), collective_id, 30,
        "middle_of_backward", chunks,
    )


def end_of_backward(operands, collective_id, chunks=4):
    rows, width = operands["grad_mid"].shape
    wide = operands["up"].shape
    pre, out = (8 * width, 384), (width, 8 * width)
    reduce = reduce_scratch(chunks, rows // chunks, width)
    return call_with_ctx(
        last_kernel, operands,
        dict(
            first_grad=((rows, width), bf16), result=((rows, width), bf16),
            gains=((16, width), f32),
        ),
        dict(
            part=[pltpu.VMEM((rows, 8 * width), bf16)],
            pre=[pltpu.VMEM(pre, bf16)],
            out=[pltpu.VMEM(out, bf16)],
            line=[pltpu.VMEM((8, 128), f32)],
            both_pieces=[pltpu.VMEM((16, width), f32)],
            pieces=[pltpu.VMEM((8, 16, width), f32)],
            gain_slots=[pltpu.VMEM((8, 16, width), f32)],
            piece_sems=seven(),
            owner_sems=seven(),
            slots=[pltpu.VMEM((8, 8, 128), f32)] + seven(),
            reduce=reduce,
            last_reduce=reduce,
        ),
        dict(up=wide, gate=wide, pre=pre, out=out), ("up", "gate"), collective_id, 48,
        "end_of_backward", chunks,
    )


def per_device(
    inputs,
    cotangent,
    doc_bounds,
    attn_gain,
    w_query,
    w_key,
    w_value,
    w_out,
    mlp_gain,
    w_gate,
    w_up,
    w_down,
):
    ctx_rank = lax.axis_index("ctx")
    wt_rank = lax.axis_index("wt")
    micro_count, block_rows, share_width = inputs.shape
    rows = micro_count * block_rows
    gain_attn = attn_gain.astype(f32)
    gain_mlp = mlp_gain.astype(f32)
    own_gain_attn = lax.dynamic_slice_in_dim(gain_attn, wt_rank * share_width, share_width, 1)
    own_gain_mlp = lax.dynamic_slice_in_dim(gain_mlp, wt_rank * share_width, share_width, 1)
    w_qkv = jnp.concatenate([w_query[0], w_key[0], w_value[0]], axis=1)
    w_o, w_g, w_u, w_d = w_out[0], w_gate[0], w_up[0], w_down[0]
    begin = inputs.reshape(rows, share_width)
    cot = cotangent.reshape(rows, share_width)

    places = ctx_rank * block_rows + jnp.arange(block_rows, dtype=jnp.int32)
    offsets = jnp.concatenate(
        [places - doc_begins(doc_bounds[b], places) for b in range(micro_count)]
    )
    angles = offsets.astype(f32)[:, None] * rope_freqs(HD)[None, :]
    cos_half, sin_half = jnp.cos(angles), jnp.sin(angles)
    cosine = jnp.concatenate([cos_half] * 4, axis=1)
    sine = jnp.concatenate([sin_half] * 4, axis=1)
    key_lane = jnp.arange(128)[None, :] < HD
    kv_cosine = jnp.where(key_lane, cosine, 1.0)
    kv_sine = jnp.where(key_lane, sine, 0.0)

    def forward(whole, share, tick):
        hidden = whole.astype(f32)
        factor = lax.rsqrt(jnp.mean(hidden * hidden, axis=-1, keepdims=True) + eps)
        attn_in = (hidden * factor * gain_attn).astype(bf16)
        pre = jnp.dot(attn_in, w_qkv, preferred_element_type=f32)
        q_pre, kv_pre = pre[:, :256], pre[:, 256:]
        mix, logs, mixed, kv = attention(
            doc_bounds, q_pre, kv_pre, cosine, sine, kv_cosine, kv_sine, 1
        )
        part = jnp.dot(mix, w_o, preferred_element_type=f32).astype(bf16)
        mid, mid_whole = forward_mid(part, share, 2)
        mid_wide = mid_whole.astype(f32)
        mid_factor = lax.rsqrt(jnp.mean(mid_wide * mid_wide, axis=-1, keepdims=True) + eps)
        mlp_in = (mid_wide * mid_factor * gain_mlp).astype(bf16)
        gate = jnp.dot(mlp_in, w_g, preferred_element_type=f32)
        up = jnp.dot(mlp_in, w_u, preferred_element_type=f32)
        inner = lax.optimization_barrier((jax.nn.silu(gate) * up).astype(bf16))
        part = jnp.dot(inner, w_d, preferred_element_type=f32).astype(bf16)
        saved = SimpleNamespace(
            whole=whole, share=share, factor=factor, attn_in=attn_in, q_pre=q_pre, kv=kv,
            mix=mix, logs=logs, mixed=mixed, mid=mid, mid_whole=mid_whole,
            mid_factor=mid_factor, mlp_in=mlp_in, gate=gate, up=up, inner=inner,
        )
        return part, saved

    def line_of(part, whole, factor, gain):
        dots = jnp.sum(part * (whole.astype(f32) * factor * gain), axis=1)
        return jnp.concatenate(
            [dots.reshape(rows // 128, 128), jnp.zeros((8 - rows // 128, 128), f32)]
        )

    def behind_mlp(grad, saved):
        gate, up = saved.gate, saved.up
        grad_inner = times_transposed(grad, w_d)
        sigmoid = jax.nn.sigmoid(gate)
        grad_gate = (grad_inner * up * sigmoid * (1.0 + gate * (1.0 - sigmoid))).astype(bf16)
        grad_up = (grad_inner * gate * sigmoid).astype(bf16)
        part = times_transposed(grad_gate, w_g) + times_transposed(grad_up, w_u)
        line = line_of(part, saved.mid_whole, saved.mid_factor, gain_mlp)
        return part.astype(bf16), line, grad_gate, grad_up

    def backward(grad, grad_share, saved):
        part, line, _, _ = behind_mlp(grad, saved)
        grad_mid, grad_attn = backward_sum(
            "mid", part, line, grad_share, saved.mid, saved.mid_factor, own_gain_mlp,
            [], 3,
        )
        grad_mix = times_transposed(grad_attn, w_o).astype(bf16)
        grad_query, grad_kv = attention_back(
            doc_bounds, saved.q_pre, cosine, sine, kv_cosine, kv_sine, saved.kv,
            saved.logs, saved.mixed, grad_mix, 4,
        )
        grad_pre = jnp.concatenate([grad_query, grad_kv], axis=1)
        part = times_transposed(grad_pre, w_qkv)
        line = line_of(part, saved.whole, saved.factor, gain_attn)
        return (
            part.astype(bf16), line, grad_mid, saved.share, saved.factor,
            own_gain_attn,
        )

    whole_cot = lax.all_gather(cot, "wt", axis=1, tiled=True)
    part, saved = forward(wt_gather(begin, 6), begin, 0)
    share, whole = forward_pass(part, saved.mid, begin, 7)
    part, saved = forward(whole, share, 1)
    last_part = part

    operands = backward(whole_cot, cot, saved)
    section = lax.axis_index("section")
    grad_share, grad = backward_sum("pass", *operands, [cot], 9)
    part, line, grad_gate, grad_up = behind_mlp(grad, saved)
    half = saved.inner.shape[1] // 2
    mids = middle_of_backward(
        dict(
            bounds=doc_bounds, part=part, line=line, above=grad_share, mid=saved.mid,
            factor=saved.mid_factor, gain=own_gain_mlp, flat=saved.q_pre, cosine=cosine,
            sine=sine, kv_cosine=kv_cosine, kv_sine=kv_sine, kv=saved.kv, logs=saved.logs,
            mixed=saved.mixed, w_out=w_o,
            down_a=contract_rows(saved.inner[:, :half], grad).astype(bf16),
            down_b=contract_rows(saved.inner[:, half:], grad).astype(bf16),
        ),
        8,
    )
    ends = end_of_backward(
        dict(
            grad_pre=mids.grad_pre, w_qkv=w_qkv, attn_in=saved.attn_in, mix=saved.mix,
            whole=mids.whole, grad_mid=mids.grad_mid, hidden=saved.share,
            factor=saved.factor, gain=own_gain_attn, piece=mids.piece, last_part=last_part,
            last_mid=saved.mid,
            up=contract_rows(saved.mlp_in, grad_up).astype(bf16),
            gate=contract_rows(saved.mlp_in, grad_gate).astype(bf16),
        ),
        10,
    )
    first_grad, result, gains = ends.first_grad, ends.result, ends.gains
    up, gate, pre, out = (
        one.astype(f32) for one in (ends.own_up, ends.own_gate, ends.own_pre, ends.own_out)
    )
    down = jnp.concatenate([mids.own_down_a, mids.own_down_b], axis=0).astype(f32)
    boundary = jnp.where(section == 0, first_grad, result)
    return (
        boundary.reshape(1, micro_count, block_rows, share_width),
        gains[0][None],
        pre[:, :256][None],
        pre[:, 256:320][None],
        pre[:, 320:][None],
        out[None],
        gains[8][None],
        gate[None],
        up[None],
        down[None],
    )


def solution(mesh):
    return jax.shard_map(
        per_device,
        mesh=mesh,
        in_specs=(
            P(None, "ctx", "wt"),
            P(None, "ctx", "wt"),
            P(),
            P("section", None),
            P("section", None, "wt"),
            P("section", None, "wt"),
            P("section", None, "wt"),
            P("section", "wt", None),
            P("section", None),
            P("section", None, "wt"),
            P("section", None, "wt"),
            P("section", "wt", None),
        ),
        out_specs=(
            P("section", None, "ctx", "wt"),
            P("section", "ctx"),
            P("section", "ctx", "wt"),
            P("section", "ctx", "wt"),
            P("section", "ctx", "wt"),
            P("section", "wt", "ctx"),
            P("section", "ctx"),
            P("section", "ctx", "wt"),
            P("section", "ctx", "wt"),
            P("section", "wt", "ctx"),
        ),
        check_vma=False,
    )
```
